32 devices in a mesh: shard: 4 (over z), context: 4 (over y, x), tensor: 2 (over core).
Axes of the slice: x: 2, y: 2, z: 4, core: 2. Of those that a mesh axis runs over, the one named last changes fastest.
Arguments:
- hidden_in: bfloat16 [4, 4096, 576], P('shard', ('context', 'tensor')), may hold values from -6 to 6
- segment_ids: int32 [4, 4096], P('shard'), may hold values from 0 to 3, as said below
- norm_gains: bfloat16 [2, 576], P(None, 'shard'), may hold values from 0.25 to 1.75
- w_query: bfloat16 [576, 576], P(None, 'shard'), may hold values from -0.375 to 0.375
- w_key: bfloat16 [576, 192], P(None, 'shard'), may hold values from -0.25 to 0.25
- w_value: bfloat16 [576, 192], P(None, 'shard'), may hold values from -0.25 to 0.25
- w_output: bfloat16 [576, 576], P(None, 'shard'), may hold values from -3 to 3
- w_gate: bfloat16 [1536, 576], P('tensor', 'shard'), may hold values from -0.25 to 0.25
- w_up: bfloat16 [1536, 576], P('tensor', 'shard'), may hold values from -0.25 to 0.25
- w_down: bfloat16 [1536, 576], P('tensor', 'shard'), may hold values from -0.15625 to 0.15625
- cotangent: bfloat16 [4, 4096, 576], P('shard', ('context', 'tensor')), may hold values from -6 to 6
Outputs:
- layer_out: bfloat16 [4, 4096, 576], P('shard', ('context', 'tensor'))
- grad_hidden: float32 [4, 4096, 576], P('shard', ('context', 'tensor'))
- grad_gains: float32 [2, 576], P(None, 'shard')
- grad_query: float32 [576, 576], P(None, 'shard')
- grad_key: float32 [576, 192], P(None, 'shard')
- grad_value: float32 [576, 192], P(None, 'shard')
- grad_output: float32 [576, 576], P(None, 'shard')
- grad_gate: float32 [1536, 576], P('tensor', 'shard')
- grad_up: float32 [1536, 576], P('tensor', 'shard')
- grad_down: float32 [1536, 576], P('tensor', 'shard')
The draws below stay inside these ranges and needn't reach their ends.
Inputs may be any that keep to these rules, and one draw needn't show every extreme that they name: `segment_ids`: within a row the ids never fall, start at 0 and end at 3; every id occurs in every row.
All inputs are finite; a program needn't handle non-finite values.
Results may differ from the reference program's by a relative error of at most 0.023.
Values may be sent and summed in bfloat16 or wider, within the bound.
No kernel may reach another device: no remote copies, remote signals or barrier semaphores. Data moves between devices by JAX's collectives and lax.ppermute only.
A program may use at most 256 MiB of HBM per device.

```python
import math
import jax
import jax.numpy as jnp
from jax import lax

D = 576
HEADS = 9
KV_HEADS = 3
HEAD_DIM = 64
FF = 1536
TOK_DEV = 512
DOCS = 4
KV_WIDTH = 192
LEN = 4096
SEQS = 4


def draw_segment_ids(key, part):
    key = jax.random.fold_in(key, 11)
    keys_list = jax.random.split(key, 3)
    first_cut = jax.random.randint(keys_list[0], (SEQS, 1), 1, TOK_DEV // 2 + 1)
    second_cut = jax.random.randint(keys_list[1], (SEQS, 1), LEN - TOK_DEV // 2, LEN - 1)
    spread_draw = jax.random.randint(keys_list[2], (SEQS, 1), 0, LEN)
    third_cut = second_cut + 1 + spread_draw % (LEN - 1 - second_cut)
    position = jnp.arange(LEN, dtype=jnp.int32)[None, :]
    doc_ids = (position >= first_cut).astype(jnp.int32) + (position >= second_cut).astype(jnp.int32) + (position >= third_cut).astype(jnp.int32)
    return doc_ids.astype(jnp.int32)


def levels(own_key, extent, cuts, low, high):
    level, own = 1.0, jax.random.fold_in(own_key, 6)
    for axis_at, blocks in cuts:
        draws = jnp.exp(jax.random.uniform(jax.random.fold_in(own, axis_at), (blocks,), jnp.float32, low / len(cuts), high / len(cuts)))
        level = level * jnp.repeat(draws, extent[axis_at] // blocks).reshape([-1 if axis == axis_at else 1 for axis in range(len(extent))])
    return level


def noise(stream_key, dims, spread, bound, shards=(), kind=jnp.bfloat16):
    values = jax.random.normal(stream_key, dims, jnp.float32) * spread
    if len(shards) > 0:
        values = levels(stream_key, dims, shards, -0.22, 0.18) * values
    return jnp.clip(values, min=-bound, max=bound).astype(kind)


def setup_inputs(seed: int = 0) -> dict:
    streams_of = jax.random.split(jax.random.key(seed), 12)
    hidden_in = noise(streams_of[0], (SEQS, LEN, D), 1.0, 6.0, ((0, 4), (1, 8)))
    segment_ids = draw_segment_ids(jax.random.fold_in(streams_of[11], 71), 0)
    norm_gains = jnp.clip(1.0 + 0.15 * jax.random.normal(streams_of[2], (2, D), jnp.float32), 0.25, 1.75).astype(jnp.bfloat16)
    w_query = noise(streams_of[3], (D, D), (D // 2) ** -0.5, 0.375, ((1, 4),))
    w_key = noise(streams_of[4], (D, KV_WIDTH), D ** -0.5, 0.25, ((1, 4),))
    w_value = noise(streams_of[5], (D, KV_WIDTH), D ** -0.5, 0.25, ((1, 4),))
    w_output = noise(streams_of[6], (D, D), (max(1, D * 32 // LEN)) ** -0.5, 3.0, ((1, 4),))
    w_gate = noise(streams_of[7], (FF, D), D ** -0.5, 0.25, ((0, 2), (1, 4)))
    w_up = noise(streams_of[8], (FF, D), D ** -0.5, 0.25, ((0, 2), (1, 4)))
    w_down = noise(streams_of[9], (FF, D), FF ** -0.5, 0.15625, ((0, 2), (1, 4)))
    cotangent = noise(streams_of[10], (SEQS, LEN, D), 1.0, 6.0, ((0, 4), (1, 8)))
    return dict(hidden_in=hidden_in, segment_ids=segment_ids, norm_gains=norm_gains, w_query=w_query, w_key=w_key, w_value=w_value, w_output=w_output, w_gate=w_gate, w_up=w_up, w_down=w_down, cotangent=cotangent)


rope_base = 100000.0
norm_eps = 1e-05
masked_score = -1e+30
highest = lax.Precision.HIGHEST

@jax.custom_vjp
def low(v):
    return lax.optimization_barrier(v.astype(jnp.bfloat16)).astype(jnp.float32)

@jax.custom_vjp
def low_back(v):
    return v

def low_keep(v):
    return (low(v), None)

def low_pass(kept, grad):
    return (grad,)

def back_keep(v):
    return (v, None)

def back_low(kept, grad):
    return (low(grad),)
low.defvjp(low_keep, low_pass)
low_back.defvjp(back_keep, back_low)

def rms_scale(hidden, gain_row):
    return hidden * lax.rsqrt(lax.optimization_barrier(jnp.mean(hidden * hidden, axis=-1, keepdims=True)) + norm_eps) * gain_row

def doc_positions(seg_row):
    length = seg_row.shape[0]
    one_hot = (seg_row[None, :] == jnp.arange(DOCS, dtype=jnp.int32)[:, None]).astype(jnp.int32)
    doc_counts = lax.optimization_barrier(jnp.sum(one_hot, axis=1))
    starts = jnp.cumsum(doc_counts) - doc_counts
    doc_first = lax.optimization_barrier(jnp.sum(one_hot * starts[:, None], axis=0))
    return jnp.arange(length, dtype=jnp.int32) - doc_first

def rotate(matrix, positions, head_count):
    head_size = matrix.shape[1] // head_count
    half_size = head_size // 2
    frequency = rope_base ** (-jnp.arange(half_size, dtype=jnp.float32) * 2.0 / head_size)
    angles = positions.astype(jnp.float32)[:, None] * frequency[None, :]
    cosine = jnp.cos(angles)[:, None, :]
    sine_table = jnp.sin(angles)[:, None, :]
    per_head = matrix.reshape(matrix.shape[0], head_count, head_size)
    leading = per_head[..., :half_size]
    trailing = per_head[..., half_size:]
    turned = jnp.concatenate([leading * cosine - trailing * sine_table, trailing * cosine + leading * sine_table], axis=-1)
    return turned.reshape(matrix.shape)

def attention(queries, keys, values, seg_row):
    length = queries.shape[0]
    group = HEADS // KV_HEADS
    key_heads = keys.reshape(length, KV_HEADS, HEAD_DIM)
    value_heads = values.reshape(length, KV_HEADS, HEAD_DIM)
    key_index = jnp.arange(length, dtype=jnp.int32)
    score_scale = 1.0 / math.sqrt(HEAD_DIM)

    def one_block(block_index):
        first_row = block_index * TOK_DEV
        query_block = lax.dynamic_slice_in_dim(queries, first_row, TOK_DEV, 0).reshape(TOK_DEV, KV_HEADS, group, HEAD_DIM)
        raw_scores = low_back(jnp.einsum('rgmd,kgd->gmrk', query_block, key_heads, precision=highest))
        query_seg = lax.dynamic_slice_in_dim(seg_row, first_row, TOK_DEV, 0)
        query_index = first_row + jnp.arange(TOK_DEV, dtype=jnp.int32)
        allowed = (seg_row[None, :] == query_seg[:, None]) & (key_index[None, :] <= query_index[:, None])
        scores = jnp.where(allowed, raw_scores * score_scale, masked_score)
        row_peak = lax.optimization_barrier(jnp.max(scores, axis=-1, keepdims=True))
        shifted_exp = jnp.exp(scores - row_peak)
        probabilities = shifted_exp / lax.optimization_barrier(jnp.sum(shifted_exp, axis=-1, keepdims=True))
        mixed = jnp.einsum('gmrk,kgd->rgmd', low(probabilities), value_heads, precision=highest)
        return mixed.reshape(TOK_DEV, HEADS * HEAD_DIM)
    blocks = lax.map(jax.checkpoint(one_block), jnp.arange(length // TOK_DEV, dtype=jnp.int32))
    return blocks.reshape(length, HEADS * HEAD_DIM)

def layer_forward(inputs, weight_set, seg_row):
    norm_gains, w_query, w_key, w_value, w_output, w_gate, w_up, w_down = weight_set
    positions = doc_positions(seg_row)
    normed = low(rms_scale(inputs, norm_gains[0]))
    queries = low(rotate(low_back(jnp.dot(normed, w_query, precision=highest)), positions, HEADS))
    keys = low(rotate(low_back(jnp.dot(normed, w_key, precision=highest)), positions, KV_HEADS))
    values = low(low_back(jnp.dot(normed, w_value, precision=highest)))
    mixed = low(low_back(attention(queries, keys, values, seg_row)))
    middle = inputs + low_back(jnp.dot(mixed, w_output, precision=highest))
    second_in = low(rms_scale(middle, norm_gains[1]))
    gate = low_back(jnp.dot(second_in, w_gate.T, precision=highest))
    upward = low_back(jnp.dot(second_in, w_up.T, precision=highest))
    hidden_units = low(gate / (1.0 + jnp.exp(-gate)) * upward)
    return middle + jnp.dot(hidden_units, w_down, precision=highest)

def reference(hidden_in, segment_ids, norm_gains, w_query, w_key, w_value, w_output, w_gate, w_up, w_down, cotangent):
    weights = (norm_gains.astype(jnp.float32), w_query.astype(jnp.float32), w_key.astype(jnp.float32), w_value.astype(jnp.float32), w_output.astype(jnp.float32), w_gate.astype(jnp.float32), w_up.astype(jnp.float32), w_down.astype(jnp.float32))

    def per_sequence(totals, sequence_item):
        inputs, seg_row, cot_row = sequence_item

        def forward(inputs_f, weight_set):
            return layer_forward(inputs_f, weight_set, seg_row)
        layer_value, pull_back = jax.vjp(forward, inputs.astype(jnp.float32), weights)
        input_grad, weight_grads = pull_back(cot_row.astype(jnp.float32))
        totals = jax.tree.map(lambda left_sum, right_sum: left_sum + right_sum, totals, weight_grads)
        return (totals, (layer_value.astype(jnp.bfloat16), input_grad))
    zero_grads = jax.tree.map(jnp.zeros_like, weights)
    final, (outputs, input_grads) = lax.scan(per_sequence, zero_grads, (hidden_in, segment_ids, cotangent))
    return (outputs, input_grads, final[0], final[1], final[2], final[3], final[4], final[5], final[6], final[7])
```

```python
import functools

import jax
import jax.numpy as jnp
from jax import lax
from jax.experimental import pallas as pl
from jax.experimental.pallas import tpu as pltpu
from jax.sharding import PartitionSpec as P

HEADS = 9
KV_HEADS = 3
DOCS = 4
GROUP = HEADS // KV_HEADS

rope_base = 100000.0
norm_eps = 1e-05
masked_score = -1e30

f32 = jnp.float32
bf16 = jnp.bfloat16
SEQ = ("context", "tensor")


def mm(left, right, left_dim, right_dim):
    return lax.dot_general(
        left, right, (((left_dim,), (right_dim,)), ((), ())), preferred_element_type=f32
    )


def flip(count, mask):
    return [(i, i ^ mask) for i in range(count)]


def swap(value, axis, mask):
    return lax.ppermute(value, axis, flip(lax.axis_size(axis), mask))


def doc_starts(seg_row):
    one_hot = (seg_row[None, :] == jnp.arange(DOCS, dtype=jnp.int32)[:, None]).astype(jnp.int32)
    doc_counts = jnp.sum(one_hot, axis=1)
    starts = jnp.cumsum(doc_counts) - doc_counts
    return jnp.sum(one_hot * starts[:, None], axis=0)


def inverse_rms(hidden):
    return lax.rsqrt(jnp.mean(hidden * hidden, axis=-1, keepdims=True) + norm_eps)


def norm_back(grad, hidden, gain):
    inverse = inverse_rms(hidden)
    unit = hidden * inverse
    scaled = grad * gain
    return (scaled - unit * jnp.mean(scaled * unit, axis=-1, keepdims=True)) * inverse


def turn(feature_rows, cosine, sine, sign):
    half = cosine.shape[0]
    tokens = feature_rows.shape[1]
    parts = feature_rows.reshape(-1, 2, half, tokens)
    first, second = parts[:, 0], parts[:, 1]
    turned = jnp.stack(
        [first * cosine - sign * (second * sine), second * cosine + sign * (first * sine)], axis=1
    )
    return turned.reshape(feature_rows.shape)


def key_ranges(info_ref, chunk):
    low = info_ref[1 + 4 * chunk]
    full_from = info_ref[2 + 4 * chunk]
    full_to = info_ref[3 + 4 * chunk]
    high = info_ref[4 + 4 * chunk]
    return low, full_from, full_to, high


def allowed_mask(block, key_block, bounds_ref):
    columns = bounds_ref.shape[1]
    key_index = block * key_block + lax.broadcasted_iota(jnp.int32, (key_block, columns), 0)
    return (key_index >= bounds_ref[0:1, :]) & (key_index <= bounds_ref[1:2, :])


def forward_kernel(
    key_block, info_ref, q_ref, k_ref, vt_ref, bounds_ref, o_ref, lse_ref, m_ref, l_ref, acc_ref
):
    chunk = pl.program_id(1)
    me = info_ref[0]
    size = k_ref.shape[2]
    m_ref[...] = jnp.full_like(m_ref, masked_score)
    l_ref[...] = jnp.zeros_like(l_ref)
    acc_ref[...] = jnp.zeros_like(acc_ref)

    def step(block, masked):
        place = pl.multiple_of((block ^ me) * key_block, key_block)
        keys = k_ref[0, pl.ds(place, key_block), :]
        values = vt_ref[:, pl.ds(place, key_block)]
        mask = allowed_mask(block, key_block, bounds_ref) if masked else None
        for member in range(GROUP):
            rows = slice(member * size, (member + 1) * size)
            scores = mm(keys, q_ref[rows, :], 1, 0)
            if masked:
                scores = jnp.where(mask, scores, masked_score)
            old = m_ref[member : member + 1, :]
            new = jnp.maximum(old, jnp.max(scores, axis=0, keepdims=True))
            factor = jnp.exp(old - new)
            weights = jnp.exp(scores - new)
            m_ref[member : member + 1, :] = new
            l_ref[member : member + 1, :] = l_ref[member : member + 1, :] * factor + jnp.sum(
                weights, axis=0, keepdims=True
            )
            acc_ref[rows, :] = acc_ref[rows, :] * factor + mm(values, weights.astype(bf16), 1, 0)

    low, full_from, full_to, high = key_ranges(info_ref, chunk)
    pl.loop(low, full_from)(lambda b: step(b, True))
    pl.loop(full_from, full_to)(lambda b: step(b, False))
    pl.loop(full_to, high)(lambda b: step(b, True))
    for member in range(GROUP):
        rows = slice(member * size, (member + 1) * size)
        total = l_ref[member : member + 1, :]
        o_ref[rows, :] = acc_ref[rows, :] / total
        lse_ref[0, member : member + 1, :] = m_ref[member : member + 1, :] + jnp.log(total)


def backward_kernel(
    key_block,
    scale,
    info_ref,
    q_ref,
    do_ref,
    k_ref,
    kt_ref,
    v_ref,
    lse_ref,
    delta_ref,
    bounds_ref,
    dq_ref,
    dk_ref,
    dv_ref,
):
    chunk = pl.program_id(1)
    me = info_ref[0]
    size = k_ref.shape[2]
    dq_ref[...] = jnp.zeros_like(dq_ref)

    @pl.when(chunk == 0)
    def _():
        dk_ref[...] = jnp.zeros_like(dk_ref)
        dv_ref[...] = jnp.zeros_like(dv_ref)

    def step(block, masked):
        place = pl.multiple_of((block ^ me) * key_block, key_block)
        keys = k_ref[0, pl.ds(place, key_block), :]
        values = v_ref[0, pl.ds(place, key_block), :]
        keys_t = kt_ref[:, pl.ds(place, key_block)]
        mask = allowed_mask(block, key_block, bounds_ref) if masked else None
        dk = dv = None
        for member in range(GROUP):
            rows = slice(member * size, (member + 1) * size)
            queries = q_ref[rows, :]
            grads = do_ref[rows, :]
            scores = mm(keys, queries, 1, 0)
            if masked:
                scores = jnp.where(mask, scores, masked_score)
            probs = jnp.exp(scores - lse_ref[0, member : member + 1, :])
            prob_grad = mm(values, grads, 1, 0)
            raw = (probs * (prob_grad - delta_ref[0, member : member + 1, :])).astype(bf16)
            dv_now = mm(grads, probs.astype(bf16), 1, 1)
            dk_now = mm(queries, raw, 1, 1)
            dv = dv_now if dv is None else dv + dv_now
            dk = dk_now if dk is None else dk + dk_now
            dq_ref[rows, :] += mm(keys_t, raw, 1, 0) * scale
        dk_ref[:, pl.ds(place, key_block)] += dk
        dv_ref[:, pl.ds(place, key_block)] += dv

    low, full_from, full_to, high = key_ranges(info_ref, chunk)
    pl.loop(low, full_from)(lambda b: step(b, True))
    pl.loop(full_from, full_to)(lambda b: step(b, False))
    pl.loop(full_to, high)(lambda b: step(b, True))


def grid_spec(in_specs, out_specs, scratch, groups):
    return pltpu.PrefetchScalarGridSpec(
        num_scalar_prefetch=1,
        grid=(groups, 2),
        in_specs=in_specs,
        out_specs=out_specs,
        scratch_shapes=scratch,
    )


def attend(info, queries_t, keys, values_t, bounds, key_block):
    length, size = keys.shape[1], keys.shape[2]
    tokens = queries_t.shape[1]
    chunk = tokens // 2
    wide = GROUP * size
    head_block = pl.BlockSpec((wide, chunk), lambda g, c, info: (g, c))
    stat_block = pl.BlockSpec((1, GROUP, chunk), lambda g, c, info: (g, 0, c))
    elements = HEADS * tokens * length // 2
    return pl.pallas_call(
        functools.partial(forward_kernel, key_block),
        out_shape=(
            jax.ShapeDtypeStruct((HEADS * size, tokens), f32),
            jax.ShapeDtypeStruct((KV_HEADS, GROUP, tokens), f32),
        ),
        grid_spec=grid_spec(
            [
                head_block,
                pl.BlockSpec((1, length, size), lambda g, c, info: (g, 0, 0)),
                pl.BlockSpec((size, length), lambda g, c, info: (g, 0)),
                pl.BlockSpec((2, chunk), lambda g, c, info: (0, c)),
            ],
            (head_block, stat_block),
            [
                pltpu.VMEM((GROUP, chunk), f32),
                pltpu.VMEM((GROUP, chunk), f32),
                pltpu.VMEM((wide, chunk), f32),
            ],
            KV_HEADS,
        ),
        compiler_params=pltpu.CompilerParams(vmem_limit_bytes=48 * 1024 * 1024),
        cost_estimate=pl.CostEstimate(
            flops=16 * elements * size, bytes_accessed=4 * 1024 * 1024, transcendentals=elements
        ),
        name="attend",
    )(info, queries_t, keys, values_t, bounds)


def attend_back(
    group, info, queries_t, grads_t, keys, keys_t, values, log_total, delta, bounds, key_block, scale
):
    length, size = keys.shape[1], keys.shape[2]
    tokens = queries_t.shape[1]
    chunk = tokens // 2
    wide = GROUP * size
    head_block = pl.BlockSpec((wide, chunk), lambda g, c, info: (group, c))
    head_out = pl.BlockSpec((wide, chunk), lambda g, c, info: (0, c))
    stat_block = pl.BlockSpec((1, GROUP, chunk), lambda g, c, info: (group, 0, c))
    token_block = pl.BlockSpec((1, length, size), lambda g, c, info: (group, 0, 0))
    feature_block = pl.BlockSpec((size, length), lambda g, c, info: (group, 0))
    feature_out = pl.BlockSpec((size, length), lambda g, c, info: (0, 0))
    elements = GROUP * tokens * length // 2
    return pl.pallas_call(
        functools.partial(backward_kernel, key_block, scale),
        out_shape=(
            jax.ShapeDtypeStruct((wide, tokens), f32),
            jax.ShapeDtypeStruct((size, length), f32),
            jax.ShapeDtypeStruct((size, length), f32),
        ),
        grid_spec=grid_spec(
            [
                head_block,
                head_block,
                token_block,
                feature_block,
                token_block,
                stat_block,
                stat_block,
                pl.BlockSpec((2, chunk), lambda g, c, info: (0, c)),
            ],
            (head_out, feature_out, feature_out),
            [],
            1,
        ),
        compiler_params=pltpu.CompilerParams(vmem_limit_bytes=56 * 1024 * 1024),
        cost_estimate=pl.CostEstimate(
            flops=40 * elements * size, bytes_accessed=12 * 1024 * 1024, transcendentals=elements
        ),
        name="attend_back",
    )(info, queries_t, grads_t, keys, keys_t, values, log_total, delta, bounds)


def project_kernel(pieces, *refs):
    x_refs = refs[:pieces]
    key_ref, value_ref, gain_ref, cos_ref, sin_ref = refs[pieces : pieces + 5]
    a_ref, k_ref, kt_ref, v_ref, vt_ref, held, sems = refs[pieces + 5 :]
    step = pl.program_id(0)

    @pl.when(step == 0)
    def _():
        for number in range(pieces):
            pltpu.make_async_copy(x_refs[number], held.at[number], sems.at[number]).start()

    for number in range(pieces):

        @pl.when(step == number)
        def _(number=number):
            pltpu.make_async_copy(x_refs[number], held.at[number], sems.at[number]).wait()

    x = held[step].astype(f32)
    a = (x * inverse_rms(x) * gain_ref[0:1, :]).astype(bf16)
    a_ref[...] = a
    k_lin = mm(key_ref[...], a, 1, 1)
    cosine, sine = cos_ref[...], sin_ref[...]
    size = k_ref.shape[2]
    half = size // 2
    for group in range(KV_HEADS):
        first = k_lin[group * size : group * size + half, :]
        second = k_lin[group * size + half : (group + 1) * size, :]
        turned = jnp.concatenate(
            [first * cosine - second * sine, second * cosine + first * sine], axis=0
        )
        kt_ref[group * size : (group + 1) * size, :] = turned.astype(bf16)
        k_ref[group] = turned.T.astype(bf16)
    v_lin = mm(value_ref[...], a, 1, 1)
    vt_ref[...] = v_lin.astype(bf16)
    for group in range(KV_HEADS):
        v_ref[group] = v_lin[group * size : (group + 1) * size, :].T.astype(bf16)


def project(x_pieces, key_t, value_t, gains, cosine, sine):
    pieces = len(x_pieces)
    rows, width = x_pieces[0].shape
    kv_width = key_t.shape[0]
    size = kv_width // KV_HEADS
    length = pieces * rows
    whole = lambda array: pl.BlockSpec(array.shape, lambda i: (0,) * array.ndim)
    table = pl.BlockSpec((size // 2, rows), lambda i: (0, i))
    by_token = pl.BlockSpec((KV_HEADS, rows, size), lambda i: (0, i, 0))
    by_feature = pl.BlockSpec((kv_width, rows), lambda i: (0, i))
    return pl.pallas_call(
        functools.partial(project_kernel, pieces),
        out_shape=(
            jax.ShapeDtypeStruct((length, width), bf16),
            jax.ShapeDtypeStruct((KV_HEADS, length, size), bf16),
            jax.ShapeDtypeStruct((kv_width, length), bf16),
            jax.ShapeDtypeStruct((KV_HEADS, length, size), bf16),
            jax.ShapeDtypeStruct((kv_width, length), bf16),
        ),
        grid=(pieces,),
        in_specs=[pl.BlockSpec(memory_space=pl.ANY)] * pieces
        + [whole(key_t), whole(value_t), whole(gains), table, table],
        out_specs=(
            pl.BlockSpec((rows, width), lambda i: (i, 0)),
            by_token,
            by_feature,
            by_token,
            by_feature,
        ),
        scratch_shapes=[
            pltpu.VMEM((pieces, rows, width), bf16),
            pltpu.SemaphoreType.DMA((pieces,)),
        ],
        compiler_params=pltpu.CompilerParams(vmem_limit_bytes=48 * 1024 * 1024),
        cost_estimate=pl.CostEstimate(
            flops=8 * length * width * kv_width, bytes_accessed=8 * length * width, transcendentals=0
        ),
        name="project",
    )(*x_pieces, key_t, value_t, gains, cosine, sine)


def feed_tile(second, second_t, cot, cot_t, weights, grad_ref, sum_ref, db_ref):
    gate_t, up_t, down_t = weights
    gate = mm(second, gate_t, 1, 0)
    upward = mm(second, up_t, 1, 0)
    d_hidden = mm(cot, down_t, 1, 0)
    sig = 1.0 / (1.0 + jnp.exp(-gate))
    silu = gate * sig
    hidden = (silu * upward).astype(bf16)
    d_gate = (d_hidden * upward * sig * (1.0 + gate * (1.0 - sig))).astype(bf16)
    d_up = (d_hidden * silu).astype(bf16)
    sum_ref[...] += mm(hidden, down_t, 1, 1)
    db_ref[...] += mm(d_gate, gate_t, 1, 1) + mm(d_up, up_t, 1, 1)
    grad_ref[0] = mm(second_t, d_gate, 1, 0).astype(bf16)
    grad_ref[1] = mm(second_t, d_up, 1, 0).astype(bf16)
    grad_ref[2] = mm(cot_t, hidden, 1, 0).astype(bf16)


def gather_rows(info_ref, piece_refs, held):
    for mask, piece in enumerate(piece_refs):
        spot = info_ref[0] ^ mask
        for matrix in range(held.shape[0]):
            held[matrix, spot] = piece[matrix]
    return [
        held[matrix].reshape(held.shape[1] * held.shape[2], held.shape[3])
        for matrix in range(held.shape[0])
    ]


def feed_first_kernel(count, info_ref, *refs):
    w_refs, wo_refs = refs[:count], refs[count : 2 * count]
    x_ref, o_ref, cot_ref, gain_ref = refs[2 * count : 2 * count + 4]
    h_ref, second_ref, sum_ref, db_ref, grad_ref, output_ref = refs[2 * count + 4 : 2 * count + 10]
    second_t, cot_t, held, held_output = refs[2 * count + 10 :]
    width = x_ref.shape[1]

    @pl.when(pl.program_id(0) == 0)
    def _():
        output_t = gather_rows(info_ref, wo_refs, held_output)[0][:, :width]
        output_ref[...] = output_t
        mixed = o_ref[...].T.astype(bf16)
        middle = x_ref[...].astype(f32) + mm(mixed, output_t, 1, 1)
        second = middle * inverse_rms(middle) * gain_ref[1:2, :]
        h_ref[...] = middle
        second_ref[...] = second.astype(bf16)
        second_t[...] = second.T.astype(bf16)
        cot_t[...] = cot_ref[...].astype(f32).T.astype(bf16)
        sum_ref[...] = middle
        db_ref[...] = jnp.zeros_like(db_ref)

    weights = gather_rows(info_ref, w_refs, held)
    feed_tile(
        second_ref[...], second_t[...], cot_ref[...], cot_t[...], weights, grad_ref, sum_ref, db_ref
    )


def feed_second_kernel(count, info_ref, *refs):
    w_refs = refs[:count]
    h_ref, o_ref, cot_ref, second_ref, sum_in_ref, db_in_ref, gain_ref, wo_ref = refs[
        count : count + 8
    ]
    layer_ref, mg_ref, do_ref, delta_ref, gg_ref, go_ref, grad_ref = refs[count + 8 : count + 15]
    second_t, cot_t, sum_ref, db_ref, held = refs[count + 15 :]
    width = h_ref.shape[1]
    step = pl.program_id(0)

    @pl.when(step == 0)
    def _():
        second_t[...] = second_ref[...].astype(f32).T.astype(bf16)
        cot_t[...] = cot_ref[...].astype(f32).T.astype(bf16)
        sum_ref[...] = sum_in_ref[...]
        db_ref[...] = db_in_ref[...]

    weights = gather_rows(info_ref, w_refs, held)
    feed_tile(
        second_ref[...], second_t[...], cot_ref[...], cot_t[...], weights, grad_ref, sum_ref, db_ref
    )

    @pl.when(step == pl.num_programs(0) - 1)
    def _():
        layer_ref[...] = sum_ref[...].astype(bf16)
        middle = h_ref[...]
        inverse = inverse_rms(middle)
        unit = middle * inverse
        grad = db_ref[...]
        gg_ref[...] = jnp.sum(grad * unit, axis=0, keepdims=True)
        scaled = grad * gain_ref[1:2, :]
        back = (scaled - unit * jnp.mean(scaled * unit, axis=-1, keepdims=True)) * inverse
        middle_grad = cot_ref[...].astype(f32) + back
        mg_ref[...] = middle_grad
        low = middle_grad.astype(bf16)
        low_t = middle_grad.T.astype(bf16)
        d_o = mm(wo_ref[...].astype(f32).T.astype(bf16), low, 1, 1).astype(bf16)
        do_ref[...] = d_o
        mixed = o_ref[...]
        product = d_o.astype(f32) * mixed
        size = width // HEADS
        for head in range(HEADS):
            delta_ref[head // GROUP, head % GROUP : head % GROUP + 1, :] = jnp.sum(
                product[head * size : (head + 1) * size, :], axis=0, keepdims=True
            )
        go_ref[...] = mm(low_t, mixed.astype(bf16), 1, 1).astype(bf16)


def feed_specs(pieces, rows, width):
    part, units = pieces[0].shape[1:]
    tile = 256 if units % 256 == 0 else units
    whole = lambda shape: pl.BlockSpec(shape, lambda i, info: (0,) * len(shape))
    tokens = whole((rows, width))
    features = whole((width, rows))
    gains = whole((2, width))
    tiles = pl.BlockSpec((3, part, tile), lambda i, info: (0, 0, i))
    outputs = pl.BlockSpec((1, part, units), lambda i, info: (3, 0, 0))
    grads = pl.BlockSpec((3, width, tile), lambda i, info: (0, 0, i))
    held = pltpu.VMEM((3, len(pieces), part, tile), bf16)
    held_output = pltpu.VMEM((1, len(pieces), part, units), bf16)
    return units // tile, whole, tokens, features, gains, tiles, outputs, grads, held, held_output


def feed_first(info, x, mixed_t, cot, gains, pieces):
    rows, width = x.shape
    units = pieces[0].shape[2]
    count = len(pieces)
    steps, whole, tokens, features, gain_spec, tiles, outputs, grads, held, held_output = feed_specs(
        pieces, rows, width
    )
    wide = jax.ShapeDtypeStruct((rows, width), f32)
    return pl.pallas_call(
        functools.partial(feed_first_kernel, count),
        out_shape=(
            wide,
            jax.ShapeDtypeStruct((rows, width), bf16),
            wide,
            wide,
            jax.ShapeDtypeStruct((3, width, units), bf16),
            jax.ShapeDtypeStruct((width, width), bf16),
        ),
        grid_spec=pltpu.PrefetchScalarGridSpec(
            num_scalar_prefetch=1,
            grid=(steps,),
            in_specs=[tiles] * count
            + [outputs] * count
            + [tokens, features, tokens, gain_spec],
            out_specs=(tokens, tokens, tokens, tokens, grads, whole((width, width))),
            scratch_shapes=[
                pltpu.VMEM((width, rows), bf16),
                pltpu.VMEM((width, rows), bf16),
                held,
                held_output,
            ],
        ),
        compiler_params=pltpu.CompilerParams(vmem_limit_bytes=48 * 1024 * 1024),
        cost_estimate=pl.CostEstimate(
            flops=20 * rows * width * units, bytes_accessed=12 * units * width, transcendentals=0
        ),
        name="feed_first",
    )(info, *pieces, *pieces, x, mixed_t, cot, gains)


def feed_second(info, middle, mixed_t, cot, second, layer_sum, d_second, gains, output_t, pieces):
    rows, width = middle.shape
    units = pieces[0].shape[2]
    count = len(pieces)
    steps, whole, tokens, features, gain_spec, tiles, outputs, grads, held, held_output = feed_specs(
        pieces, rows, width
    )
    return pl.pallas_call(
        functools.partial(feed_second_kernel, count),
        out_shape=(
            jax.ShapeDtypeStruct((rows, width), bf16),
            jax.ShapeDtypeStruct((rows, width), f32),
            jax.ShapeDtypeStruct((width, rows), bf16),
            jax.ShapeDtypeStruct((KV_HEADS, GROUP, rows), f32),
            jax.ShapeDtypeStruct((1, width), f32),
            jax.ShapeDtypeStruct((width, width), bf16),
            jax.ShapeDtypeStruct((3, width, units), bf16),
        ),
        grid_spec=pltpu.PrefetchScalarGridSpec(
            num_scalar_prefetch=1,
            grid=(steps,),
            in_specs=[tiles] * count
            + [tokens, features, tokens, tokens, tokens, tokens, gain_spec, whole((width, width))],
            out_specs=(
                tokens,
                tokens,
                features,
                whole((KV_HEADS, GROUP, rows)),
                whole((1, width)),
                whole((width, width)),
                grads,
            ),
            scratch_shapes=[
                pltpu.VMEM((width, rows), bf16),
                pltpu.VMEM((width, rows), bf16),
                pltpu.VMEM((rows, width), f32),
                pltpu.VMEM((rows, width), f32),
                held,
            ],
        ),
        compiler_params=pltpu.CompilerParams(vmem_limit_bytes=48 * 1024 * 1024),
        cost_estimate=pl.CostEstimate(
            flops=20 * rows * width * units, bytes_accessed=12 * units * width, transcendentals=0
        ),
        name="feed_second",
    )(info, *pieces, middle, mixed_t, cot, second, layer_sum, d_second, gains, output_t)


def shard_pieces(piece):
    return [piece] + [swap(piece, "shard", mask) for mask in range(1, lax.axis_size("shard"))]


def in_order(pieces):
    me = lax.axis_index("shard")
    out = jnp.zeros((len(pieces),) + pieces[0].shape, pieces[0].dtype)
    for mask, piece in enumerate(pieces):
        out = lax.dynamic_update_index_in_dim(out, piece, me ^ mask, 0)
    return out


def scatter_shards(pieces):
    count = lax.axis_size("shard")
    me = lax.axis_index("shard")
    total = lax.dynamic_index_in_dim(pieces, me, 0, False).astype(f32)
    for mask in range(1, count):
        sent = lax.dynamic_index_in_dim(pieces, me ^ mask, 0, False).astype(bf16)
        total = total + swap(sent, "shard", mask).astype(f32)
    return total


def sum_context(value):
    total = value.astype(f32)
    low = value.astype(bf16)
    for mask in range(1, lax.axis_size("context")):
        total = total + swap(low, "context", mask).astype(f32)
    return total


def per_device(
    hidden_in,
    segment_ids,
    norm_gains,
    w_query,
    w_key,
    w_value,
    w_output,
    w_gate,
    w_up,
    w_down,
    cotangent,
):
    rows, width = hidden_in.shape[1], hidden_in.shape[2]
    half = rows // 2
    seg_row = segment_ids[0]
    length = seg_row.shape[0]
    shards = lax.axis_size("shard")
    contexts = lax.axis_size("context")
    blocks = lax.axis_size(SEQ)
    me = lax.axis_index(SEQ)
    core = lax.axis_index("tensor")
    context = lax.axis_index("context")
    part = w_query.shape[1]
    kv_part = w_key.shape[1]
    kv_width = kv_part * shards
    units = w_gate.shape[0]
    head_size = width // HEADS
    scale = head_size**-0.5

    rows_own = hidden_in[0]
    near = [rows_own] + [swap(rows_own, "context", mask) for mask in range(1, contexts)]
    x_pieces = []
    for item in near:
        x_pieces += [item, swap(item, "tensor", 1)]

    gain_rows = part - 2 * kv_part
    key_values = jnp.concatenate(
        [w_key.T, w_value.T, jnp.pad(norm_gains, ((0, gain_rows - 2), (0, width - part)))], axis=0
    )
    pack = jnp.where(core == 0, w_query.T, key_values)
    pack_mine = in_order(shard_pieces(pack))
    pack_theirs = swap(pack_mine, "tensor", 1)
    query_t = jnp.where(core == 0, pack_mine, pack_theirs).reshape(width, width)
    other = jnp.where(core == 0, pack_theirs, pack_mine)
    key_t = other[:, :kv_part].reshape(kv_width, width)
    value_t = other[:, kv_part : 2 * kv_part].reshape(kv_width, width)
    gains = other[:, 2 * kv_part : 2 * kv_part + 2, :part]
    gains = gains.transpose(1, 0, 2).reshape(2, width).astype(f32)

    later = jnp.stack([w_gate.T, w_up.T, w_down.T, jnp.pad(w_output.T, ((0, 0), (0, units - width)))])
    later, pack = lax.optimization_barrier((later, pack))
    later_pieces = shard_pieces(later)

    cot_own = cotangent[0]
    cot = jnp.concatenate(
        [cot_own[:half], lax.ppermute(cot_own[half:], SEQ, flip(blocks, blocks - 1))], axis=0
    )

    starts = doc_starts(seg_row)
    index = jnp.arange(length, dtype=jnp.int32)
    order = jnp.arange(blocks, dtype=jnp.int32) ^ me
    place = (order[:, None] * rows + jnp.arange(rows, dtype=jnp.int32)[None, :]).reshape(-1)
    placed_starts = jnp.concatenate(
        [lax.dynamic_slice_in_dim(starts, (me ^ r) * rows, rows, 0) for r in range(blocks)]
    )
    positions = (place - placed_starts).astype(f32)
    frequency = rope_base ** (-jnp.arange(head_size // 2, dtype=f32) * 2.0 / head_size)
    angles = frequency[:, None] * positions[None, :]
    cosine, sine = jnp.cos(angles), jnp.sin(angles)

    def chunks(array, axis):
        return jnp.concatenate(
            [
                lax.slice_in_dim(array, 0, half, axis=axis),
                lax.slice_in_dim(array, length - half, length, axis=axis),
            ],
            axis=axis,
        )

    bounds = jnp.stack([chunks(placed_starts, 0), chunks(place, 0)])
    info = [me]
    for first in (0, half):
        chunk_start = bounds[1, first]
        low = bounds[0, first] // rows
        high = (chunk_start + half + rows - 1) // rows
        full_from = jnp.clip((bounds[0, first + half - 1] + rows - 1) // rows, low, high)
        full_to = jnp.clip((chunk_start + 1) // rows, full_from, high)
        info += [low, full_from, full_to, high]
    info = jnp.stack(info).astype(jnp.int32)

    a_all, keys, keys_t, values, values_t = project(x_pieces, key_t, value_t, gains, cosine, sine)
    a = chunks(a_all, 0)
    x = jnp.concatenate([x_pieces[0][:half], x_pieces[-1][half:]], axis=0)
    cos_q, sin_q = chunks(cosine, 1), chunks(sine, 1)
    queries_t = (turn(mm(query_t, a, 1, 1), cos_q, sin_q, 1.0).astype(bf16) * scale).astype(bf16)

    mixed_t, log_total = attend(info, queries_t, keys, values_t, bounds, rows)

    mixed_t, later_pieces = lax.optimization_barrier((mixed_t, later_pieces))
    their_pieces = [swap(item[:3], "tensor", 1) for item in later_pieces]
    if part % 16:
        later_pieces = [in_order(later_pieces).transpose(1, 0, 2, 3).reshape(4, width, units)]
        their_pieces = [in_order(their_pieces).transpose(1, 0, 2, 3).reshape(3, width, units)]
    shard = jnp.reshape(lax.axis_index("shard"), (1,)).astype(jnp.int32)
    middle, second, layer_sum, d_second, grads_mine, output_t = feed_first(
        shard, x, mixed_t, cot, gains, later_pieces
    )
    layer_chunks, middle_grad, mixed_grad_t, delta, gain_grad_second, grad_output_t, grads_theirs = (
        feed_second(
            shard, middle, mixed_t, cot, second, layer_sum, d_second, gains, output_t, their_pieces
        )
    )
    layer_value = jnp.concatenate(
        [
            layer_chunks[:half],
            lax.ppermute(layer_chunks[half:], SEQ, flip(blocks, blocks - 1)),
        ],
        axis=0,
    )

    half_width = width // 2
    wide = units
    left, right = grad_output_t[:, :half_width], grad_output_t[:, half_width:]
    output_keep = jnp.where(core == 0, left, right)
    output_give = jnp.where(core == 0, right, left)
    mixed_grad_t, grads_theirs, output_give = lax.optimization_barrier(
        (mixed_grad_t, grads_theirs, output_give)
    )
    ff_got = swap(grads_theirs, "tensor", 1)
    output_got = swap(output_give, "tensor", 1)

    def back(group, info):
        return attend_back(
            group,
            info,
            queries_t,
            mixed_grad_t,
            keys,
            keys_t,
            values,
            log_total,
            delta,
            bounds,
            rows,
            scale,
        )

    back_0 = back(0, info)
    info, ff_got, output_got, back_0 = lax.optimization_barrier((info, ff_got, output_got, back_0))
    ff_sum = grads_mine.astype(f32) + ff_got.astype(f32)
    output_sum = output_keep.astype(f32) + output_got.astype(f32)
    both = jnp.concatenate(
        [ff_sum.astype(bf16), jnp.pad(output_sum.astype(bf16), ((0, 0), (0, wide - half_width)))[None]]
    )
    if contexts == 4:
        owned = lax.dynamic_index_in_dim(both, context, 0, False)
        give = [lax.dynamic_index_in_dim(both, context ^ mask, 0, False) for mask in range(1, 4)]
        info, owned, give = lax.optimization_barrier((info, owned, give))
        got = [swap(item, "context", mask + 1) for mask, item in enumerate(give)]
    back_1 = back(1, info)
    info, back_1 = lax.optimization_barrier((info, back_1))
    back_2 = back(2, info)
    if contexts == 4:
        back_2, got = lax.optimization_barrier((back_2, got))
        owned = owned.astype(f32)
        for item in got:
            owned = owned + item.astype(f32)
        owned = scatter_shards(owned.astype(bf16).reshape(shards, part, wide))
        owned_low = owned.astype(bf16)
        final = jnp.zeros((4, part, wide), bf16)
        final = lax.dynamic_update_index_in_dim(final, owned_low, context, 0)
        for mask in range(1, 4):
            final = lax.dynamic_update_index_in_dim(
                final, swap(owned_low, "context", mask), context ^ mask, 0
            )
    else:
        large = both.reshape(4, shards, part, wide).transpose(1, 0, 2, 3)
        final = lax.psum(scatter_shards(large).astype(bf16), "context")
    final = final.astype(f32)
    grad_gate, grad_up, grad_down = final[0].T, final[1].T, final[2].T
    output_half = final[3, :, :half_width]
    output_other = swap(output_half.astype(bf16), "tensor", 1).astype(f32)
    grad_output = jnp.where(
        core == 0,
        jnp.concatenate([output_half, output_other], axis=1),
        jnp.concatenate([output_other, output_half], axis=1),
    ).T

    dq_t, dk_t, dv_t = [
        jnp.concatenate(list(parts), axis=0) for parts in zip(back_0, back_1, back_2)
    ]
    dkl_t = turn(dk_t, cosine, sine, -1.0).astype(bf16)
    dv_t = dv_t.astype(bf16)
    dql_t = turn(dq_t, cos_q, sin_q, -1.0).astype(bf16)

    terms = jnp.concatenate([dkl_t, dv_t], axis=0)
    by_block = [lax.slice_in_dim(terms, r * rows, (r + 1) * rows, axis=1) for r in range(blocks)]
    paired = [
        by_block[2 * c].astype(f32) + swap(by_block[2 * c + 1], "tensor", 1).astype(f32)
        for c in range(contexts)
    ]
    owned_terms = paired[0]
    for mask in range(1, contexts):
        owned_terms = owned_terms + swap(paired[mask].astype(bf16), "context", mask).astype(f32)
    owned_terms = owned_terms.astype(bf16)

    grad_query_t = mm(dql_t, a, 1, 0)
    grad_key_t = mm(dkl_t, a_all, 1, 0)
    grad_value_t = mm(dv_t, a_all, 1, 0)
    gain_grad_first = (
        jnp.sum(query_t.astype(f32) * grad_query_t, axis=0)
        + jnp.sum(key_t.astype(f32) * grad_key_t, axis=0)
        + jnp.sum(value_t.astype(f32) * grad_value_t, axis=0)
    ) / gains[0]
    gain_grads = jnp.concatenate([gain_grad_first[None], gain_grad_second], axis=0)
    gain_grads = gain_grads.reshape(2, shards, part).transpose(1, 0, 2)
    query_pack = grad_query_t.astype(bf16).reshape(shards, part, width)
    other_pack = jnp.concatenate(
        [
            grad_key_t.reshape(shards, kv_part, width),
            grad_value_t.reshape(shards, kv_part, width),
            jnp.pad(gain_grads, ((0, 0), (0, gain_rows - 2), (0, width - part))),
        ],
        axis=1,
    ).astype(bf16)
    keep = jnp.where(core == 0, query_pack, other_pack)
    give = jnp.where(core == 0, other_pack, query_pack)
    both = keep.astype(f32) + swap(give, "tensor", 1).astype(f32)
    small = sum_context(scatter_shards(both.astype(bf16))).astype(bf16)
    small_other = swap(small, "tensor", 1)
    grad_query = jnp.where(core == 0, small, small_other).astype(f32).T
    small = jnp.where(core == 0, small_other, small).astype(f32)
    grad_key = small[:kv_part].T
    grad_value = small[kv_part : 2 * kv_part].T
    grad_gains = small[2 * kv_part : 2 * kv_part + 2, :part]

    chunk_grad = middle_grad + norm_back(
        mm(dql_t, query_t, 0, 0), x.astype(f32), gains[0]
    )
    back = lax.ppermute(chunk_grad[half:].astype(bf16), SEQ, flip(blocks, blocks - 1))
    kv_grad = mm(owned_terms[:kv_width], key_t, 0, 0) + mm(owned_terms[kv_width:], value_t, 0, 0)
    grad_hidden = jnp.concatenate([chunk_grad[:half], back.astype(f32)], axis=0) + norm_back(
        kv_grad, rows_own.astype(f32), gains[0]
    )
    return (
        layer_value[None],
        grad_hidden[None],
        grad_gains,
        grad_query,
        grad_key,
        grad_value,
        grad_output,
        grad_gate,
        grad_up,
        grad_down,
    )


def solution(mesh):
    return jax.shard_map(
        per_device,
        mesh=mesh,
        in_specs=(
            P("shard", ("context", "tensor"), None),
            P("shard", None),
            P(None, "shard"),
            P(None, "shard"),
            P(None, "shard"),
            P(None, "shard"),
            P(None, "shard"),
            P("tensor", "shard"),
            P("tensor", "shard"),
            P("tensor", "shard"),
            P("shard", ("context", "tensor"), None),
        ),
        out_specs=(
            P("shard", ("context", "tensor"), None),
            P("shard", ("context", "tensor"), None),
            P(None, "shard"),
            P(None, "shard"),
            P(None, "shard"),
            P(None, "shard"),
            P(None, "shard"),
            P("tensor", "shard"),
            P("tensor", "shard"),
            P("tensor", "shard"),
        ),
        check_vma=False,
    )
```

```python
import functools

import jax
import jax.numpy as jnp
from jax import lax
from jax.experimental import pallas as pl
from jax.experimental.pallas import tpu as pltpu
from jax.sharding import PartitionSpec as P

HEADS = 9
KV_HEADS = 3
DOCS = 4
GROUP = HEADS // KV_HEADS

rope_base = 100000.0
norm_eps = 1e-05
masked_score = -1e30

VMEM = 60 * 1024 * 1024
f32 = jnp.float32
bf16 = jnp.bfloat16
SEQ = ("context", "tensor")


def mm(left, right, left_dim, right_dim):
    return lax.dot_general(
        left, right, (((left_dim,), (right_dim,)), ((), ())), preferred_element_type=f32
    )


def flip(count, mask):
    return [(i, i ^ mask) for i in range(count)]


def swap(value, axis, mask):
    return lax.ppermute(value, axis, flip(lax.axis_size(axis), mask))


def doc_starts(seg_row):
    one_hot = (seg_row[None, :] == jnp.arange(DOCS, dtype=jnp.int32)[:, None]).astype(jnp.int32)
    doc_counts = jnp.sum(one_hot, axis=1)
    return jnp.cumsum(doc_counts) - doc_counts


def column_rms(hidden):
    return lax.rsqrt(jnp.mean(hidden * hidden, axis=0, keepdims=True) + norm_eps)


def column_norm_back(grad, hidden, gain):
    inverse = column_rms(hidden)
    unit = hidden * inverse
    scaled = grad * gain
    return (scaled - unit * jnp.mean(scaled * unit, axis=0, keepdims=True)) * inverse


def turn_head(head, cosine, sine, sign):
    half = cosine.shape[0]
    first, second = head[:half], head[half:]
    return jnp.concatenate(
        [first * cosine - sign * (second * sine), second * cosine + sign * (first * sine)], axis=0
    )


def doc_start(info_ref, index):
    start = jnp.int32(0)
    for doc in range(1, DOCS):
        start = jnp.where(index >= info_ref[1 + doc], info_ref[1 + doc], start)
    return start


def chunk_start(info_ref, chunk, blocks, size):
    me = info_ref[0]
    return jnp.where(chunk == 0, me * 2 * size, (blocks - 1 - me) * 2 * size + size)


def key_ranges(info_ref, chunk, blocks, key_block):
    size = key_block // 2
    first = chunk_start(info_ref, chunk, blocks, size)
    low = doc_start(info_ref, first) // key_block
    high = (first + size + key_block - 1) // key_block
    full_from = (doc_start(info_ref, first + size - 1) + key_block - 1) // key_block
    full_from = jnp.minimum(jnp.maximum(full_from, low), high)
    full_to = jnp.minimum(jnp.maximum(first // key_block, full_from), high)
    return low, full_from, full_to, high


def allowed_mask(info_ref, block, key_block, chunk, blocks):
    size = key_block // 2
    first = chunk_start(info_ref, chunk, blocks, size)
    index = first + lax.broadcasted_iota(jnp.int32, (1, size), 1)
    start = doc_start(info_ref, index)
    key_index = block * key_block + lax.broadcasted_iota(jnp.int32, (key_block, size), 0)
    return (key_index >= start) & (key_index <= index)


def side_by_side(ref, size):
    return jnp.concatenate([ref[m * size : (m + 1) * size, :] for m in range(GROUP)], axis=1)


def forward_kernel(key_block, group, info_ref, *refs):
    if group:
        refs = refs[2:]
    q_ref, k_ref, vt_ref, o_ref, lse_ref, m_ref, l_ref, acc_ref, q_side = refs
    chunk = pl.program_id(1)
    me = info_ref[0]
    size = k_ref.shape[2]
    tokens = q_ref.shape[1]
    blocks = k_ref.shape[1] // key_block
    m_ref[...] = jnp.full_like(m_ref, masked_score)
    acc_ref[...] = jnp.zeros_like(acc_ref)
    q_side[...] = side_by_side(q_ref, size)

    def step(block, masked):
        place = pl.multiple_of((block ^ me) * key_block, key_block)
        keys = k_ref[0, pl.ds(place, key_block), :]
        values = vt_ref[:, pl.ds(place, key_block)]
        scores = mm(keys, q_side[...], 1, 0)
        if masked:
            mask = allowed_mask(info_ref, block, key_block, chunk, blocks)
            scores = jnp.concatenate(
                [
                    jnp.where(mask, scores[:, m * tokens : (m + 1) * tokens], masked_score)
                    for m in range(GROUP)
                ],
                axis=1,
            )
        old = m_ref[...]
        new = jnp.maximum(old, jnp.max(scores, axis=0, keepdims=True))
        factor = jnp.exp(old - new)
        weights = jnp.exp(scores - new)
        m_ref[...] = new
        values = jnp.concatenate([values, jnp.ones((16, key_block), bf16)], axis=0)
        acc_ref[...] = acc_ref[...] * factor + mm(values, weights.astype(bf16), 1, 0)

    low, full_from, full_to, high = key_ranges(info_ref, chunk, blocks, key_block)
    pl.loop(low, full_from)(lambda b: step(b, True))
    pl.loop(full_from, full_to)(lambda b: step(b, False))
    pl.loop(full_to, high)(lambda b: step(b, True))
    for member in range(GROUP):
        rows = slice(member * size, (member + 1) * size)
        lanes = slice(member * tokens, (member + 1) * tokens)
        total = acc_ref[size : size + 1, lanes]
        o_ref[rows, :] = acc_ref[:size, lanes] / total
        lse_ref[0, member : member + 1, :] = m_ref[:, lanes] + jnp.log(total)


def backward_kernel(key_block, scale, group, *refs):
    if group:
        refs = refs[:1] + refs[4:]
    (
        info_ref, q_ref, do_ref, k_ref, kt_ref, v_ref, lse_ref, delta_ref,
        cos_ref, sin_ref, cosq_ref, sinq_ref,
        dq_ref, even_ref, odd_ref, dk_ref, dv_ref, dq_sum, q_side, do_side,
    ) = refs
    chunk = pl.program_id(0)
    me = info_ref[0]
    size = k_ref.shape[2]
    blocks = dk_ref.shape[0]
    tokens = q_ref.shape[1]
    dq_sum[...] = jnp.zeros_like(dq_sum)
    q_side[...] = side_by_side(q_ref, size)
    do_side[...] = side_by_side(do_ref, size)
    log_total = jnp.concatenate([lse_ref[0, m : m + 1, :] for m in range(GROUP)], axis=1)
    delta = jnp.concatenate([delta_ref[0, m : m + 1, :] for m in range(GROUP)], axis=1)

    @pl.when(chunk == 0)
    def _():
        dk_ref[...] = jnp.zeros_like(dk_ref)
        dv_ref[...] = jnp.zeros_like(dv_ref)

    def step(block, masked):
        spot = block ^ me
        place = pl.multiple_of(spot * key_block, key_block)
        keys = k_ref[0, pl.ds(place, key_block), :]
        values = v_ref[0, pl.ds(place, key_block), :]
        keys_t = kt_ref[:, pl.ds(place, key_block)]
        scores = mm(keys, q_side[...], 1, 0)
        if masked:
            mask = allowed_mask(info_ref, block, key_block, chunk, blocks)
            scores = jnp.concatenate(
                [
                    jnp.where(mask, scores[:, m * tokens : (m + 1) * tokens], masked_score)
                    for m in range(GROUP)
                ],
                axis=1,
            )
        probs = jnp.exp(scores - log_total)
        prob_grad = mm(values, do_side[...], 1, 0)
        raw = (probs * (prob_grad - delta)).astype(bf16)
        dv = mm(do_side[...], probs.astype(bf16), 1, 1)
        dk = mm(q_side[...], raw, 1, 1)
        dq_sum[...] += mm(keys_t, raw, 1, 0)
        dk_ref[spot] += dk
        dv_ref[spot] += dv

    low, full_from, full_to, high = key_ranges(info_ref, chunk, blocks, key_block)
    pl.loop(low, full_from)(lambda b: step(b, True))
    pl.loop(full_from, full_to)(lambda b: step(b, False))
    pl.loop(full_to, high)(lambda b: step(b, True))
    for member in range(GROUP):
        rows = slice(member * size, (member + 1) * size)
        dq_ref[rows, :] = turn_head(
            dq_sum[:, member * tokens : (member + 1) * tokens] * scale, cosq_ref[...], sinq_ref[...], -1.0).astype(
            bf16
        )

    @pl.when(chunk == 1)
    def _():
        for block in range(blocks):
            columns = slice(block * key_block, (block + 1) * key_block)
            out_ref = odd_ref if block % 2 else even_ref
            out_ref[block // 2, :size, :] = turn_head(
                dk_ref[block], cos_ref[:, columns], sin_ref[:, columns], -1.0
            ).astype(bf16)
            out_ref[block // 2, size:, :] = dv_ref[block].astype(bf16)


def attend(group, groups, earlier, info, queries_t, keys, values_t, key_block):
    length, size = keys.shape[1], keys.shape[2]
    tokens = queries_t.shape[1]
    chunk = tokens // 2
    wide = GROUP * size
    head_block = pl.BlockSpec((wide, chunk), lambda g, c, info: (group + g, c))
    stat_block = pl.BlockSpec((1, GROUP, chunk), lambda g, c, info: (group + g, 0, c))
    elements = groups * GROUP * tokens * length // 2
    return pl.pallas_call(
        functools.partial(forward_kernel, key_block, group),
        out_shape=(
            jax.ShapeDtypeStruct((HEADS * size, tokens), f32),
            jax.ShapeDtypeStruct((KV_HEADS, GROUP, tokens), f32),
        ),
        grid_spec=pltpu.PrefetchScalarGridSpec(
            num_scalar_prefetch=1,
            grid=(groups, 2),
            in_specs=[pl.BlockSpec(memory_space=pl.ANY)] * len(earlier)
            + [
                head_block,
                pl.BlockSpec((1, length, size), lambda g, c, info: (group + g, 0, 0)),
                pl.BlockSpec((size, length), lambda g, c, info: (group + g, 0)),
            ],
            out_specs=(head_block, stat_block),
            scratch_shapes=[
                pltpu.VMEM((1, GROUP * chunk), f32),
                pltpu.VMEM((1, GROUP * chunk), f32),
                pltpu.VMEM((size + 16, GROUP * chunk), f32),
                pltpu.VMEM((size, GROUP * chunk), bf16),
            ],
        ),
        input_output_aliases={1 + number: number for number in range(len(earlier))},
        compiler_params=pltpu.CompilerParams(vmem_limit_bytes=VMEM),
        cost_estimate=pl.CostEstimate(
            flops=16 * elements * size, bytes_accessed=4 * 1024 * 1024, transcendentals=elements
        ),
        name="attend",
    )(info, *earlier, queries_t, keys, values_t)


def attend_back(
    group, earlier, info, queries_t, grads_t, keys, keys_t, values, log_total, delta,
    cosine, sine, cos_q, sin_q, key_block, scale,
):
    length, size = keys.shape[1], keys.shape[2]
    tokens = queries_t.shape[1]
    chunk = tokens // 2
    wide = GROUP * size
    blocks = length // key_block
    head_block = pl.BlockSpec((wide, chunk), lambda c, info: (group, c))
    stat_block = pl.BlockSpec((1, GROUP, chunk), lambda c, info: (group, 0, c))
    token_block = pl.BlockSpec((1, length, size), lambda c, info: (group, 0, 0))
    feature_block = pl.BlockSpec((size, length), lambda c, info: (group, 0))
    table = pl.BlockSpec((size // 2, length), lambda c, info: (0, 0))
    table_q = pl.BlockSpec((size // 2, chunk), lambda c, info: (0, c))
    terms = pl.BlockSpec((blocks // 2, 2 * size, key_block), lambda c, info: (0, group, 0))
    elements = GROUP * tokens * length // 2
    terms_shape = jax.ShapeDtypeStruct((blocks // 2, KV_HEADS * 2 * size, key_block), bf16)
    return pl.pallas_call(
        functools.partial(backward_kernel, key_block, scale, group),
        out_shape=(jax.ShapeDtypeStruct((HEADS * size, tokens), bf16), terms_shape, terms_shape),
        grid_spec=pltpu.PrefetchScalarGridSpec(
            num_scalar_prefetch=1,
            grid=(2,),
            in_specs=[pl.BlockSpec(memory_space=pl.ANY)] * len(earlier)
            + [
                head_block, head_block, token_block, feature_block, token_block, stat_block, stat_block,
                table, table, table_q, table_q,
            ],
            out_specs=(head_block, terms, terms),
            scratch_shapes=[
                pltpu.VMEM((blocks, size, key_block), f32),
                pltpu.VMEM((blocks, size, key_block), f32),
                pltpu.VMEM((size, GROUP * chunk), f32),
                pltpu.VMEM((size, GROUP * chunk), bf16),
                pltpu.VMEM((size, GROUP * chunk), bf16),
            ],
        ),
        input_output_aliases={1 + number: number for number in range(len(earlier))},
        compiler_params=pltpu.CompilerParams(vmem_limit_bytes=VMEM),
        cost_estimate=pl.CostEstimate(
            flops=40 * elements * size, bytes_accessed=4 * 1024 * 1024, transcendentals=elements
        ),
        name="attend_back",
    )(
        info, *earlier, queries_t, grads_t, keys, keys_t, values, log_total, delta,
        cosine, sine, cos_q, sin_q,
    )


def unpack_kernel(count, kv_part, info_ref, *refs):
    mine, theirs = refs[:count], refs[count : 2 * count]
    query_ref, key_ref, value_ref, gain_ref = refs[2 * count :]
    first = info_ref[1] == 0
    mask = 0
    for number in range(count):
        for row in range(mine[number].shape[0]):
            spot = info_ref[0] ^ mask
            left, right = mine[number][row], theirs[number][row]
            query_ref[spot] = jnp.where(first, left, right)
            other = jnp.where(first, right, left)
            key_ref[spot] = other[:kv_part]
            value_ref[spot] = other[kv_part : 2 * kv_part]
            gain_ref[spot] = other[2 * kv_part :]
            mask += 1


def unpack(info, mine, theirs, kv_part):
    count = len(mine)
    total = sum(item.shape[0] for item in mine)
    part, width = mine[0].shape[1:]
    whole = lambda shape: pl.BlockSpec(shape, lambda i, info: (0,) * len(shape))
    shapes = [(total, size, width) for size in (part, kv_part, kv_part, part - 2 * kv_part)]
    return pl.pallas_call(
        functools.partial(unpack_kernel, count, kv_part),
        out_shape=[jax.ShapeDtypeStruct(shape, bf16) for shape in shapes],
        grid_spec=pltpu.PrefetchScalarGridSpec(
            num_scalar_prefetch=1,
            grid=(1,),
            in_specs=[whole(item.shape) for item in (*mine, *theirs)],
            out_specs=[whole(shape) for shape in shapes],
        ),
        name="unpack",
    )(info, *mine, *theirs)


def project_kernel(layout, arrays, scale, *refs):
    pieces = len(layout)
    x_refs = [refs[array].at[row] for array, row in layout]
    query_ref, key_ref, value_ref, gain_ref, cos_ref, sin_ref = refs[arrays : arrays + 6]
    a_ref, k_ref, kt_ref, v_ref, vt_ref, q_ref, aq_ref, xq_ref = refs[arrays + 6 : arrays + 14]
    held, sems, cos_q, sin_q = refs[arrays + 14 :]
    step = pl.program_id(0)
    tokens = xq_ref.shape[1]
    chunk = tokens // 2

    @pl.when(step == 0)
    def _():
        for number in range(pieces):
            pltpu.make_async_copy(x_refs[number], held.at[number], sems.at[number]).start()

    for number in range(pieces):

        @pl.when(step == number)
        def _(number=number):
            pltpu.make_async_copy(x_refs[number], held.at[number], sems.at[number]).wait()

    x_low = held[step]
    x = x_low.astype(f32)
    a = (x * column_rms(x) * gain_ref[:, 0:1]).astype(bf16)
    a_ref[0] = a
    cosine, sine = cos_ref[...], sin_ref[...]
    k_lin = mm(key_ref[...], a, 1, 0)
    v_lin = mm(value_ref[...], a, 1, 0)
    vt_ref[...] = v_lin.astype(bf16)
    size = k_ref.shape[2]
    for group in range(KV_HEADS):
        rows = slice(group * size, (group + 1) * size)
        turned = turn_head(k_lin[rows], cosine, sine, 1.0)
        kt_ref[rows, :] = turned.astype(bf16)
        k_ref[group] = turned.T.astype(bf16)
        v_ref[group] = v_lin[rows].T.astype(bf16)

    @pl.when(step == 0)
    def _():
        aq_ref[:, :chunk] = a[:, :chunk]
        xq_ref[:, :chunk] = x_low[:, :chunk]
        cos_q[:, :chunk] = cosine[:, :chunk]
        sin_q[:, :chunk] = sine[:, :chunk]

    @pl.when(step == pieces - 1)
    def _():
        aq_ref[:, chunk:] = a[:, chunk:]
        xq_ref[:, chunk:] = x_low[:, chunk:]
        cos_q[:, chunk:] = cosine[:, chunk:]
        sin_q[:, chunk:] = sine[:, chunk:]
        q_lin = mm(query_ref[...], aq_ref[...], 1, 0)
        for head in range(HEADS):
            rows = slice(head * size, (head + 1) * size)
            q_ref[rows, :] = (
                turn_head(q_lin[rows], cos_q[...], sin_q[...], 1.0).astype(bf16) * scale
            ).astype(bf16)


def project(x_arrays, layout, query_t, key_t, value_t, gains, cosine, sine, scale):
    pieces = len(layout)
    arrays = len(x_arrays)
    width, rows = x_arrays[0].shape[1:]
    kv_width = key_t.shape[0]
    size = kv_width // KV_HEADS
    length = pieces * rows
    whole = lambda array: pl.BlockSpec(array.shape, lambda i: (0,) * array.ndim)
    table = pl.BlockSpec((size // 2, rows), lambda i: (0, i))
    by_token = pl.BlockSpec((KV_HEADS, rows, size), lambda i: (0, i, 0))
    by_feature = pl.BlockSpec((kv_width, rows), lambda i: (0, i))
    own = pl.BlockSpec((width, rows), lambda i: (0, 0))
    own_shape = jax.ShapeDtypeStruct((width, rows), bf16)
    return pl.pallas_call(
        functools.partial(project_kernel, layout, arrays, scale),
        out_shape=(
            jax.ShapeDtypeStruct((pieces, width, rows), bf16),
            jax.ShapeDtypeStruct((KV_HEADS, length, size), bf16),
            jax.ShapeDtypeStruct((kv_width, length), bf16),
            jax.ShapeDtypeStruct((KV_HEADS, length, size), bf16),
            jax.ShapeDtypeStruct((kv_width, length), bf16),
            own_shape,
            own_shape,
            own_shape,
        ),
        grid=(pieces,),
        in_specs=[pl.BlockSpec(memory_space=pl.ANY)] * arrays
        + [whole(query_t), whole(key_t), whole(value_t), whole(gains), table, table],
        out_specs=(
            pl.BlockSpec((1, width, rows), lambda i: (i, 0, 0)),
            by_token,
            by_feature,
            by_token,
            by_feature,
            own,
            own,
            own,
        ),
        scratch_shapes=[
            pltpu.VMEM((pieces, width, rows), bf16),
            pltpu.SemaphoreType.DMA((pieces,)),
            pltpu.VMEM((size // 2, rows), f32),
            pltpu.VMEM((size // 2, rows), f32),
        ],
        compiler_params=pltpu.CompilerParams(vmem_limit_bytes=VMEM),
        cost_estimate=pl.CostEstimate(
            flops=8 * length * width * kv_width, bytes_accessed=8 * length * width, transcendentals=0
        ),
        name="project",
    )(*x_arrays, query_t, key_t, value_t, gains, cosine, sine)


def feed_tile(second, second_t, cot, cot_t, weights, grad_ref, sum_ref, db_ref):
    gate_t, up_t, down_t = weights
    gate = mm(second, gate_t, 1, 0)
    upward = mm(second, up_t, 1, 0)
    d_hidden = mm(cot, down_t, 1, 0)
    sig = 1.0 / (1.0 + jnp.exp(-gate))
    silu = gate * sig
    hidden = (silu * upward).astype(bf16)
    d_gate = (d_hidden * upward * sig * (1.0 + gate * (1.0 - sig))).astype(bf16)
    d_up = (d_hidden * silu).astype(bf16)
    sum_ref[...] += mm(down_t, hidden, 1, 1)
    db_ref[...] += mm(gate_t, d_gate, 1, 1) + mm(up_t, d_up, 1, 1)
    grad_ref[0] = mm(second_t, d_gate, 1, 0).astype(bf16)
    grad_ref[1] = mm(second_t, d_up, 1, 0).astype(bf16)
    grad_ref[2] = mm(cot_t, hidden, 1, 0).astype(bf16)


def hold_weights(info_ref, own_ref, other_refs, held):
    shard, context = info_ref[0], info_ref[2]
    for matrix in range(held.shape[0]):
        held[matrix, shard if held.shape[1] > 1 else 0] = own_ref[matrix]
    for number, other in enumerate(other_refs):
        for mask in range(1, held.shape[1]):
            held[context ^ number, shard ^ mask] = other[mask - 1]


def held_tiles(held, tile):
    lanes = pl.ds(pl.multiple_of(pl.program_id(0) * tile, tile), tile)
    return [
        held[matrix, :, :, lanes].reshape(held.shape[1] * held.shape[2], tile) for matrix in range(3)
    ]


def feed_first_kernel(count, info_ref, *refs):
    x_ref, o_ref, cot_ref, gain_ref = refs[count : count + 4]
    h_ref, second_ref, cot_rows, second_t, sum_ref, db_ref, grad_ref, output_ref = refs[
        count + 4 : count + 12
    ]
    held = refs[count + 12]
    width = x_ref.shape[0]

    @pl.when(pl.program_id(0) == 0)
    def _():
        hold_weights(info_ref, refs[0], refs[1:count], held)
        output_t = held[3].reshape(width, held.shape[3])[:, :width]
        output_ref[...] = output_t
        middle = x_ref[...].astype(f32) + mm(output_t, o_ref[...].astype(bf16), 1, 0)
        second = middle * column_rms(middle) * gain_ref[:, 1:2]
        h_ref[...] = middle
        second_t[...] = second.astype(bf16)
        second_ref[...] = second.T.astype(bf16)
        cot_rows[...] = cot_ref[...].astype(f32).T.astype(bf16)
        sum_ref[...] = middle
        db_ref[...] = jnp.zeros_like(db_ref)

    weights = held_tiles(held, grad_ref.shape[2])
    feed_tile(
        second_ref[...], second_t[...], cot_rows[...], cot_ref[...], weights, grad_ref, sum_ref, db_ref
    )


def feed_second_kernel(count, info_ref, *refs):
    (
        h_ref, o_ref, cot_ref, second_ref, cot_rows, second_t, sum_in_ref, db_in_ref, gain_ref, wo_ref,
    ) = refs[count : count + 10]
    layer_ref, mg_ref, do_ref, delta_ref, gg_ref, go_ref, grad_ref = refs[count + 10 : count + 17]
    sum_ref, db_ref, held = refs[count + 17 :]
    width = h_ref.shape[0]
    step = pl.program_id(0)

    @pl.when(step == 0)
    def _():
        hold_weights(info_ref, refs[0], refs[1:count], held)
        sum_ref[...] = sum_in_ref[...]
        db_ref[...] = db_in_ref[...]

    weights = held_tiles(held, grad_ref.shape[2])
    feed_tile(
        second_ref[...], second_t[...], cot_rows[...], cot_ref[...], weights, grad_ref, sum_ref, db_ref
    )

    @pl.when(step == pl.num_programs(0) - 1)
    def _():
        layer_ref[...] = sum_ref[...].astype(bf16)
        middle = h_ref[...]
        inverse = column_rms(middle)
        unit = middle * inverse
        grad = db_ref[...]
        gg_ref[...] = jnp.sum(grad * unit, axis=1, keepdims=True)
        scaled = grad * gain_ref[:, 1:2]
        back = (scaled - unit * jnp.mean(scaled * unit, axis=0, keepdims=True)) * inverse
        middle_grad = cot_ref[...].astype(f32) + back
        mg_ref[...] = middle_grad
        low = middle_grad.astype(bf16)
        d_o = mm(wo_ref[...].astype(f32).T.astype(bf16), low, 1, 0).astype(bf16)
        do_ref[...] = d_o
        mixed = o_ref[...]
        product = d_o.astype(f32) * mixed
        size = width // HEADS
        for head in range(HEADS):
            delta_ref[head // GROUP, head % GROUP : head % GROUP + 1, :] = jnp.sum(
                product[head * size : (head + 1) * size, :], axis=0, keepdims=True
            )
        go_ref[...] = jnp.zeros_like(go_ref)
        go_ref[:, :width] = mm(low, mixed.astype(bf16), 1, 1).astype(bf16)


def feed_specs(pieces, rows, width):
    part, units = pieces[0].shape[1:]
    tile = 256 if units % 256 == 0 else units
    whole = lambda shape: pl.BlockSpec(shape, lambda i, info: (0,) * len(shape))
    tokens = whole((rows, width))
    features = whole((width, rows))
    gains = whole((width, 2))
    weights = [whole(item.shape) for item in pieces]
    grads = pl.BlockSpec((3, width, tile), lambda i, info: (0, 0, i))
    held = pltpu.VMEM((4, width // part, part, units), bf16)
    return units // tile, whole, tokens, features, gains, weights, grads, held


def feed_first(info, x, mixed_t, cot, gains, pieces):
    width, rows = x.shape
    units = pieces[0].shape[2]
    count = len(pieces)
    steps, whole, tokens, features, gain_spec, weights, grads, held = feed_specs(pieces, rows, width)
    wide = jax.ShapeDtypeStruct((width, rows), f32)
    flat = jax.ShapeDtypeStruct((rows, width), bf16)
    return pl.pallas_call(
        functools.partial(feed_first_kernel, count),
        out_shape=(
            wide,
            flat,
            flat,
            jax.ShapeDtypeStruct((width, rows), bf16),
            wide,
            wide,
            jax.ShapeDtypeStruct((3, width, units), bf16),
            jax.ShapeDtypeStruct((width, width), bf16),
        ),
        grid_spec=pltpu.PrefetchScalarGridSpec(
            num_scalar_prefetch=1,
            grid=(steps,),
            in_specs=weights + [features, features, features, gain_spec],
            out_specs=(
                features, tokens, tokens, features, features, features, grads, whole((width, width)),
            ),
            scratch_shapes=[held],
        ),
        compiler_params=pltpu.CompilerParams(vmem_limit_bytes=VMEM),
        cost_estimate=pl.CostEstimate(
            flops=20 * rows * width * units, bytes_accessed=12 * units * width, transcendentals=0
        ),
        name="feed_first",
    )(info, *pieces, x, mixed_t, cot, gains)


def feed_second(
    info, middle, mixed_t, cot, second, cot_rows, second_t, layer_sum, d_second, gains, output_t, pieces
):
    width, rows = middle.shape
    units = pieces[0].shape[2]
    count = len(pieces)
    steps, whole, tokens, features, gain_spec, weights, grads, held = feed_specs(pieces, rows, width)
    return pl.pallas_call(
        functools.partial(feed_second_kernel, count),
        out_shape=(
            jax.ShapeDtypeStruct((width, rows), bf16),
            jax.ShapeDtypeStruct((width, rows), f32),
            jax.ShapeDtypeStruct((width, rows), bf16),
            jax.ShapeDtypeStruct((KV_HEADS, GROUP, rows), f32),
            jax.ShapeDtypeStruct((width, 1), f32),
            jax.ShapeDtypeStruct((width, units), bf16),
            jax.ShapeDtypeStruct((3, width, units), bf16),
        ),
        grid_spec=pltpu.PrefetchScalarGridSpec(
            num_scalar_prefetch=1,
            grid=(steps,),
            in_specs=weights
            + [
                features, features, features, tokens, tokens, features, features, features, gain_spec,
                whole((width, width)),
            ],
            out_specs=(
                features,
                features,
                features,
                whole((KV_HEADS, GROUP, rows)),
                whole((width, 1)),
                whole((width, units)),
                grads,
            ),
            scratch_shapes=[
                pltpu.VMEM((width, rows), f32),
                pltpu.VMEM((width, rows), f32),
                held,
            ],
        ),
        compiler_params=pltpu.CompilerParams(vmem_limit_bytes=VMEM),
        cost_estimate=pl.CostEstimate(
            flops=20 * rows * width * units, bytes_accessed=12 * units * width, transcendentals=0
        ),
        name="feed_second",
    )(
        info, *pieces, middle, mixed_t, cot, second, cot_rows, second_t, layer_sum, d_second, gains,
        output_t,
    )


def finish_kernel(
    info_ref, even_ref, odd_ref, dq_ref, a_ref, aq_ref, xq_ref, mg_ref, query_ref, key_ref, value_ref,
    gain_ref, gg2_ref, keep_ref, give_ref, chunk_ref, send_ref, kv_sum, gg_ref, q_sum,
):
    size = even_ref.shape[1] // (2 * KV_HEADS)
    step = pl.program_id(0)

    @pl.when(step == 0)
    def _():
        dq = dq_ref[...]
        grad_query = mm(dq, aq_ref[...], 1, 1)
        q_sum[...] = grad_query.astype(bf16)
        query_t = query_ref[...].astype(f32)
        gg_ref[...] = jnp.sum(query_t * grad_query, axis=0, keepdims=True)
        d_a = mm(query_t.T.astype(bf16), dq, 1, 0)
        chunk = mg_ref[...] + column_norm_back(d_a, xq_ref[...].astype(f32), gain_ref[:, 0:1])
        chunk_ref[...] = chunk
        send_ref[...] = chunk[:, chunk.shape[1] // 2 :].astype(bf16)
        kv_sum[...] = jnp.zeros_like(kv_sum)

    kv_sum[...] += mm(even_ref[0], a_ref[0], 1, 1) + mm(odd_ref[0], a_ref[1], 1, 1)

    @pl.when(step == pl.num_programs(0) - 1)
    def _():
        total = gg_ref[...]
        grads = [[], []]
        for group in range(KV_HEADS):
            rows = slice(group * size, (group + 1) * size)
            grad_key = kv_sum[2 * group * size : (2 * group + 1) * size, :]
            grad_value = kv_sum[(2 * group + 1) * size : (2 * group + 2) * size, :]
            grads[0].append(grad_key)
            grads[1].append(grad_value)
            total = total + jnp.sum(
                key_ref[rows, :].astype(f32) * grad_key + value_ref[rows, :].astype(f32) * grad_value,
                axis=0,
                keepdims=True,
            )
        gain_grad = jnp.concatenate([total / gain_ref[:, 0:1].T, gg2_ref[...].T], axis=0)
        grads = [jnp.concatenate(items, axis=0) for items in grads]
        shards, part, width = keep_ref.shape
        kv_part = KV_HEADS * size // shards
        first = info_ref[1] == 0
        for shard in range(shards):
            queries = q_sum[shard * part : (shard + 1) * part, :].astype(f32)
            rows = slice(shard * kv_part, (shard + 1) * kv_part)
            gain_rows = jnp.concatenate(
                [gain_grad, jnp.zeros((part - 2 * kv_part - 2, width), f32)], axis=0
            )
            others = jnp.concatenate([grads[0][rows], grads[1][rows], gain_rows], axis=0)
            keep_ref[shard] = jnp.where(first, queries, others).astype(bf16)
            give_ref[shard] = jnp.where(first, others, queries).astype(bf16)


def finish(info, even, odd, dq_t, a_all, a, x, middle_grad, query_t, key_t, value_t, gains, gain_second, shards):
    pairs, terms, rows = even.shape
    width = x.shape[0]
    kv_width = key_t.shape[0]
    pack = jax.ShapeDtypeStruct((shards, width // shards, width), bf16)
    whole = lambda shape: pl.BlockSpec(shape, lambda i, info: (0,) * len(shape))
    pair = pl.BlockSpec((1, terms, rows), lambda i, info: (i, 0, 0))
    return pl.pallas_call(
        finish_kernel,
        out_shape=(
            pack,
            pack,
            jax.ShapeDtypeStruct((width, rows), f32),
            jax.ShapeDtypeStruct((width, rows // 2), bf16),
        ),
        grid_spec=pltpu.PrefetchScalarGridSpec(
            num_scalar_prefetch=1,
            grid=(pairs,),
            in_specs=[
                pair,
                pair,
                whole((width, rows)),
                pl.BlockSpec((2, width, rows), lambda i, info: (i, 0, 0)),
                whole((width, rows)),
                whole((width, rows)),
                whole((width, rows)),
                whole((width, width)),
                whole((kv_width, width)),
                whole((kv_width, width)),
                whole((width, 2)),
                whole((width, 1)),
            ],
            out_specs=(
                whole(pack.shape),
                whole(pack.shape),
                whole((width, rows)),
                whole((width, rows // 2)),
            ),
            scratch_shapes=[
                pltpu.VMEM((terms, width), f32),
                pltpu.VMEM((1, width), f32),
                pltpu.VMEM((width, width), bf16),
            ],
        ),
        compiler_params=pltpu.CompilerParams(vmem_limit_bytes=VMEM),
        cost_estimate=pl.CostEstimate(
            flops=4 * pairs * rows * width * terms, bytes_accessed=8 * 1024 * 1024, transcendentals=0
        ),
        name="finish",
    )(info, even, odd, dq_t, a_all, a, x, middle_grad, query_t, key_t, value_t, gains, gain_second)


def last_kernel(count, *refs):
    own_ref = refs[0]
    got_refs = refs[1 : 1 + count]
    x_ref, chunk_ref, back_ref, key_ref, value_ref, gain_ref, out_ref = refs[1 + count :]
    total = own_ref[0].astype(f32)
    for got in got_refs:
        total = total + got[...].astype(f32)
    total = total.astype(bf16)
    size = total.shape[0] // (2 * KV_HEADS)
    keys = [total[2 * g * size : (2 * g + 1) * size] for g in range(KV_HEADS)]
    values = [total[(2 * g + 1) * size : (2 * g + 2) * size] for g in range(KV_HEADS)]
    weights = jnp.concatenate([key_ref[...], value_ref[...]], axis=0).astype(f32).T.astype(bf16)
    d_a = mm(weights, jnp.concatenate(keys + values, axis=0), 1, 0)
    back = column_norm_back(d_a, x_ref[...].astype(f32), gain_ref[:, 0:1])
    half = back_ref.shape[1]
    out_ref[:, :half] = chunk_ref[:, :half] + back[:, :half]
    out_ref[:, half:] = back_ref[...].astype(f32) + back[:, half:]


def last(pair, got, x_own, chunk_grad, back, key_t, value_t, gains):
    width, rows = x_own.shape
    whole = lambda shape: pl.BlockSpec(shape, lambda i: (0,) * len(shape))
    own = pl.BlockSpec((1,) + pair.shape[1:], lambda i: (0, 0, 0))
    return pl.pallas_call(
        functools.partial(last_kernel, len(got)),
        out_shape=jax.ShapeDtypeStruct((width, rows), f32),
        grid=(1,),
        in_specs=[own] + [whole(item.shape) for item in (*got, x_own, chunk_grad, back, key_t, value_t, gains)],
        out_specs=whole((width, rows)),
        compiler_params=pltpu.CompilerParams(vmem_limit_bytes=VMEM // 4 * 3),
        cost_estimate=pl.CostEstimate(
            flops=2 * rows * width * pair.shape[1], bytes_accessed=6 * 1024 * 1024, transcendentals=0
        ),
        name="last",
    )(pair, *got, x_own, chunk_grad, back, key_t, value_t, gains)


def add_kernel(info_ref, keep_ref, got_ref, output_ref, *out_refs):
    for mask, out_ref in enumerate(out_refs):

        @pl.when(pl.program_id(0) == mask)
        def _(mask=mask, out_ref=out_ref):
            matrix = info_ref[0] ^ mask

            @pl.when(matrix < 3)
            def _():
                out_ref[...] = (keep_ref[0].astype(f32) + got_ref[0].astype(f32)).astype(bf16)

            @pl.when(matrix >= 3)
            def _():
                out_ref[...] = output_ref[...]


def add_rotated(info, keep, got, output):
    _, width, units = keep.shape
    feed = pl.BlockSpec((1, width, units), lambda i, info: (jnp.minimum(info[0] ^ i, 2), 0, 0))
    whole = pl.BlockSpec((width, units), lambda i, info: (0, 0))
    return pl.pallas_call(
        add_kernel,
        out_shape=[jax.ShapeDtypeStruct((width, units), bf16)] * 4,
        grid_spec=pltpu.PrefetchScalarGridSpec(
            num_scalar_prefetch=1,
            grid=(4,),
            in_specs=[feed, feed, whole],
            out_specs=[whole] * 4,
        ),
        compiler_params=pltpu.CompilerParams(vmem_limit_bytes=VMEM // 4 * 3),
        name="add_rotated",
    )(info, keep, got, output)


def shard_pieces(piece):
    return [piece] + [swap(piece, "shard", mask) for mask in range(1, lax.axis_size("shard"))]


def in_order(pieces):
    me = lax.axis_index("shard")
    bit = 1
    while bit < len(pieces):
        odd = (me & bit) > 0
        pieces = [jnp.where(odd, pieces[j ^ bit], pieces[j]) for j in range(len(pieces))]
        bit *= 2
    return jnp.stack(pieces)


def scatter_shards(pieces):
    count = lax.axis_size("shard")
    me = lax.axis_index("shard")
    total = lax.dynamic_index_in_dim(pieces, me, 0, False).astype(f32)
    for mask in range(1, count):
        sent = lax.dynamic_index_in_dim(pieces, me ^ mask, 0, False).astype(bf16)
        total = total + swap(sent, "shard", mask).astype(f32)
    return total


def scatter_doubling(pieces):
    me = lax.axis_index("shard")
    mask = pieces.shape[0] // 2
    while mask:
        halves = pieces.reshape((2, mask) + pieces.shape[1:])
        upper = (me & mask) > 0
        sent = jnp.where(upper, halves[0], halves[1])
        kept = jnp.where(upper, halves[1], halves[0])
        total = kept.astype(f32) + swap(sent, "shard", mask).astype(f32)
        pieces = total.astype(bf16)
        mask //= 2
    return pieces[0]


def sum_context(value):
    total = value.astype(f32)
    low = value.astype(bf16)
    for mask in range(1, lax.axis_size("context")):
        total = total + swap(low, "context", mask).astype(f32)
    return total


def per_device(
    hidden_in,
    segment_ids,
    norm_gains,
    w_query,
    w_key,
    w_value,
    w_output,
    w_gate,
    w_up,
    w_down,
    cotangent,
):
    rows, width = hidden_in.shape[1], hidden_in.shape[2]
    half = rows // 2
    seg_row = segment_ids[0]
    length = seg_row.shape[0]
    shards = lax.axis_size("shard")
    contexts = lax.axis_size("context")
    blocks = lax.axis_size(SEQ)
    me = lax.axis_index(SEQ)
    core = lax.axis_index("tensor")
    context = lax.axis_index("context")
    part = w_query.shape[1]
    kv_part = w_key.shape[1]
    kv_width = kv_part * shards
    units = w_gate.shape[0]
    head_size = width // HEADS
    scale = head_size**-0.5

    starts = doc_starts(seg_row)
    place = (
        (jnp.arange(blocks, dtype=jnp.int32) ^ me)[:, None] * rows
        + jnp.arange(rows, dtype=jnp.int32)[None, :]
    ).reshape(1, -1)
    placed_starts = jnp.max(jnp.where(place >= starts[:, None], starts[:, None], 0), axis=0)
    positions = (place[0] - placed_starts).astype(f32)
    frequency = rope_base ** (-jnp.arange(head_size // 2, dtype=f32) * 2.0 / head_size)
    angles = frequency[:, None] * positions[None, :]
    cosine, sine = jnp.cos(angles), jnp.sin(angles)
    info = jnp.concatenate([jnp.reshape(me, (1,)).astype(jnp.int32), starts])

    x_own = hidden_in[0].T
    by_context = contexts == 4 and part % 16 == 0

    gain_rows = part - 2 * kv_part
    key_values = jnp.concatenate(
        [w_key.T, w_value.T, jnp.pad(norm_gains, ((0, gain_rows - 2), (0, width - part)))], axis=0
    )
    pack = jnp.where(core == 0, w_query.T, key_values)
    pack_mine = shard_pieces(pack)
    later = jnp.stack([w_gate.T, w_up.T, w_down.T, jnp.pad(w_output.T, ((0, 0), (0, units - width)))])
    if by_context:
        x_one, x_two = swap(x_own, "context", 1), swap(x_own, "context", 2)
        later_c = lax.dynamic_index_in_dim(later, context, 0, False)
        x_one, x_two, pack_mine, later_c, cosine, sine = lax.optimization_barrier(
            (x_one, x_two, pack_mine, later_c, cosine, sine)
        )
        x_three = [swap(x_two[:, :half], "context", 1), swap(x_one[:, half:], "context", 2)]
        fetched = shard_pieces(later_c)[1:]
        x_far = swap(jnp.stack([x_own, x_one, x_two]), "tensor", 1)
        x_three = jnp.concatenate(x_three, axis=1)
        x_last = swap(x_three, "tensor", 1)
        x_arrays = [x_own[None], x_one[None], x_two[None], x_three[None], x_far, x_last[None]]
        layout = ((0, 0), (4, 0), (1, 0), (4, 1), (2, 0), (4, 2), (3, 0), (5, 0))
    else:
        near = [x_own] + [swap(x_own, "context", mask) for mask in range(1, contexts)]
        x_arrays = [item[None] for item in near] + [swap(jnp.stack(near), "tensor", 1)]
        layout = tuple((c if r == 0 else contexts, 0 if r == 0 else c) for c in range(contexts) for r in (0, 1))
        later_pieces = shard_pieces(later)
    pack_mine = jnp.stack(pack_mine)
    pack_theirs = swap(pack_mine, "tensor", 1)
    shard = lax.axis_index("shard")
    places = jnp.stack([shard, core, context]).astype(jnp.int32)
    query_t, key_t, value_t, gain_parts = unpack(places, [pack_mine], [pack_theirs], kv_part)
    query_t = query_t.reshape(width, width)
    key_t = key_t.reshape(kv_width, width)
    value_t = value_t.reshape(kv_width, width)
    gains = gain_parts[:, :2, :part].transpose(0, 2, 1).reshape(width, 2).astype(f32)

    def chunks(array, axis):
        return jnp.concatenate(
            [
                lax.slice_in_dim(array, 0, half, axis=axis),
                lax.slice_in_dim(array, length - half, length, axis=axis),
            ],
            axis=axis,
        )

    a_all, keys, keys_t, values, values_t, queries_t, a, x = project(
        x_arrays, layout, query_t, key_t, value_t, gains, cosine, sine, scale
    )
    cos_q, sin_q = chunks(cosine, 1), chunks(sine, 1)

    cot_own = cotangent[0].T
    if by_context:
        queries_t, cot_own, fetched = lax.optimization_barrier((queries_t, cot_own, fetched))
        fetched = jnp.stack(fetched)
        fetched = [fetched] + [swap(fetched, "context", mask) for mask in range(1, 4)]
    cot_got = lax.ppermute(cot_own[:, half:], SEQ, flip(blocks, blocks - 1))
    cot = jnp.concatenate([cot_own[:, :half], cot_got], axis=1)
    attended = attend(0, 2, (), info, queries_t, keys, values_t, rows)

    if by_context:
        attended, fetched, cot, later = lax.optimization_barrier((attended, fetched, cot, later))
        mine_all = [later] + fetched
    else:
        later_pieces = in_order(later_pieces).transpose(1, 0, 2, 3).reshape(4, width, units)
        attended, later_pieces = lax.optimization_barrier((attended, later_pieces))
        mine_all = [later_pieces]
    theirs_all = [swap(item, "tensor", 1) for item in mine_all]
    mixed_t, log_total = attend(2, 1, attended, info, queries_t, keys, values_t, rows)
    middle, second, cot_rows, second_t, layer_sum, d_second, grads_theirs, output_t = feed_first(
        places, x, mixed_t, cot, gains, theirs_all
    )
    ff_got = swap(grads_theirs, "tensor", 1)
    layer_chunks, middle_grad, mixed_grad_t, delta, gain_grad_second, output_sum, grads_mine = (
        feed_second(
            places, middle, mixed_t, cot, second, cot_rows, second_t, layer_sum, d_second, gains,
            output_t, mine_all,
        )
    )
    layer_got = lax.ppermute(layer_chunks[:, half:], SEQ, flip(blocks, blocks - 1))

    wide = units

    def back(group, earlier, info):
        return attend_back(
            group, earlier, info, queries_t, mixed_grad_t, keys, keys_t, values, log_total, delta,
            cosine, sine, cos_q, sin_q, rows, scale,
        )

    if contexts == 4:
        both = add_rotated(places[2:], grads_mine, ff_got, output_sum)
        info, both = lax.optimization_barrier((info, both))
        got = [swap(item, "context", mask) for mask, item in enumerate(both) if mask]
        terms = back(0, (), info)
        terms, layer_got = lax.optimization_barrier((terms, layer_got))
        terms = back(1, terms, info)
        terms, got = lax.optimization_barrier((terms, got))
        owned = both[0].astype(f32)
        for item in got:
            owned = owned + item.astype(f32)
        owned = owned.reshape(shards, part, wide)
        kept = lax.dynamic_index_in_dim(owned, shard, 0, False)
        sent = [
            lax.dynamic_index_in_dim(owned, shard ^ mask, 0, False).astype(bf16)
            for mask in range(1, shards)
        ]
        terms, kept, sent = lax.optimization_barrier((terms, kept, sent))
        got = [swap(item, "shard", mask + 1) for mask, item in enumerate(sent)]
        terms = back(2, terms, info)
        terms, got = lax.optimization_barrier((terms, got))
        for item in got:
            kept = kept + item.astype(f32)
        owned_low = kept.astype(bf16)
        spread = [owned_low] + [swap(owned_low, "context", mask) for mask in range(1, 4)]
    else:
        both = add_rotated(places[2:] * 0, grads_mine, ff_got, output_sum)
        terms = back(0, (), info)
        terms = back(1, terms, info)
        terms = back(2, terms, info)
    dq_t, even, odd = terms
    odd_got = swap(odd, "tensor", 1)
    layer_value = jnp.concatenate([layer_chunks[:, :half], layer_got], axis=1).T
    finished = finish(
        places, even, odd, dq_t, a_all, a, x, middle_grad, query_t, key_t, value_t, gains,
        gain_grad_second, shards,
    )
    if contexts == 4:
        odd_got, spread, finished = lax.optimization_barrier((odd_got, spread, finished))
        for bit in (1, 2):
            away = (context & bit) > 0
            spread = [jnp.where(away, spread[j ^ bit], spread[j]) for j in range(4)]
        final = spread
    else:
        large = jnp.stack(both).reshape(4, shards, part, wide).transpose(1, 0, 2, 3)
        final = lax.psum(scatter_shards(large).astype(bf16), "context")
    keep, give, chunk_grad, chunk_send = finished
    pair = (even.astype(f32) + odd_got.astype(f32)).astype(bf16)

    grad_gate, grad_up, grad_down = [final[matrix].astype(f32).T for matrix in range(3)]
    output_low = final[3][:, :width]
    grad_output = (output_low.astype(f32) + swap(output_low, "tensor", 1).astype(f32)).T

    both = (keep.astype(f32) + swap(give, "tensor", 1).astype(f32)).astype(bf16)
    pairs = [pair[mask] for mask in range(1, contexts)]
    both, pairs, chunk_send = lax.optimization_barrier((both, pairs, chunk_send))
    pair_got = [swap(item, "context", mask + 1) for mask, item in enumerate(pairs)]
    returned = lax.ppermute(chunk_send, SEQ, flip(blocks, blocks - 1))
    small = scatter_doubling(both)
    small, pair_got, returned = lax.optimization_barrier((small, pair_got, returned))
    small = sum_context(small).astype(bf16)
    small_other = swap(small, "tensor", 1)
    grad_query = jnp.where(core == 0, small, small_other).astype(f32).T
    small = jnp.where(core == 0, small_other, small).astype(f32)
    grad_key = small[:kv_part].T
    grad_value = small[kv_part : 2 * kv_part].T
    gain_grads = small[2 * kv_part : 2 * kv_part + 2]
    grad_gains = lax.dynamic_slice_in_dim(gain_grads, shard * part, part, 1)

    grad_hidden = last(pair, pair_got, x_own, chunk_grad, returned, key_t, value_t, gains).T
    return (
        layer_value[None],
        grad_hidden[None],
        grad_gains,
        grad_query,
        grad_key,
        grad_value,
        grad_output,
        grad_gate,
        grad_up,
        grad_down,
    )


def solution(mesh):
    return jax.shard_map(
        per_device,
        mesh=mesh,
        in_specs=(
            P("shard", ("context", "tensor"), None),
            P("shard", None),
            P(None, "shard"),
            P(None, "shard"),
            P(None, "shard"),
            P(None, "shard"),
            P(None, "shard"),
            P("tensor", "shard"),
            P("tensor", "shard"),
            P("tensor", "shard"),
            P("shard", ("context", "tensor"), None),
        ),
        out_specs=(
            P("shard", ("context", "tensor"), None),
            P("shard", ("context", "tensor"), None),
            P(None, "shard"),
            P(None, "shard"),
            P(None, "shard"),
            P(None, "shard"),
            P(None, "shard"),
            P("tensor", "shard"),
            P("tensor", "shard"),
            P("tensor", "shard"),
        ),
        check_vma=False,
    )
```

```python
import functools

import jax
import jax.numpy as jnp
from jax import lax
from jax.experimental import pallas as pl
from jax.experimental.pallas import tpu as pltpu
from jax.sharding import PartitionSpec as P

HEADS = 9
KV_HEADS = 3
DOCS = 4
GROUP = HEADS // KV_HEADS

rope_base = 100000.0
norm_eps = 1e-05
masked_score = -1e30

VMEM = 60 * 1024 * 1024
f32 = jnp.float32
bf16 = jnp.bfloat16
SEQ = ("context", "tensor")


def mm(left, right, left_dim, right_dim):
    return lax.dot_general(
        left, right, (((left_dim,), (right_dim,)), ((), ())), preferred_element_type=f32
    )


def flip(count, mask):
    return [(i, i ^ mask) for i in range(count)]


def swap(value, axis, mask):
    return lax.ppermute(value, axis, flip(lax.axis_size(axis), mask))


def doc_starts(seg_row):
    one_hot = (seg_row[None, :] == jnp.arange(DOCS, dtype=jnp.int32)[:, None]).astype(jnp.int32)
    doc_counts = jnp.sum(one_hot, axis=1)
    return jnp.cumsum(doc_counts) - doc_counts


def column_rms(hidden):
    return lax.rsqrt(jnp.mean(hidden * hidden, axis=0, keepdims=True) + norm_eps)


def column_norm_back(grad, hidden, gain):
    inverse = column_rms(hidden)
    unit = hidden * inverse
    scaled = grad * gain
    return (scaled - unit * jnp.mean(scaled * unit, axis=0, keepdims=True)) * inverse


def turn_head(head, cosine, sine, sign):
    half = cosine.shape[0]
    first, second = head[:half], head[half:]
    return jnp.concatenate(
        [first * cosine - sign * (second * sine), second * cosine + sign * (first * sine)], axis=0
    )


def doc_start(info_ref, index):
    start = jnp.int32(0)
    for doc in range(1, DOCS):
        start = jnp.where(index >= info_ref[1 + doc], info_ref[1 + doc], start)
    return start


def chunk_start(info_ref, chunk, blocks, size):
    me = info_ref[0]
    return jnp.where(chunk == 0, me * 2 * size, (blocks - 1 - me) * 2 * size + size)


def key_ranges(info_ref, chunk, blocks, key_block):
    size = key_block // 2
    first = chunk_start(info_ref, chunk, blocks, size)
    low = doc_start(info_ref, first) // key_block
    high = (first + size + key_block - 1) // key_block
    full_from = (doc_start(info_ref, first + size - 1) + key_block - 1) // key_block
    full_from = jnp.minimum(jnp.maximum(full_from, low), high)
    full_to = jnp.minimum(jnp.maximum(first // key_block, full_from), high)
    return low, full_from, full_to, high


def allowed_mask(info_ref, block, key_block, chunk, blocks):
    size = key_block // 2
    first = chunk_start(info_ref, chunk, blocks, size)
    index = first + lax.broadcasted_iota(jnp.int32, (1, size), 1)
    start = doc_start(info_ref, index)
    key_index = block * key_block + lax.broadcasted_iota(jnp.int32, (key_block, size), 0)
    return (key_index >= start) & (key_index <= index)


def side_by_side(ref, size):
    return jnp.concatenate([ref[m * size : (m + 1) * size, :] for m in range(GROUP)], axis=1)


def forward_kernel(key_block, group, info_ref, *refs):
    if group:
        refs = refs[2:]
    q_ref, k_ref, vt_ref, o_ref, lse_ref, m_ref, l_ref, acc_ref, q_side = refs
    chunk = pl.program_id(1)
    me = info_ref[0]
    size = k_ref.shape[2]
    tokens = q_ref.shape[1]
    blocks = k_ref.shape[1] // key_block
    m_ref[...] = jnp.full_like(m_ref, masked_score)
    acc_ref[...] = jnp.zeros_like(acc_ref)
    q_side[...] = side_by_side(q_ref, size)

    def block_scores(block, masked):
        place = pl.multiple_of((block ^ me) * key_block, key_block)
        scores = mm(k_ref[0, pl.ds(place, key_block), :], q_side[...], 1, 0)
        if masked:
            mask = allowed_mask(info_ref, block, key_block, chunk, blocks)
            scores = jnp.concatenate(
                [
                    jnp.where(mask, scores[:, m * tokens : (m + 1) * tokens], masked_score)
                    for m in range(GROUP)
                ],
                axis=1,
            )
        return scores

    def step(first, count, masked):
        scores = [block_scores(first + i, masked) for i in range(count)]
        old = m_ref[...]
        new = old
        for item in scores:
            new = jnp.maximum(new, jnp.max(item, axis=0, keepdims=True))
        m_ref[...] = new
        total = acc_ref[...] * jnp.exp(old - new)
        for i, item in enumerate(scores):
            place = pl.multiple_of(((first + i) ^ me) * key_block, key_block)
            weights = jnp.exp(item - new).astype(bf16)
            values = jnp.concatenate(
                [vt_ref[:, pl.ds(place, key_block)], jnp.ones((16, key_block), bf16)], axis=0
            )
            total = total + mm(values, weights, 1, 0)
        acc_ref[...] = total

    low, full_from, full_to, high = key_ranges(info_ref, chunk, blocks, key_block)
    pairs = (full_to - full_from) // 2
    pl.loop(low, full_from)(lambda b: step(b, 1, True))
    pl.loop(0, pairs)(lambda b: step(full_from + 2 * b, 2, False))
    pl.loop(full_from + 2 * pairs, full_to)(lambda b: step(b, 1, False))
    pl.loop(full_to, high)(lambda b: step(b, 1, True))
    for member in range(GROUP):
        rows = slice(member * size, (member + 1) * size)
        lanes = slice(member * tokens, (member + 1) * tokens)
        total = acc_ref[size : size + 1, lanes]
        o_ref[rows, :] = acc_ref[:size, lanes] / total
        lse_ref[0, member : member + 1, :] = m_ref[:, lanes] + jnp.log(total)


def backward_kernel(key_block, scale, group, *refs):
    if group:
        refs = refs[:1] + refs[4:]
    (
        info_ref, q_ref, do_ref, k_ref, kt_ref, v_ref, lse_ref, delta_ref,
        cos_ref, sin_ref, cosq_ref, sinq_ref,
        dq_ref, even_ref, odd_ref, dk_ref, dv_ref, dq_sum, q_side, do_side,
    ) = refs
    chunk = pl.program_id(0)
    me = info_ref[0]
    size = k_ref.shape[2]
    blocks = dk_ref.shape[0]
    tokens = q_ref.shape[1]
    dq_sum[...] = jnp.zeros_like(dq_sum)
    q_side[...] = side_by_side(q_ref, size)
    do_side[...] = side_by_side(do_ref, size)
    log_total = jnp.concatenate([lse_ref[0, m : m + 1, :] for m in range(GROUP)], axis=1)
    delta = jnp.concatenate([delta_ref[0, m : m + 1, :] for m in range(GROUP)], axis=1)

    @pl.when(chunk == 0)
    def _():
        dk_ref[...] = jnp.zeros_like(dk_ref)
        dv_ref[...] = jnp.zeros_like(dv_ref)

    def step(block, masked):
        spot = block ^ me
        place = pl.multiple_of(spot * key_block, key_block)
        keys = k_ref[0, pl.ds(place, key_block), :]
        values = v_ref[0, pl.ds(place, key_block), :]
        keys_t = kt_ref[:, pl.ds(place, key_block)]
        scores = mm(keys, q_side[...], 1, 0)
        if masked:
            mask = allowed_mask(info_ref, block, key_block, chunk, blocks)
            scores = jnp.concatenate(
                [
                    jnp.where(mask, scores[:, m * tokens : (m + 1) * tokens], masked_score)
                    for m in range(GROUP)
                ],
                axis=1,
            )
        probs = jnp.exp(scores - log_total)
        prob_grad = mm(values, do_side[...], 1, 0)
        raw = (probs * (prob_grad - delta)).astype(bf16)
        dv = mm(do_side[...], probs.astype(bf16), 1, 1)
        dk = mm(q_side[...], raw, 1, 1)
        dq_sum[...] += mm(keys_t, raw, 1, 0)
        dk_ref[spot] += dk
        dv_ref[spot] += dv

    low, full_from, full_to, high = key_ranges(info_ref, chunk, blocks, key_block)
    pl.loop(low, full_from)(lambda b: step(b, True))
    pl.loop(full_from, full_to)(lambda b: step(b, False))
    pl.loop(full_to, high)(lambda b: step(b, True))
    for member in range(GROUP):
        rows = slice(member * size, (member + 1) * size)
        dq_ref[rows, :] = turn_head(
            dq_sum[:, member * tokens : (member + 1) * tokens] * scale, cosq_ref[...], sinq_ref[...], -1.0).astype(
            bf16
        )

    @pl.when(chunk == 1)
    def _():
        for block in range(blocks):
            columns = slice(block * key_block, (block + 1) * key_block)
            out_ref = odd_ref if block % 2 else even_ref
            out_ref[block // 2, :size, :] = turn_head(
                dk_ref[block], cos_ref[:, columns], sin_ref[:, columns], -1.0
            ).astype(bf16)
            out_ref[block // 2, size:, :] = dv_ref[block].astype(bf16)


def attend(group, groups, earlier, info, queries_t, keys, values_t, key_block):
    length, size = keys.shape[1], keys.shape[2]
    tokens = queries_t.shape[1]
    chunk = tokens // 2
    wide = GROUP * size
    head_block = pl.BlockSpec((wide, chunk), lambda g, c, info: (group + g, c))
    stat_block = pl.BlockSpec((1, GROUP, chunk), lambda g, c, info: (group + g, 0, c))
    elements = groups * GROUP * tokens * length // 2
    return pl.pallas_call(
        functools.partial(forward_kernel, key_block, group),
        out_shape=(
            jax.ShapeDtypeStruct((HEADS * size, tokens), f32),
            jax.ShapeDtypeStruct((KV_HEADS, GROUP, tokens), f32),
        ),
        grid_spec=pltpu.PrefetchScalarGridSpec(
            num_scalar_prefetch=1,
            grid=(groups, 2),
            in_specs=[pl.BlockSpec(memory_space=pl.ANY)] * len(earlier)
            + [
                head_block,
                pl.BlockSpec((1, length, size), lambda g, c, info: (group + g, 0, 0)),
                pl.BlockSpec((size, length), lambda g, c, info: (group + g, 0)),
            ],
            out_specs=(head_block, stat_block),
            scratch_shapes=[
                pltpu.VMEM((1, GROUP * chunk), f32),
                pltpu.VMEM((1, GROUP * chunk), f32),
                pltpu.VMEM((size + 16, GROUP * chunk), f32),
                pltpu.VMEM((size, GROUP * chunk), bf16),
            ],
        ),
        input_output_aliases={1 + number: number for number in range(len(earlier))},
        compiler_params=pltpu.CompilerParams(vmem_limit_bytes=VMEM),
        cost_estimate=pl.CostEstimate(
            flops=16 * elements * size, bytes_accessed=4 * 1024 * 1024, transcendentals=elements
        ),
        name="attend",
    )(info, *earlier, queries_t, keys, values_t)


def attend_back(
    group, earlier, info, queries_t, grads_t, keys, keys_t, values, log_total, delta,
    cosine, sine, cos_q, sin_q, key_block, scale,
):
    length, size = keys.shape[1], keys.shape[2]
    tokens = queries_t.shape[1]
    chunk = tokens // 2
    wide = GROUP * size
    blocks = length // key_block
    head_block = pl.BlockSpec((wide, chunk), lambda c, info: (group, c))
    stat_block = pl.BlockSpec((1, GROUP, chunk), lambda c, info: (group, 0, c))
    token_block = pl.BlockSpec((1, length, size), lambda c, info: (group, 0, 0))
    feature_block = pl.BlockSpec((size, length), lambda c, info: (group, 0))
    table = pl.BlockSpec((size // 2, length), lambda c, info: (0, 0))
    table_q = pl.BlockSpec((size // 2, chunk), lambda c, info: (0, c))
    terms = pl.BlockSpec((blocks // 2, 2 * size, key_block), lambda c, info: (0, group, 0))
    elements = GROUP * tokens * length // 2
    terms_shape = jax.ShapeDtypeStruct((blocks // 2, KV_HEADS * 2 * size, key_block), bf16)
    return pl.pallas_call(
        functools.partial(backward_kernel, key_block, scale, group),
        out_shape=(jax.ShapeDtypeStruct((HEADS * size, tokens), bf16), terms_shape, terms_shape),
        grid_spec=pltpu.PrefetchScalarGridSpec(
            num_scalar_prefetch=1,
            grid=(2,),
            in_specs=[pl.BlockSpec(memory_space=pl.ANY)] * len(earlier)
            + [
                head_block, head_block, token_block, feature_block, token_block, stat_block, stat_block,
                table, table, table_q, table_q,
            ],
            out_specs=(head_block, terms, terms),
            scratch_shapes=[
                pltpu.VMEM((blocks, size, key_block), f32),
                pltpu.VMEM((blocks, size, key_block), f32),
                pltpu.VMEM((size, GROUP * chunk), f32),
                pltpu.VMEM((size, GROUP * chunk), bf16),
                pltpu.VMEM((size, GROUP * chunk), bf16),
            ],
        ),
        input_output_aliases={1 + number: number for number in range(len(earlier))},
        compiler_params=pltpu.CompilerParams(vmem_limit_bytes=VMEM),
        cost_estimate=pl.CostEstimate(
            flops=40 * elements * size, bytes_accessed=4 * 1024 * 1024, transcendentals=elements
        ),
        name="attend_back",
    )(
        info, *earlier, queries_t, grads_t, keys, keys_t, values, log_total, delta,
        cosine, sine, cos_q, sin_q,
    )


def unpack_kernel(count, kv_part, info_ref, *refs):
    mine, theirs = refs[:count], refs[count : 2 * count]
    query_ref, key_ref, value_ref, gain_ref = refs[2 * count :]
    first = info_ref[1] == 0
    mask = 0
    for number in range(count):
        for row in range(mine[number].shape[0]):
            spot = info_ref[0] ^ mask
            left, right = mine[number][row], theirs[number][row]
            query_ref[spot] = jnp.where(first, left, right)
            other = jnp.where(first, right, left)
            key_ref[spot] = other[:kv_part]
            value_ref[spot] = other[kv_part : 2 * kv_part]
            gain_ref[spot] = other[2 * kv_part :]
            mask += 1


def unpack(info, mine, theirs, kv_part):
    count = len(mine)
    total = sum(item.shape[0] for item in mine)
    part, width = mine[0].shape[1:]
    whole = lambda shape: pl.BlockSpec(shape, lambda i, info: (0,) * len(shape))
    shapes = [(total, size, width) for size in (part, kv_part, kv_part, part - 2 * kv_part)]
    return pl.pallas_call(
        functools.partial(unpack_kernel, count, kv_part),
        out_shape=[jax.ShapeDtypeStruct(shape, bf16) for shape in shapes],
        grid_spec=pltpu.PrefetchScalarGridSpec(
            num_scalar_prefetch=1,
            grid=(1,),
            in_specs=[whole(item.shape) for item in (*mine, *theirs)],
            out_specs=[whole(shape) for shape in shapes],
        ),
        name="unpack",
    )(info, *mine, *theirs)


def project_kernel(layout, arrays, scale, *refs):
    pieces = len(layout)
    x_refs = [refs[array].at[row] for array, row in layout]
    query_ref, key_ref, value_ref, gain_ref, cos_ref, sin_ref = refs[arrays : arrays + 6]
    a_ref, k_ref, kt_ref, v_ref, vt_ref, q_ref, aq_ref, xq_ref = refs[arrays + 6 : arrays + 14]
    held, sems, cos_q, sin_q = refs[arrays + 14 :]
    step = pl.program_id(0)
    tokens = xq_ref.shape[1]
    chunk = tokens // 2

    @pl.when(step == 0)
    def _():
        for number in range(pieces):
            pltpu.make_async_copy(x_refs[number], held.at[number], sems.at[number]).start()

    for number in range(pieces):

        @pl.when(step == number)
        def _(number=number):
            pltpu.make_async_copy(x_refs[number], held.at[number], sems.at[number]).wait()

    x_low = held[step]
    x = x_low.astype(f32)
    a = (x * column_rms(x) * gain_ref[:, 0:1]).astype(bf16)
    a_ref[0] = a
    cosine, sine = cos_ref[...], sin_ref[...]
    k_lin = mm(key_ref[...], a, 1, 0)
    v_lin = mm(value_ref[...], a, 1, 0)
    vt_ref[...] = v_lin.astype(bf16)
    size = k_ref.shape[2]
    for group in range(KV_HEADS):
        rows = slice(group * size, (group + 1) * size)
        turned = turn_head(k_lin[rows], cosine, sine, 1.0)
        kt_ref[rows, :] = turned.astype(bf16)
        k_ref[group] = turned.T.astype(bf16)
        v_ref[group] = v_lin[rows].T.astype(bf16)

    @pl.when(step == 0)
    def _():
        aq_ref[:, :chunk] = a[:, :chunk]
        xq_ref[:, :chunk] = x_low[:, :chunk]
        cos_q[:, :chunk] = cosine[:, :chunk]
        sin_q[:, :chunk] = sine[:, :chunk]

    @pl.when(step == pieces - 1)
    def _():
        aq_ref[:, chunk:] = a[:, chunk:]
        xq_ref[:, chunk:] = x_low[:, chunk:]
        cos_q[:, chunk:] = cosine[:, chunk:]
        sin_q[:, chunk:] = sine[:, chunk:]
        q_lin = mm(query_ref[...], aq_ref[...], 1, 0)
        for head in range(HEADS):
            rows = slice(head * size, (head + 1) * size)
            q_ref[rows, :] = (
                turn_head(q_lin[rows], cos_q[...], sin_q[...], 1.0).astype(bf16) * scale
            ).astype(bf16)


def project(x_arrays, layout, query_t, key_t, value_t, gains, cosine, sine, scale):
    pieces = len(layout)
    arrays = len(x_arrays)
    width, rows = x_arrays[0].shape[1:]
    kv_width = key_t.shape[0]
    size = kv_width // KV_HEADS
    length = pieces * rows
    whole = lambda array: pl.BlockSpec(array.shape, lambda i: (0,) * array.ndim)
    table = pl.BlockSpec((size // 2, rows), lambda i: (0, i))
    by_token = pl.BlockSpec((KV_HEADS, rows, size), lambda i: (0, i, 0))
    by_feature = pl.BlockSpec((kv_width, rows), lambda i: (0, i))
    own = pl.BlockSpec((width, rows), lambda i: (0, 0))
    own_shape = jax.ShapeDtypeStruct((width, rows), bf16)
    return pl.pallas_call(
        functools.partial(project_kernel, layout, arrays, scale),
        out_shape=(
            jax.ShapeDtypeStruct((pieces, width, rows), bf16),
            jax.ShapeDtypeStruct((KV_HEADS, length, size), bf16),
            jax.ShapeDtypeStruct((kv_width, length), bf16),
            jax.ShapeDtypeStruct((KV_HEADS, length, size), bf16),
            jax.ShapeDtypeStruct((kv_width, length), bf16),
            own_shape,
            own_shape,
            own_shape,
        ),
        grid=(pieces,),
        in_specs=[pl.BlockSpec(memory_space=pl.ANY)] * arrays
        + [whole(query_t), whole(key_t), whole(value_t), whole(gains), table, table],
        out_specs=(
            pl.BlockSpec((1, width, rows), lambda i: (i, 0, 0)),
            by_token,
            by_feature,
            by_token,
            by_feature,
            own,
            own,
            own,
        ),
        scratch_shapes=[
            pltpu.VMEM((pieces, width, rows), bf16),
            pltpu.SemaphoreType.DMA((pieces,)),
            pltpu.VMEM((size // 2, rows), f32),
            pltpu.VMEM((size // 2, rows), f32),
        ],
        compiler_params=pltpu.CompilerParams(vmem_limit_bytes=VMEM),
        cost_estimate=pl.CostEstimate(
            flops=8 * length * width * kv_width, bytes_accessed=8 * length * width, transcendentals=0
        ),
        name="project",
    )(*x_arrays, query_t, key_t, value_t, gains, cosine, sine)


def feed_tile(second, second_t, cot, cot_t, weights, grad_ref, sum_ref, db_ref):
    gate_t, up_t, down_t = weights
    gate = mm(second, gate_t, 1, 0)
    upward = mm(second, up_t, 1, 0)
    d_hidden = mm(cot, down_t, 1, 0)
    sig = 1.0 / (1.0 + jnp.exp(-gate))
    silu = gate * sig
    hidden = (silu * upward).astype(bf16)
    d_gate = (d_hidden * upward * sig * (1.0 + gate * (1.0 - sig))).astype(bf16)
    d_up = (d_hidden * silu).astype(bf16)
    sum_ref[...] += mm(down_t, hidden, 1, 1)
    db_ref[...] += mm(gate_t, d_gate, 1, 1) + mm(up_t, d_up, 1, 1)
    grad_ref[0] = mm(second_t, d_gate, 1, 0).astype(bf16)
    grad_ref[1] = mm(second_t, d_up, 1, 0).astype(bf16)
    grad_ref[2] = mm(cot_t, hidden, 1, 0).astype(bf16)


def hold_weights(info_ref, own_ref, other_refs, held):
    shard, context = info_ref[0], info_ref[2]
    for matrix in range(held.shape[0]):
        held[matrix, shard if held.shape[1] > 1 else 0] = own_ref[matrix]
    for number, other in enumerate(other_refs):
        for mask in range(1, held.shape[1]):
            held[context ^ number, shard ^ mask] = other[mask - 1]


def held_tiles(held, tile):
    lanes = pl.ds(pl.multiple_of(pl.program_id(0) * tile, tile), tile)
    return [
        held[matrix, :, :, lanes].reshape(held.shape[1] * held.shape[2], tile) for matrix in range(3)
    ]


def feed_first_kernel(count, info_ref, *refs):
    x_ref, o_ref, cot_ref, gain_ref = refs[count : count + 4]
    h_ref, second_ref, cot_rows, second_t, sum_ref, db_ref, grad_ref, output_ref = refs[
        count + 4 : count + 12
    ]
    held = refs[count + 12]
    width = x_ref.shape[0]

    @pl.when(pl.program_id(0) == 0)
    def _():
        hold_weights(info_ref, refs[0], refs[1:count], held)
        output_t = held[3].reshape(width, held.shape[3])[:, :width]
        output_ref[...] = output_t
        middle = x_ref[...].astype(f32) + mm(output_t, o_ref[...].astype(bf16), 1, 0)
        second = middle * column_rms(middle) * gain_ref[:, 1:2]
        h_ref[...] = middle
        second_t[...] = second.astype(bf16)
        second_ref[...] = second.T.astype(bf16)
        cot_rows[...] = cot_ref[...].astype(f32).T.astype(bf16)
        sum_ref[...] = middle
        db_ref[...] = jnp.zeros_like(db_ref)

    weights = held_tiles(held, grad_ref.shape[2])
    feed_tile(
        second_ref[...], second_t[...], cot_rows[...], cot_ref[...], weights, grad_ref, sum_ref, db_ref
    )


def feed_second_kernel(count, info_ref, *refs):
    (
        h_ref, o_ref, cot_ref, second_ref, cot_rows, second_t, sum_in_ref, db_in_ref, gain_ref, wo_ref,
    ) = refs[count : count + 10]
    layer_ref, send_ref, mg_ref, do_ref, delta_ref, gg_ref, go_ref, grad_ref = refs[
        count + 10 : count + 18
    ]
    sum_ref, db_ref, held = refs[count + 18 :]
    width = h_ref.shape[0]
    step = pl.program_id(0)

    @pl.when(step == 0)
    def _():
        hold_weights(info_ref, refs[0], refs[1:count], held)
        sum_ref[...] = sum_in_ref[...]
        db_ref[...] = db_in_ref[...]

    weights = held_tiles(held, grad_ref.shape[2])
    feed_tile(
        second_ref[...], second_t[...], cot_rows[...], cot_ref[...], weights, grad_ref, sum_ref, db_ref
    )

    @pl.when(step == pl.num_programs(0) - 1)
    def _():
        chunk = layer_ref.shape[1]
        layer_ref[...] = sum_ref[:, :chunk].astype(bf16)
        send_ref[...] = sum_ref[:, chunk:].astype(bf16)
        middle = h_ref[...]
        inverse = column_rms(middle)
        unit = middle * inverse
        grad = db_ref[...]
        gg_ref[...] = jnp.sum(grad * unit, axis=1, keepdims=True)
        scaled = grad * gain_ref[:, 1:2]
        back = (scaled - unit * jnp.mean(scaled * unit, axis=0, keepdims=True)) * inverse
        middle_grad = cot_ref[...].astype(f32) + back
        mg_ref[...] = middle_grad
        low = middle_grad.astype(bf16)
        d_o = mm(wo_ref[...].astype(f32).T.astype(bf16), low, 1, 0).astype(bf16)
        do_ref[...] = d_o
        mixed = o_ref[...]
        product = d_o.astype(f32) * mixed
        size = width // HEADS
        for head in range(HEADS):
            delta_ref[head // GROUP, head % GROUP : head % GROUP + 1, :] = jnp.sum(
                product[head * size : (head + 1) * size, :], axis=0, keepdims=True
            )
        go_ref[...] = jnp.zeros_like(go_ref)
        go_ref[:, :width] = mm(low, mixed.astype(bf16), 1, 1).astype(bf16)


def feed_specs(pieces, rows, width):
    part, units = pieces[0].shape[1:]
    tile = units
    whole = lambda shape: pl.BlockSpec(shape, lambda i, info: (0,) * len(shape))
    tokens = whole((rows, width))
    features = whole((width, rows))
    gains = whole((width, 2))
    weights = [whole(item.shape) for item in pieces]
    grads = pl.BlockSpec((3, width, tile), lambda i, info: (0, 0, i))
    held = pltpu.VMEM((4, width // part, part, units), bf16)
    return units // tile, whole, tokens, features, gains, weights, grads, held


def feed_first(info, x, mixed_t, cot, gains, pieces):
    width, rows = x.shape
    units = pieces[0].shape[2]
    count = len(pieces)
    steps, whole, tokens, features, gain_spec, weights, grads, held = feed_specs(pieces, rows, width)
    wide = jax.ShapeDtypeStruct((width, rows), f32)
    flat = jax.ShapeDtypeStruct((rows, width), bf16)
    return pl.pallas_call(
        functools.partial(feed_first_kernel, count),
        out_shape=(
            wide,
            flat,
            flat,
            jax.ShapeDtypeStruct((width, rows), bf16),
            wide,
            wide,
            jax.ShapeDtypeStruct((3, width, units), bf16),
            jax.ShapeDtypeStruct((width, width), bf16),
        ),
        grid_spec=pltpu.PrefetchScalarGridSpec(
            num_scalar_prefetch=1,
            grid=(steps,),
            in_specs=weights + [features, features, features, gain_spec],
            out_specs=(
                features, tokens, tokens, features, features, features, grads, whole((width, width)),
            ),
            scratch_shapes=[held],
        ),
        compiler_params=pltpu.CompilerParams(vmem_limit_bytes=VMEM),
        cost_estimate=pl.CostEstimate(
            flops=20 * rows * width * units, bytes_accessed=12 * units * width, transcendentals=0
        ),
        name="feed_first",
    )(info, *pieces, x, mixed_t, cot, gains)


def feed_second(
    info, middle, mixed_t, cot, second, cot_rows, second_t, layer_sum, d_second, gains, output_t, pieces
):
    width, rows = middle.shape
    units = pieces[0].shape[2]
    count = len(pieces)
    steps, whole, tokens, features, gain_spec, weights, grads, held = feed_specs(pieces, rows, width)
    return pl.pallas_call(
        functools.partial(feed_second_kernel, count),
        out_shape=(
            jax.ShapeDtypeStruct((width, rows // 2), bf16),
            jax.ShapeDtypeStruct((width, rows // 2), bf16),
            jax.ShapeDtypeStruct((width, rows), f32),
            jax.ShapeDtypeStruct((width, rows), bf16),
            jax.ShapeDtypeStruct((KV_HEADS, GROUP, rows), f32),
            jax.ShapeDtypeStruct((width, 1), f32),
            jax.ShapeDtypeStruct((width, units), bf16),
            jax.ShapeDtypeStruct((3, width, units), bf16),
        ),
        grid_spec=pltpu.PrefetchScalarGridSpec(
            num_scalar_prefetch=1,
            grid=(steps,),
            in_specs=weights
            + [
                features, features, features, tokens, tokens, features, features, features, gain_spec,
                whole((width, width)),
            ],
            out_specs=(
                whole((width, rows // 2)),
                whole((width, rows // 2)),
                features,
                features,
                whole((KV_HEADS, GROUP, rows)),
                whole((width, 1)),
                whole((width, units)),
                grads,
            ),
            scratch_shapes=[
                pltpu.VMEM((width, rows), f32),
                pltpu.VMEM((width, rows), f32),
                held,
            ],
        ),
        compiler_params=pltpu.CompilerParams(vmem_limit_bytes=VMEM),
        cost_estimate=pl.CostEstimate(
            flops=20 * rows * width * units, bytes_accessed=12 * units * width, transcendentals=0
        ),
        name="feed_second",
    )(
        info, *pieces, middle, mixed_t, cot, second, cot_rows, second_t, layer_sum, d_second, gains,
        output_t,
    )


def finish_kernel(
    info_ref, even_ref, odd_ref, dq_ref, a_ref, aq_ref, xq_ref, mg_ref, query_ref, key_ref, value_ref,
    gain_ref, gg2_ref, keep_ref, give_ref, chunk_ref, send_ref, kv_sum, gg_ref, q_sum,
):
    size = even_ref.shape[1] // (2 * KV_HEADS)
    step = pl.program_id(0)

    @pl.when(step == 0)
    def _():
        dq = dq_ref[...]
        grad_query = mm(dq, aq_ref[...], 1, 1)
        q_sum[...] = grad_query.astype(bf16)
        query_t = query_ref[...].astype(f32)
        gg_ref[...] = jnp.sum(query_t * grad_query, axis=0, keepdims=True)
        d_a = mm(query_t.T.astype(bf16), dq, 1, 0)
        chunk = mg_ref[...] + column_norm_back(d_a, xq_ref[...].astype(f32), gain_ref[:, 0:1])
        chunk_ref[...] = chunk
        send_ref[...] = chunk[:, chunk.shape[1] // 2 :].astype(bf16)
        kv_sum[...] = jnp.zeros_like(kv_sum)

    kv_sum[...] += mm(even_ref[0], a_ref[0], 1, 1) + mm(odd_ref[0], a_ref[1], 1, 1)

    @pl.when(step == pl.num_programs(0) - 1)
    def _():
        total = gg_ref[...]
        grads = [[], []]
        for group in range(KV_HEADS):
            rows = slice(group * size, (group + 1) * size)
            grad_key = kv_sum[2 * group * size : (2 * group + 1) * size, :]
            grad_value = kv_sum[(2 * group + 1) * size : (2 * group + 2) * size, :]
            grads[0].append(grad_key)
            grads[1].append(grad_value)
            total = total + jnp.sum(
                key_ref[rows, :].astype(f32) * grad_key + value_ref[rows, :].astype(f32) * grad_value,
                axis=0,
                keepdims=True,
            )
        gain_grad = jnp.concatenate([total / gain_ref[:, 0:1].T, gg2_ref[...].T], axis=0)
        grads = [jnp.concatenate(items, axis=0) for items in grads]
        shards, part, width = keep_ref.shape
        kv_part = KV_HEADS * size // shards
        first = info_ref[1] == 0
        for shard in range(shards):
            queries = q_sum[shard * part : (shard + 1) * part, :].astype(f32)
            rows = slice(shard * kv_part, (shard + 1) * kv_part)
            gain_rows = jnp.concatenate(
                [gain_grad, jnp.zeros((part - 2 * kv_part - 2, width), f32)], axis=0
            )
            others = jnp.concatenate([grads[0][rows], grads[1][rows], gain_rows], axis=0)
            keep_ref[shard] = jnp.where(first, queries, others).astype(bf16)
            give_ref[shard] = jnp.where(first, others, queries).astype(bf16)


def finish(info, even, odd, dq_t, a_all, a, x, middle_grad, query_t, key_t, value_t, gains, gain_second, shards):
    pairs, terms, rows = even.shape
    width = x.shape[0]
    kv_width = key_t.shape[0]
    pack = jax.ShapeDtypeStruct((shards, width // shards, width), bf16)
    whole = lambda shape: pl.BlockSpec(shape, lambda i, info: (0,) * len(shape))
    pair = pl.BlockSpec((1, terms, rows), lambda i, info: (i, 0, 0))
    return pl.pallas_call(
        finish_kernel,
        out_shape=(
            pack,
            pack,
            jax.ShapeDtypeStruct((width, rows), f32),
            jax.ShapeDtypeStruct((width, rows // 2), bf16),
        ),
        grid_spec=pltpu.PrefetchScalarGridSpec(
            num_scalar_prefetch=1,
            grid=(pairs,),
            in_specs=[
                pair,
                pair,
                whole((width, rows)),
                pl.BlockSpec((2, width, rows), lambda i, info: (i, 0, 0)),
                whole((width, rows)),
                whole((width, rows)),
                whole((width, rows)),
                whole((width, width)),
                whole((kv_width, width)),
                whole((kv_width, width)),
                whole((width, 2)),
                whole((width, 1)),
            ],
            out_specs=(
                whole(pack.shape),
                whole(pack.shape),
                whole((width, rows)),
                whole((width, rows // 2)),
            ),
            scratch_shapes=[
                pltpu.VMEM((terms, width), f32),
                pltpu.VMEM((1, width), f32),
                pltpu.VMEM((width, width), bf16),
            ],
        ),
        compiler_params=pltpu.CompilerParams(vmem_limit_bytes=VMEM),
        cost_estimate=pl.CostEstimate(
            flops=4 * pairs * rows * width * terms, bytes_accessed=8 * 1024 * 1024, transcendentals=0
        ),
        name="finish",
    )(info, even, odd, dq_t, a_all, a, x, middle_grad, query_t, key_t, value_t, gains, gain_second)


def last_kernel(count, *refs):
    own_ref = refs[0]
    got_refs = refs[1 : 1 + count]
    x_ref, chunk_ref, back_ref, key_ref, value_ref, gain_ref, out_ref = refs[1 + count :]
    total = own_ref[...].astype(f32)
    for got in got_refs:
        total = total + got[...].astype(f32)
    total = total.astype(bf16)
    size = total.shape[0] // (2 * KV_HEADS)
    keys = [total[2 * g * size : (2 * g + 1) * size] for g in range(KV_HEADS)]
    values = [total[(2 * g + 1) * size : (2 * g + 2) * size] for g in range(KV_HEADS)]
    weights = jnp.concatenate([key_ref[...], value_ref[...]], axis=0).astype(f32).T.astype(bf16)
    d_a = mm(weights, jnp.concatenate(keys + values, axis=0), 1, 0)
    back = column_norm_back(d_a, x_ref[...].astype(f32), gain_ref[:, 0:1])
    half = back_ref.shape[1]
    out_ref[:, :half] = chunk_ref[:, :half] + back[:, :half]
    out_ref[:, half:] = back_ref[...].astype(f32) + back[:, half:]


def last(pair, got, x_own, chunk_grad, back, key_t, value_t, gains):
    width, rows = x_own.shape
    whole = lambda shape: pl.BlockSpec(shape, lambda i: (0,) * len(shape))
    return pl.pallas_call(
        functools.partial(last_kernel, len(got)),
        out_shape=jax.ShapeDtypeStruct((width, rows), f32),
        grid=(1,),
        in_specs=[whole(item.shape) for item in (pair, *got, x_own, chunk_grad, back, key_t, value_t, gains)],
        out_specs=whole((width, rows)),
        compiler_params=pltpu.CompilerParams(vmem_limit_bytes=VMEM // 4 * 3),
        cost_estimate=pl.CostEstimate(
            flops=2 * rows * width * pair.shape[0], bytes_accessed=6 * 1024 * 1024, transcendentals=0
        ),
        name="last",
    )(pair, *got, x_own, chunk_grad, back, key_t, value_t, gains)


def add_kernel(info_ref, keep_ref, got_ref, output_ref, *out_refs):
    for mask, out_ref in enumerate(out_refs):

        @pl.when(pl.program_id(0) == mask)
        def _(mask=mask, out_ref=out_ref):
            matrix = info_ref[0] ^ mask

            @pl.when(matrix < 3)
            def _():
                out_ref[...] = (keep_ref[0].astype(f32) + got_ref[0].astype(f32)).astype(bf16)

            @pl.when(matrix >= 3)
            def _():
                out_ref[...] = output_ref[...]


def add_rotated(info, keep, got, output):
    _, width, units = keep.shape
    feed = pl.BlockSpec((1, width, units), lambda i, info: (jnp.minimum(info[0] ^ i, 2), 0, 0))
    whole = pl.BlockSpec((width, units), lambda i, info: (0, 0))
    return pl.pallas_call(
        add_kernel,
        out_shape=[jax.ShapeDtypeStruct((width, units), bf16)] * 4,
        grid_spec=pltpu.PrefetchScalarGridSpec(
            num_scalar_prefetch=1,
            grid=(4,),
            in_specs=[feed, feed, whole],
            out_specs=[whole] * 4,
        ),
        compiler_params=pltpu.CompilerParams(vmem_limit_bytes=VMEM),
        name="add_rotated",
    )(info, keep, got, output)


def shard_pieces(piece):
    return [piece] + [swap(piece, "shard", mask) for mask in range(1, lax.axis_size("shard"))]


def in_order(pieces):
    me = lax.axis_index("shard")
    bit = 1
    while bit < len(pieces):
        odd = (me & bit) > 0
        pieces = [jnp.where(odd, pieces[j ^ bit], pieces[j]) for j in range(len(pieces))]
        bit *= 2
    return jnp.stack(pieces)


def scatter_shards(pieces):
    count = lax.axis_size("shard")
    me = lax.axis_index("shard")
    total = lax.dynamic_index_in_dim(pieces, me, 0, False).astype(f32)
    for mask in range(1, count):
        sent = lax.dynamic_index_in_dim(pieces, me ^ mask, 0, False).astype(bf16)
        total = total + swap(sent, "shard", mask).astype(f32)
    return total


def scatter_doubling(pieces):
    me = lax.axis_index("shard")
    mask = pieces.shape[0] // 2
    while mask:
        halves = pieces.reshape((2, mask) + pieces.shape[1:])
        upper = (me & mask) > 0
        sent = jnp.where(upper, halves[0], halves[1])
        kept = jnp.where(upper, halves[1], halves[0])
        total = kept.astype(f32) + swap(sent, "shard", mask).astype(f32)
        pieces = total.astype(bf16)
        mask //= 2
    return pieces[0]


def sum_context(value):
    total = value.astype(f32)
    low = value.astype(bf16)
    for mask in range(1, lax.axis_size("context")):
        total = total + swap(low, "context", mask).astype(f32)
    return total


def per_device(
    hidden_in,
    segment_ids,
    norm_gains,
    w_query,
    w_key,
    w_value,
    w_output,
    w_gate,
    w_up,
    w_down,
    cotangent,
):
    rows, width = hidden_in.shape[1], hidden_in.shape[2]
    half = rows // 2
    seg_row = segment_ids[0]
    length = seg_row.shape[0]
    shards = lax.axis_size("shard")
    contexts = lax.axis_size("context")
    blocks = lax.axis_size(SEQ)
    me = lax.axis_index(SEQ)
    core = lax.axis_index("tensor")
    context = lax.axis_index("context")
    part = w_query.shape[1]
    kv_part = w_key.shape[1]
    kv_width = kv_part * shards
    units = w_gate.shape[0]
    head_size = width // HEADS
    scale = head_size**-0.5

    starts = doc_starts(seg_row)
    place = (
        (jnp.arange(blocks, dtype=jnp.int32) ^ me)[:, None] * rows
        + jnp.arange(rows, dtype=jnp.int32)[None, :]
    ).reshape(1, -1)
    placed_starts = jnp.max(jnp.where(place >= starts[:, None], starts[:, None], 0), axis=0)
    positions = (place[0] - placed_starts).astype(f32)
    frequency = rope_base ** (-jnp.arange(head_size // 2, dtype=f32) * 2.0 / head_size)
    angles = frequency[:, None] * positions[None, :]
    cosine, sine = jnp.cos(angles), jnp.sin(angles)
    info = jnp.concatenate([jnp.reshape(me, (1,)).astype(jnp.int32), starts])

    x_own = hidden_in[0].T
    by_context = contexts == 4 and part % 16 == 0

    gain_rows = part - 2 * kv_part
    key_values = jnp.concatenate(
        [w_key.T, w_value.T, jnp.pad(norm_gains, ((0, gain_rows - 2), (0, width - part)))], axis=0
    )
    pack = jnp.where(core == 0, w_query.T, key_values)
    later = jnp.stack([w_gate.T, w_up.T, w_down.T, jnp.pad(w_output.T, ((0, 0), (0, units - width)))])
    if by_context:
        x_one, x_two = swap(x_own, "context", 1), swap(x_own, "context", 2)
        later_c = lax.dynamic_index_in_dim(later, context, 0, False)
        pack_mine = shard_pieces(pack)
        x_one, x_two, pack_mine, later_c, cosine, sine = lax.optimization_barrier(
            (x_one, x_two, pack_mine, later_c, cosine, sine)
        )
        fetched = shard_pieces(later_c)[1:]
        x_three = [swap(x_two[:, :half], "context", 1), swap(x_one[:, half:], "context", 2)]
        x_three, fetched, pack_mine = lax.optimization_barrier((x_three, fetched, pack_mine))
        x_near = jnp.stack([x_own, x_one, x_two, jnp.concatenate(x_three, axis=1)])
        pack_mine, fetched = jnp.stack(pack_mine), jnp.stack(fetched)
        x_near, pack_mine, fetched = lax.optimization_barrier((x_near, pack_mine, fetched))
        x_far = swap(x_near, "tensor", 1)
        x_arrays = [x_near, x_far]
        layout = tuple((r % 2, r // 2) for r in range(8))
        fetched = [fetched] + [swap(fetched, "context", mask) for mask in range(1, 4)]
    else:
        near = [x_own] + [swap(x_own, "context", mask) for mask in range(1, contexts)]
        x_arrays = [item[None] for item in near] + [swap(jnp.stack(near), "tensor", 1)]
        layout = tuple((c if r == 0 else contexts, 0 if r == 0 else c) for c in range(contexts) for r in (0, 1))
        later_pieces = shard_pieces(later)
        pack_mine = jnp.stack(shard_pieces(pack))
    pack_theirs = swap(pack_mine, "tensor", 1)
    shard = lax.axis_index("shard")
    places = jnp.stack([shard, core, context]).astype(jnp.int32)
    query_t, key_t, value_t, gain_parts = unpack(places, [pack_mine], [pack_theirs], kv_part)
    query_t = query_t.reshape(width, width)
    key_t = key_t.reshape(kv_width, width)
    value_t = value_t.reshape(kv_width, width)
    gains = gain_parts[:, :2, :part].transpose(0, 2, 1).reshape(width, 2).astype(f32)

    def chunks(array, axis):
        return jnp.concatenate(
            [
                lax.slice_in_dim(array, 0, half, axis=axis),
                lax.slice_in_dim(array, length - half, length, axis=axis),
            ],
            axis=axis,
        )

    a_all, keys, keys_t, values, values_t, queries_t, a, x = project(
        x_arrays, layout, query_t, key_t, value_t, gains, cosine, sine, scale
    )
    cos_q, sin_q = chunks(cosine, 1), chunks(sine, 1)

    queries_t, cot_own = lax.optimization_barrier((queries_t, cotangent[0].T))
    cot_got = lax.ppermute(cot_own[:, half:], SEQ, flip(blocks, blocks - 1))
    cot = jnp.concatenate([cot_own[:, :half], cot_got], axis=1)
    attended = attend(0, 2, (), info, queries_t, keys, values_t, rows)

    if by_context:
        attended, fetched, cot, later = lax.optimization_barrier((attended, fetched, cot, later))
        mine_all = [later] + fetched
    else:
        later_pieces = in_order(later_pieces).transpose(1, 0, 2, 3).reshape(4, width, units)
        attended, later_pieces = lax.optimization_barrier((attended, later_pieces))
        mine_all = [later_pieces]
    theirs_all = [swap(item, "tensor", 1) for item in mine_all]
    mixed_t, log_total = attend(2, 1, attended, info, queries_t, keys, values_t, rows)
    middle, second, cot_rows, second_t, layer_sum, d_second, grads_theirs, output_t = feed_first(
        places, x, mixed_t, cot, gains, theirs_all
    )
    ff_got = swap(grads_theirs, "tensor", 1)
    layer_keep, layer_send, middle_grad, mixed_grad_t, delta, gain_grad_second, output_sum, grads_mine = (
        feed_second(
            places, middle, mixed_t, cot, second, cot_rows, second_t, layer_sum, d_second, gains,
            output_t, mine_all,
        )
    )
    wide = units

    def back(group, earlier, info):
        return attend_back(
            group, earlier, info, queries_t, mixed_grad_t, keys, keys_t, values, log_total, delta,
            cosine, sine, cos_q, sin_q, rows, scale,
        )

    pair_of = flip(blocks, blocks - 1)
    if contexts == 4:
        both = add_rotated(places[2:], grads_mine, ff_got, output_sum)
        info, both = lax.optimization_barrier((info, both))
        got = [swap(item, "context", mask) for mask, item in enumerate(both) if mask]
        terms = back(0, (), info)
        terms = back(1, terms, info)
        terms, got = lax.optimization_barrier((terms, got))
        owned = both[0].astype(f32)
        for item in got:
            owned = owned + item.astype(f32)
        owned = owned.reshape(shards, part, wide)
        kept = lax.dynamic_index_in_dim(owned, shard, 0, False)
        sent = [
            lax.dynamic_index_in_dim(owned, shard ^ mask, 0, False).astype(bf16)
            for mask in range(1, shards)
        ]
        terms, kept, sent, layer_send = lax.optimization_barrier((terms, kept, sent, layer_send))
        got = [swap(item, "shard", mask + 1) for mask, item in enumerate(sent)]
        layer_got = lax.ppermute(layer_send, SEQ, pair_of)
        terms = back(2, terms, info)
        terms, got, layer_got = lax.optimization_barrier((terms, got, layer_got))
        for item in got:
            kept = kept + item.astype(f32)
        owned_low = kept.astype(bf16)
        spread = [owned_low] + [swap(owned_low, "context", mask) for mask in range(1, 4)]
    else:
        layer_got = lax.ppermute(layer_send, SEQ, pair_of)
        ff_sum = grads_mine.astype(f32) + ff_got.astype(f32)
        both = [*ff_sum, output_sum]
        terms = back(0, (), info)
        terms = back(1, terms, info)
        terms = back(2, terms, info)
    dq_t, even, odd = terms
    odd_got = swap(odd, "tensor", 1)
    finished = finish(
        places, even, odd, dq_t, a_all, a, x, middle_grad, query_t, key_t, value_t, gains,
        gain_grad_second, shards,
    )
    if contexts == 4:
        odd_got, spread, finished = lax.optimization_barrier((odd_got, spread, finished))
        for bit in (1, 2):
            away = (context & bit) > 0
            spread = [jnp.where(away, spread[j ^ bit], spread[j]) for j in range(4)]
        final = spread
    else:
        large = jnp.stack([item.astype(bf16) for item in both]).reshape(4, shards, part, wide).transpose(1, 0, 2, 3)
        final = lax.psum(scatter_shards(large).astype(bf16), "context")
    keep, give, chunk_grad, chunk_send = finished
    pair = [
        (even[mask].astype(f32) + odd_got[mask].astype(f32)).astype(bf16) for mask in range(contexts)
    ]

    grad_gate, grad_up, grad_down = [final[matrix].astype(f32).T for matrix in range(3)]
    output_low = final[3][:, :width]
    grad_output = (output_low.astype(f32) + swap(output_low, "tensor", 1).astype(f32)).T

    both = (keep.astype(f32) + swap(give, "tensor", 1).astype(f32)).astype(bf16)
    both, pair, chunk_send = lax.optimization_barrier((both, pair, chunk_send))
    pair_got = [swap(item, "context", mask) for mask, item in enumerate(pair) if mask]
    returned = lax.ppermute(chunk_send, SEQ, flip(blocks, blocks - 1))
    small = scatter_doubling(both)
    small, pair_got, returned, layer_got = lax.optimization_barrier(
        (small, pair_got, returned, layer_got)
    )
    layer_value = jnp.concatenate([layer_keep, layer_got], axis=1).T
    grad_hidden = last(pair[0], pair_got, x_own, chunk_grad, returned, key_t, value_t, gains).T
    small = sum_context(small).astype(bf16)
    small, grad_hidden = lax.optimization_barrier((small, grad_hidden))
    small_other = swap(small, "tensor", 1)
    grad_query = jnp.where(core == 0, small, small_other).astype(f32).T
    small = jnp.where(core == 0, small_other, small).astype(f32)
    grad_key = small[:kv_part].T
    grad_value = small[kv_part : 2 * kv_part].T
    gain_grads = small[2 * kv_part : 2 * kv_part + 2]
    grad_gains = lax.dynamic_slice_in_dim(gain_grads, shard * part, part, 1)

    return (
        layer_value[None],
        grad_hidden[None],
        grad_gains,
        grad_query,
        grad_key,
        grad_value,
        grad_output,
        grad_gate,
        grad_up,
        grad_down,
    )


def solution(mesh):
    return jax.shard_map(
        per_device,
        mesh=mesh,
        in_specs=(
            P("shard", ("context", "tensor"), None),
            P("shard", None),
            P(None, "shard"),
            P(None, "shard"),
            P(None, "shard"),
            P(None, "shard"),
            P(None, "shard"),
            P("tensor", "shard"),
            P("tensor", "shard"),
            P("tensor", "shard"),
            P("shard", ("context", "tensor"), None),
        ),
        out_specs=(
            P("shard", ("context", "tensor"), None),
            P("shard", ("context", "tensor"), None),
            P(None, "shard"),
            P(None, "shard"),
            P(None, "shard"),
            P(None, "shard"),
            P(None, "shard"),
            P("tensor", "shard"),
            P("tensor", "shard"),
            P("tensor", "shard"),
        ),
        check_vma=False,
    )
```

```python
import functools

import jax
import jax.numpy as jnp
from jax import lax
from jax.experimental import pallas as pl
from jax.experimental.pallas import tpu as pltpu
from jax.sharding import PartitionSpec as P

HEADS = 9
KV_HEADS = 3
DOCS = 4
GROUP = HEADS // KV_HEADS

rope_base = 100000.0
norm_eps = 1e-05
masked_score = -1e30

VMEM = 60 * 1024 * 1024
f32 = jnp.float32
bf16 = jnp.bfloat16
SEQ = ("context", "tensor")


def mm(left, right, left_dim, right_dim):
    return lax.dot_general(
        left, right, (((left_dim,), (right_dim,)), ((), ())), preferred_element_type=f32
    )


def flip(count, mask):
    return [(i, i ^ mask) for i in range(count)]


def swap(value, axis, mask):
    return lax.ppermute(value, axis, flip(lax.axis_size(axis), mask))


def doc_starts(seg_row):
    one_hot = (seg_row[None, :] == jnp.arange(DOCS, dtype=jnp.int32)[:, None]).astype(jnp.int32)
    doc_counts = jnp.sum(one_hot, axis=1)
    return jnp.cumsum(doc_counts) - doc_counts


def column_rms(hidden):
    return lax.rsqrt(jnp.mean(hidden * hidden, axis=0, keepdims=True) + norm_eps)


def column_norm_back(grad, hidden, gain):
    inverse = column_rms(hidden)
    unit = hidden * inverse
    scaled = grad * gain
    return (scaled - unit * jnp.mean(scaled * unit, axis=0, keepdims=True)) * inverse


def turn_head(head, cosine, sine, sign):
    half = cosine.shape[0]
    first, second = head[:half], head[half:]
    return jnp.concatenate(
        [first * cosine - sign * (second * sine), second * cosine + sign * (first * sine)], axis=0
    )


def doc_start(info_ref, index):
    start = jnp.int32(0)
    for doc in range(1, DOCS):
        start = jnp.where(index >= info_ref[1 + doc], info_ref[1 + doc], start)
    return start


def chunk_start(info_ref, chunk, blocks, size):
    me = info_ref[0]
    return jnp.where(chunk == 0, me * 2 * size, (blocks - 1 - me) * 2 * size + size)


def key_ranges(info_ref, chunk, blocks, key_block):
    size = key_block // 2
    first = chunk_start(info_ref, chunk, blocks, size)
    low = doc_start(info_ref, first) // key_block
    high = (first + size + key_block - 1) // key_block
    full_from = (doc_start(info_ref, first + size - 1) + key_block - 1) // key_block
    high = high - jnp.where(chunk == 0, 1, 0)
    full_from = jnp.minimum(jnp.maximum(full_from, low), high)
    full_to = jnp.minimum(jnp.maximum(first // key_block, full_from), high)
    return low, full_from, full_to, high


def allowed_mask(info_ref, block, key_block, chunk, blocks, keys):
    size = key_block // 2
    first = chunk_start(info_ref, chunk, blocks, size)
    index = first + lax.broadcasted_iota(jnp.int32, (1, size), 1)
    start = doc_start(info_ref, index)
    key_index = block * key_block + lax.broadcasted_iota(jnp.int32, (keys, size), 0)
    return (key_index >= start) & (key_index <= index)


def side_by_side(ref, size):
    return jnp.concatenate([ref[m * size : (m + 1) * size, :] for m in range(GROUP)], axis=1)


def forward_kernel(key_block, group, info_ref, *refs):
    if group:
        refs = refs[2:]
    q_ref, k_ref, vt_ref, o_ref, lse_ref, m_ref, l_ref, acc_ref, q_side = refs
    chunk = pl.program_id(1)
    me = info_ref[0]
    size = k_ref.shape[2]
    tokens = q_ref.shape[1]
    blocks = k_ref.shape[1] // key_block
    m_ref[...] = jnp.full_like(m_ref, masked_score)
    acc_ref[...] = jnp.zeros_like(acc_ref)
    q_side[...] = side_by_side(q_ref, size)

    def block_scores(block, masked, keys):
        place = pl.multiple_of((block ^ me) * key_block, key_block)
        scores = mm(k_ref[0, pl.ds(place, keys), :], q_side[...], 1, 0)
        if masked:
            mask = allowed_mask(info_ref, block, key_block, chunk, blocks, keys)
            scores = jnp.concatenate(
                [
                    jnp.where(mask, scores[:, m * tokens : (m + 1) * tokens], masked_score)
                    for m in range(GROUP)
                ],
                axis=1,
            )
        return scores

    def step(first, count, masked, keys=key_block):
        scores = [block_scores(first + i, masked, keys) for i in range(count)]
        old = m_ref[...]
        new = old
        for item in scores:
            new = jnp.maximum(new, jnp.max(item, axis=0, keepdims=True))
        m_ref[...] = new
        total = acc_ref[...] * jnp.exp(old - new)
        for i, item in enumerate(scores):
            place = pl.multiple_of(((first + i) ^ me) * key_block, key_block)
            weights = jnp.exp(item - new).astype(bf16)
            values = jnp.concatenate(
                [vt_ref[:, pl.ds(place, keys)], jnp.ones((16, keys), bf16)], axis=0
            )
            total = total + mm(values, weights, 1, 0)
        acc_ref[...] = total

    low, full_from, full_to, high = key_ranges(info_ref, chunk, blocks, key_block)
    pairs = (full_to - full_from) // 2
    pl.loop(low, full_from)(lambda b: step(b, 1, True))
    pl.loop(0, pairs)(lambda b: step(full_from + 2 * b, 2, False))
    pl.loop(full_from + 2 * pairs, full_to)(lambda b: step(b, 1, False))
    pl.loop(full_to, high)(lambda b: step(b, 1, True))
    pl.when(chunk == 0)(lambda: step(me, 1, True, key_block // 2))
    for member in range(GROUP):
        rows = slice(member * size, (member + 1) * size)
        lanes = slice(member * tokens, (member + 1) * tokens)
        total = acc_ref[size : size + 1, lanes]
        o_ref[rows, :] = acc_ref[:size, lanes] / total
        lse_ref[0, member : member + 1, :] = m_ref[:, lanes] + jnp.log(total)


def backward_kernel(key_block, scale, group, *refs):
    if group:
        refs = refs[:1] + refs[4:]
    (
        info_ref, q_ref, do_ref, k_ref, kt_ref, v_ref, lse_ref, delta_ref,
        cos_ref, sin_ref, cosq_ref, sinq_ref,
        dq_ref, even_ref, odd_ref, dk_ref, dv_ref, dq_sum, q_side, do_side,
    ) = refs
    chunk = pl.program_id(0)
    me = info_ref[0]
    size = k_ref.shape[2]
    blocks = dk_ref.shape[0]
    tokens = q_ref.shape[1]
    dq_sum[...] = jnp.zeros_like(dq_sum)
    q_side[...] = side_by_side(q_ref, size)
    do_side[...] = side_by_side(do_ref, size)
    log_total = jnp.concatenate([lse_ref[0, m : m + 1, :] for m in range(GROUP)], axis=1)
    delta = jnp.concatenate([delta_ref[0, m : m + 1, :] for m in range(GROUP)], axis=1)

    @pl.when(chunk == 0)
    def _():
        dk_ref[...] = jnp.zeros_like(dk_ref)
        dv_ref[...] = jnp.zeros_like(dv_ref)

    def step(block, masked, count=key_block):
        spot = block ^ me
        place = pl.multiple_of(spot * key_block, key_block)
        keys = k_ref[0, pl.ds(place, count), :]
        values = v_ref[0, pl.ds(place, count), :]
        keys_t = kt_ref[:, pl.ds(place, count)]
        scores = mm(keys, q_side[...], 1, 0)
        if masked:
            mask = allowed_mask(info_ref, block, key_block, chunk, blocks, count)
            scores = jnp.concatenate(
                [
                    jnp.where(mask, scores[:, m * tokens : (m + 1) * tokens], masked_score)
                    for m in range(GROUP)
                ],
                axis=1,
            )
        probs = jnp.exp(scores - log_total)
        prob_grad = mm(values, do_side[...], 1, 0)
        raw = (probs * (prob_grad - delta)).astype(bf16)
        dv = mm(do_side[...], probs.astype(bf16), 1, 1)
        dk = mm(q_side[...], raw, 1, 1)
        dq_sum[...] += mm(keys_t, raw, 1, 0)
        dk_ref[spot, :, :count] += dk
        dv_ref[spot, :, :count] += dv

    low, full_from, full_to, high = key_ranges(info_ref, chunk, blocks, key_block)
    pl.loop(low, full_from)(lambda b: step(b, True))
    pl.loop(full_from, full_to)(lambda b: step(b, False))
    pl.loop(full_to, high)(lambda b: step(b, True))
    pl.when(chunk == 0)(lambda: step(me, True, key_block // 2))
    for member in range(GROUP):
        rows = slice(member * size, (member + 1) * size)
        dq_ref[rows, :] = turn_head(
            dq_sum[:, member * tokens : (member + 1) * tokens] * scale, cosq_ref[...], sinq_ref[...], -1.0).astype(
            bf16
        )

    @pl.when(chunk == 1)
    def _():
        for block in range(blocks):
            columns = slice(block * key_block, (block + 1) * key_block)
            out_ref = odd_ref if block % 2 else even_ref
            out_ref[block // 2, :size, :] = turn_head(
                dk_ref[block], cos_ref[:, columns], sin_ref[:, columns], -1.0
            ).astype(bf16)
            out_ref[block // 2, size:, :] = dv_ref[block].astype(bf16)


def attend(group, groups, earlier, info, queries_t, keys, values_t, key_block):
    length, size = keys.shape[1], keys.shape[2]
    tokens = queries_t.shape[1]
    chunk = tokens // 2
    wide = GROUP * size
    head_block = pl.BlockSpec((wide, chunk), lambda g, c, info: (group + g, c))
    stat_block = pl.BlockSpec((1, GROUP, chunk), lambda g, c, info: (group + g, 0, c))
    elements = groups * GROUP * tokens * length // 2
    return pl.pallas_call(
        functools.partial(forward_kernel, key_block, group),
        out_shape=(
            jax.ShapeDtypeStruct((HEADS * size, tokens), f32),
            jax.ShapeDtypeStruct((KV_HEADS, GROUP, tokens), f32),
        ),
        grid_spec=pltpu.PrefetchScalarGridSpec(
            num_scalar_prefetch=1,
            grid=(groups, 2),
            in_specs=[pl.BlockSpec(memory_space=pl.ANY)] * len(earlier)
            + [
                head_block,
                pl.BlockSpec((1, length, size), lambda g, c, info: (group + g, 0, 0)),
                pl.BlockSpec((size, length), lambda g, c, info: (group + g, 0)),
            ],
            out_specs=(head_block, stat_block),
            scratch_shapes=[
                pltpu.VMEM((1, GROUP * chunk), f32),
                pltpu.VMEM((1, GROUP * chunk), f32),
                pltpu.VMEM((size + 16, GROUP * chunk), f32),
                pltpu.VMEM((size, GROUP * chunk), bf16),
            ],
        ),
        input_output_aliases={1 + number: number for number in range(len(earlier))},
        compiler_params=pltpu.CompilerParams(vmem_limit_bytes=VMEM),
        cost_estimate=pl.CostEstimate(
            flops=16 * elements * size, bytes_accessed=4 * 1024 * 1024, transcendentals=elements
        ),
        name="attend",
    )(info, *earlier, queries_t, keys, values_t)


def attend_back(
    group, earlier, info, queries_t, grads_t, keys, keys_t, values, log_total, delta,
    cosine, sine, cos_q, sin_q, key_block, scale,
):
    length, size = keys.shape[1], keys.shape[2]
    tokens = queries_t.shape[1]
    chunk = tokens // 2
    wide = GROUP * size
    blocks = length // key_block
    head_block = pl.BlockSpec((wide, chunk), lambda c, info: (group, c))
    stat_block = pl.BlockSpec((1, GROUP, chunk), lambda c, info: (group, 0, c))
    token_block = pl.BlockSpec((1, length, size), lambda c, info: (group, 0, 0))
    feature_block = pl.BlockSpec((size, length), lambda c, info: (group, 0))
    table = pl.BlockSpec((size // 2, length), lambda c, info: (0, 0))
    table_q = pl.BlockSpec((size // 2, chunk), lambda c, info: (0, c))
    terms = pl.BlockSpec((blocks // 2, 2 * size, key_block), lambda c, info: (0, group, 0))
    elements = GROUP * tokens * length // 2
    terms_shape = jax.ShapeDtypeStruct((blocks // 2, KV_HEADS * 2 * size, key_block), bf16)
    return pl.pallas_call(
        functools.partial(backward_kernel, key_block, scale, group),
        out_shape=(jax.ShapeDtypeStruct((HEADS * size, tokens), bf16), terms_shape, terms_shape),
        grid_spec=pltpu.PrefetchScalarGridSpec(
            num_scalar_prefetch=1,
            grid=(2,),
            in_specs=[pl.BlockSpec(memory_space=pl.ANY)] * len(earlier)
            + [
                head_block, head_block, token_block, feature_block, token_block, stat_block, stat_block,
                table, table, table_q, table_q,
            ],
            out_specs=(head_block, terms, terms),
            scratch_shapes=[
                pltpu.VMEM((blocks, size, key_block), f32),
                pltpu.VMEM((blocks, size, key_block), f32),
                pltpu.VMEM((size, GROUP * chunk), f32),
                pltpu.VMEM((size, GROUP * chunk), bf16),
                pltpu.VMEM((size, GROUP * chunk), bf16),
            ],
        ),
        input_output_aliases={1 + number: number for number in range(len(earlier))},
        compiler_params=pltpu.CompilerParams(vmem_limit_bytes=VMEM),
        cost_estimate=pl.CostEstimate(
            flops=40 * elements * size, bytes_accessed=4 * 1024 * 1024, transcendentals=elements
        ),
        name="attend_back",
    )(
        info, *earlier, queries_t, grads_t, keys, keys_t, values, log_total, delta,
        cosine, sine, cos_q, sin_q,
    )


def unpack_kernel(count, kv_part, info_ref, *refs):
    mine, theirs = refs[:count], refs[count : 2 * count]
    query_ref, key_ref, value_ref, gain_ref = refs[2 * count :]
    first = info_ref[1] == 0
    mask = 0
    for number in range(count):
        for row in range(mine[number].shape[0]):
            spot = info_ref[0] ^ mask
            left, right = mine[number][row], theirs[number][row]
            query_ref[spot] = jnp.where(first, left, right)
            other = jnp.where(first, right, left)
            key_ref[spot] = other[:kv_part]
            value_ref[spot] = other[kv_part : 2 * kv_part]
            gain_ref[spot] = other[2 * kv_part :]
            mask += 1


def unpack(info, mine, theirs, kv_part):
    count = len(mine)
    total = sum(item.shape[0] for item in mine)
    part, width = mine[0].shape[1:]
    whole = lambda shape: pl.BlockSpec(shape, lambda i, info: (0,) * len(shape))
    shapes = [(total, size, width) for size in (part, kv_part, kv_part, part - 2 * kv_part)]
    return pl.pallas_call(
        functools.partial(unpack_kernel, count, kv_part),
        out_shape=[jax.ShapeDtypeStruct(shape, bf16) for shape in shapes],
        grid_spec=pltpu.PrefetchScalarGridSpec(
            num_scalar_prefetch=1,
            grid=(1,),
            in_specs=[whole(item.shape) for item in (*mine, *theirs)],
            out_specs=[whole(shape) for shape in shapes],
        ),
        name="unpack",
    )(info, *mine, *theirs)


def project_kernel(layout, arrays, scale, *refs):
    pieces = len(layout)
    x_refs = [refs[array].at[row] for array, row in layout]
    query_ref, key_ref, value_ref, gain_ref, cos_ref, sin_ref = refs[arrays : arrays + 6]
    a_ref, k_ref, kt_ref, v_ref, vt_ref, q_ref, aq_ref, xq_ref = refs[arrays + 6 : arrays + 14]
    held, sems, cos_q, sin_q = refs[arrays + 14 :]
    step = pl.program_id(0)
    tokens = xq_ref.shape[1]
    chunk = tokens // 2

    @pl.when(step == 0)
    def _():
        for number in range(pieces):
            pltpu.make_async_copy(x_refs[number], held.at[number], sems.at[number]).start()

    for number in range(pieces):

        @pl.when(step == number)
        def _(number=number):
            pltpu.make_async_copy(x_refs[number], held.at[number], sems.at[number]).wait()

    x_low = held[step]
    x = x_low.astype(f32)
    a = (x * column_rms(x) * gain_ref[:, 0:1]).astype(bf16)
    a_ref[0] = a
    cosine, sine = cos_ref[...], sin_ref[...]
    k_lin = mm(key_ref[...], a, 1, 0)
    v_lin = mm(value_ref[...], a, 1, 0)
    vt_ref[...] = v_lin.astype(bf16)
    size = k_ref.shape[2]
    for group in range(KV_HEADS):
        rows = slice(group * size, (group + 1) * size)
        turned = turn_head(k_lin[rows], cosine, sine, 1.0)
        kt_ref[rows, :] = turned.astype(bf16)
        k_ref[group] = turned.T.astype(bf16)
        v_ref[group] = v_lin[rows].T.astype(bf16)

    @pl.when(step == 0)
    def _():
        aq_ref[:, :chunk] = a[:, :chunk]
        xq_ref[:, :chunk] = x_low[:, :chunk]
        cos_q[:, :chunk] = cosine[:, :chunk]
        sin_q[:, :chunk] = sine[:, :chunk]

    @pl.when(step == pieces - 1)
    def _():
        aq_ref[:, chunk:] = a[:, chunk:]
        xq_ref[:, chunk:] = x_low[:, chunk:]
        cos_q[:, chunk:] = cosine[:, chunk:]
        sin_q[:, chunk:] = sine[:, chunk:]
        q_lin = mm(query_ref[...], aq_ref[...], 1, 0)
        for head in range(HEADS):
            rows = slice(head * size, (head + 1) * size)
            q_ref[rows, :] = (
                turn_head(q_lin[rows], cos_q[...], sin_q[...], 1.0).astype(bf16) * scale
            ).astype(bf16)


def project(x_arrays, layout, query_t, key_t, value_t, gains, cosine, sine, scale):
    pieces = len(layout)
    arrays = len(x_arrays)
    width, rows = x_arrays[0].shape[1:]
    kv_width = key_t.shape[0]
    size = kv_width // KV_HEADS
    length = pieces * rows
    whole = lambda array: pl.BlockSpec(array.shape, lambda i: (0,) * array.ndim)
    table = pl.BlockSpec((size // 2, rows), lambda i: (0, i))
    by_token = pl.BlockSpec((KV_HEADS, rows, size), lambda i: (0, i, 0))
    by_feature = pl.BlockSpec((kv_width, rows), lambda i: (0, i))
    own = pl.BlockSpec((width, rows), lambda i: (0, 0))
    own_shape = jax.ShapeDtypeStruct((width, rows), bf16)
    return pl.pallas_call(
        functools.partial(project_kernel, layout, arrays, scale),
        out_shape=(
            jax.ShapeDtypeStruct((pieces, width, rows), bf16),
            jax.ShapeDtypeStruct((KV_HEADS, length, size), bf16),
            jax.ShapeDtypeStruct((kv_width, length), bf16),
            jax.ShapeDtypeStruct((KV_HEADS, length, size), bf16),
            jax.ShapeDtypeStruct((kv_width, length), bf16),
            own_shape,
            own_shape,
            own_shape,
        ),
        grid=(pieces,),
        in_specs=[pl.BlockSpec(memory_space=pl.ANY)] * arrays
        + [whole(query_t), whole(key_t), whole(value_t), whole(gains), table, table],
        out_specs=(
            pl.BlockSpec((1, width, rows), lambda i: (i, 0, 0)),
            by_token,
            by_feature,
            by_token,
            by_feature,
            own,
            own,
            own,
        ),
        scratch_shapes=[
            pltpu.VMEM((pieces, width, rows), bf16),
            pltpu.SemaphoreType.DMA((pieces,)),
            pltpu.VMEM((size // 2, rows), f32),
            pltpu.VMEM((size // 2, rows), f32),
        ],
        compiler_params=pltpu.CompilerParams(vmem_limit_bytes=VMEM),
        cost_estimate=pl.CostEstimate(
            flops=8 * length * width * kv_width, bytes_accessed=8 * length * width, transcendentals=0
        ),
        name="project",
    )(*x_arrays, query_t, key_t, value_t, gains, cosine, sine)


def feed_tile(second, second_t, cot, cot_t, weights, grad_ref, sum_ref, db_ref):
    gate_t, up_t, down_t = weights
    gate = mm(second, gate_t, 1, 0)
    upward = mm(second, up_t, 1, 0)
    d_hidden = mm(cot, down_t, 1, 0)
    sig = 1.0 / (1.0 + jnp.exp(-gate))
    silu = gate * sig
    hidden = (silu * upward).astype(bf16)
    d_gate = (d_hidden * upward * sig * (1.0 + gate * (1.0 - sig))).astype(bf16)
    d_up = (d_hidden * silu).astype(bf16)
    sum_ref[...] += mm(down_t, hidden, 1, 1)
    db_ref[...] += mm(gate_t, d_gate, 1, 1) + mm(up_t, d_up, 1, 1)
    grad_ref[0] = mm(second_t, d_gate, 1, 0).astype(bf16)
    grad_ref[1] = mm(second_t, d_up, 1, 0).astype(bf16)
    grad_ref[2] = mm(cot_t, hidden, 1, 0).astype(bf16)


def hold_weights(info_ref, own_ref, other_refs, held):
    shard, context = info_ref[0], info_ref[2]
    for matrix in range(held.shape[0]):
        held[matrix, shard if held.shape[1] > 1 else 0] = own_ref[matrix]
    for number, other in enumerate(other_refs):
        for mask in range(1, held.shape[1]):
            held[context ^ number, shard ^ mask] = other[mask - 1]


def held_tiles(held, tile):
    lanes = pl.ds(pl.multiple_of(pl.program_id(0) * tile, tile), tile)
    return [
        held[matrix, :, :, lanes].reshape(held.shape[1] * held.shape[2], tile) for matrix in range(3)
    ]


def feed_first_kernel(count, info_ref, *refs):
    x_ref, o_ref, cot_ref, gain_ref = refs[count : count + 4]
    h_ref, second_ref, cot_rows, second_t, sum_ref, db_ref, grad_ref, output_ref = refs[
        count + 4 : count + 12
    ]
    held = refs[count + 12]
    width = x_ref.shape[0]

    @pl.when(pl.program_id(0) == 0)
    def _():
        hold_weights(info_ref, refs[0], refs[1:count], held)
        output_t = held[3].reshape(width, held.shape[3])[:, :width]
        output_ref[...] = output_t
        middle = x_ref[...].astype(f32) + mm(output_t, o_ref[...].astype(bf16), 1, 0)
        second = middle * column_rms(middle) * gain_ref[:, 1:2]
        h_ref[...] = middle
        second_t[...] = second.astype(bf16)
        second_ref[...] = second.T.astype(bf16)
        cot_rows[...] = cot_ref[...].astype(f32).T.astype(bf16)
        sum_ref[...] = middle
        db_ref[...] = jnp.zeros_like(db_ref)

    weights = held_tiles(held, grad_ref.shape[2])
    feed_tile(
        second_ref[...], second_t[...], cot_rows[...], cot_ref[...], weights, grad_ref, sum_ref, db_ref
    )


def feed_second_kernel(count, info_ref, *refs):
    (
        h_ref, o_ref, cot_ref, second_ref, cot_rows, second_t, sum_in_ref, db_in_ref, gain_ref, wo_ref,
    ) = refs[count : count + 10]
    layer_ref, send_ref, mg_ref, do_ref, delta_ref, gg_ref, go_ref, grad_ref = refs[
        count + 10 : count + 18
    ]
    sum_ref, db_ref, held = refs[count + 18 :]
    width = h_ref.shape[0]
    step = pl.program_id(0)

    @pl.when(step == 0)
    def _():
        hold_weights(info_ref, refs[0], refs[1:count], held)
        sum_ref[...] = sum_in_ref[...]
        db_ref[...] = db_in_ref[...]

    weights = held_tiles(held, grad_ref.shape[2])
    feed_tile(
        second_ref[...], second_t[...], cot_rows[...], cot_ref[...], weights, grad_ref, sum_ref, db_ref
    )

    @pl.when(step == pl.num_programs(0) - 1)
    def _():
        chunk = layer_ref.shape[1]
        layer_ref[...] = sum_ref[:, :chunk].astype(bf16)
        send_ref[...] = sum_ref[:, chunk:].astype(bf16)
        middle = h_ref[...]
        inverse = column_rms(middle)
        unit = middle * inverse
        grad = db_ref[...]
        gg_ref[...] = jnp.sum(grad * unit, axis=1, keepdims=True)
        scaled = grad * gain_ref[:, 1:2]
        back = (scaled - unit * jnp.mean(scaled * unit, axis=0, keepdims=True)) * inverse
        middle_grad = cot_ref[...].astype(f32) + back
        mg_ref[...] = middle_grad
        low = middle_grad.astype(bf16)
        d_o = mm(wo_ref[...].astype(f32).T.astype(bf16), low, 1, 0).astype(bf16)
        do_ref[...] = d_o
        mixed = o_ref[...]
        product = d_o.astype(f32) * mixed
        size = width // HEADS
        for head in range(HEADS):
            delta_ref[head // GROUP, head % GROUP : head % GROUP + 1, :] = jnp.sum(
                product[head * size : (head + 1) * size, :], axis=0, keepdims=True
            )
        go_ref[...] = jnp.zeros_like(go_ref)
        go_ref[:, :width] = mm(low, mixed.astype(bf16), 1, 1).astype(bf16)


def feed_specs(pieces, rows, width):
    part, units = pieces[0].shape[1:]
    tile = units
    whole = lambda shape: pl.BlockSpec(shape, lambda i, info: (0,) * len(shape))
    tokens = whole((rows, width))
    features = whole((width, rows))
    gains = whole((width, 2))
    weights = [whole(item.shape) for item in pieces]
    grads = pl.BlockSpec((3, width, tile), lambda i, info: (0, 0, i))
    held = pltpu.VMEM((4, width // part, part, units), bf16)
    return units // tile, whole, tokens, features, gains, weights, grads, held


def feed_first(info, x, mixed_t, cot, gains, pieces):
    width, rows = x.shape
    units = pieces[0].shape[2]
    count = len(pieces)
    steps, whole, tokens, features, gain_spec, weights, grads, held = feed_specs(pieces, rows, width)
    wide = jax.ShapeDtypeStruct((width, rows), f32)
    flat = jax.ShapeDtypeStruct((rows, width), bf16)
    return pl.pallas_call(
        functools.partial(feed_first_kernel, count),
        out_shape=(
            wide,
            flat,
            flat,
            jax.ShapeDtypeStruct((width, rows), bf16),
            wide,
            wide,
            jax.ShapeDtypeStruct((3, width, units), bf16),
            jax.ShapeDtypeStruct((width, width), bf16),
        ),
        grid_spec=pltpu.PrefetchScalarGridSpec(
            num_scalar_prefetch=1,
            grid=(steps,),
            in_specs=weights + [features, features, features, gain_spec],
            out_specs=(
                features, tokens, tokens, features, features, features, grads, whole((width, width)),
            ),
            scratch_shapes=[held],
        ),
        compiler_params=pltpu.CompilerParams(vmem_limit_bytes=VMEM),
        cost_estimate=pl.CostEstimate(
            flops=20 * rows * width * units, bytes_accessed=12 * units * width, transcendentals=0
        ),
        name="feed_first",
    )(info, *pieces, x, mixed_t, cot, gains)


def feed_second(
    info, middle, mixed_t, cot, second, cot_rows, second_t, layer_sum, d_second, gains, output_t, pieces
):
    width, rows = middle.shape
    units = pieces[0].shape[2]
    count = len(pieces)
    steps, whole, tokens, features, gain_spec, weights, grads, held = feed_specs(pieces, rows, width)
    return pl.pallas_call(
        functools.partial(feed_second_kernel, count),
        out_shape=(
            jax.ShapeDtypeStruct((width, rows // 2), bf16),
            jax.ShapeDtypeStruct((width, rows // 2), bf16),
            jax.ShapeDtypeStruct((width, rows), f32),
            jax.ShapeDtypeStruct((width, rows), bf16),
            jax.ShapeDtypeStruct((KV_HEADS, GROUP, rows), f32),
            jax.ShapeDtypeStruct((width, 1), f32),
            jax.ShapeDtypeStruct((width, units), bf16),
            jax.ShapeDtypeStruct((3, width, units), bf16),
        ),
        grid_spec=pltpu.PrefetchScalarGridSpec(
            num_scalar_prefetch=1,
            grid=(steps,),
            in_specs=weights
            + [
                features, features, features, tokens, tokens, features, features, features, gain_spec,
                whole((width, width)),
            ],
            out_specs=(
                whole((width, rows // 2)),
                whole((width, rows // 2)),
                features,
                features,
                whole((KV_HEADS, GROUP, rows)),
                whole((width, 1)),
                whole((width, units)),
                grads,
            ),
            scratch_shapes=[
                pltpu.VMEM((width, rows), f32),
                pltpu.VMEM((width, rows), f32),
                held,
            ],
        ),
        compiler_params=pltpu.CompilerParams(vmem_limit_bytes=VMEM),
        cost_estimate=pl.CostEstimate(
            flops=20 * rows * width * units, bytes_accessed=12 * units * width, transcendentals=0
        ),
        name="feed_second",
    )(
        info, *pieces, middle, mixed_t, cot, second, cot_rows, second_t, layer_sum, d_second, gains,
        output_t,
    )


def finish_kernel(
    info_ref, even_ref, odd_ref, dq_ref, a_ref, aq_ref, xq_ref, mg_ref, query_ref, key_ref, value_ref,
    gain_ref, gg2_ref, keep_ref, give_ref, chunk_ref, send_ref, kv_sum, gg_ref, q_sum,
):
    size = even_ref.shape[1] // (2 * KV_HEADS)
    step = pl.program_id(0)

    @pl.when(step == 0)
    def _():
        dq = dq_ref[...]
        grad_query = mm(dq, aq_ref[...], 1, 1)
        q_sum[...] = grad_query.astype(bf16)
        query_t = query_ref[...].astype(f32)
        gg_ref[...] = jnp.sum(query_t * grad_query, axis=0, keepdims=True)
        d_a = mm(query_t.T.astype(bf16), dq, 1, 0)
        chunk = mg_ref[...] + column_norm_back(d_a, xq_ref[...].astype(f32), gain_ref[:, 0:1])
        chunk_ref[...] = chunk
        send_ref[...] = chunk[:, chunk.shape[1] // 2 :].astype(bf16)
        kv_sum[...] = jnp.zeros_like(kv_sum)

    kv_sum[...] += mm(even_ref[0], a_ref[0], 1, 1) + mm(odd_ref[0], a_ref[1], 1, 1)

    @pl.when(step == pl.num_programs(0) - 1)
    def _():
        total = gg_ref[...]
        grads = [[], []]
        for group in range(KV_HEADS):
            rows = slice(group * size, (group + 1) * size)
            grad_key = kv_sum[2 * group * size : (2 * group + 1) * size, :]
            grad_value = kv_sum[(2 * group + 1) * size : (2 * group + 2) * size, :]
            grads[0].append(grad_key)
            grads[1].append(grad_value)
            total = total + jnp.sum(
                key_ref[rows, :].astype(f32) * grad_key + value_ref[rows, :].astype(f32) * grad_value,
                axis=0,
                keepdims=True,
            )
        gain_grad = jnp.concatenate([total / gain_ref[:, 0:1].T, gg2_ref[...].T], axis=0)
        grads = [jnp.concatenate(items, axis=0) for items in grads]
        shards, part, width = keep_ref.shape
        kv_part = KV_HEADS * size // shards
        first = info_ref[1] == 0
        for shard in range(shards):
            queries = q_sum[shard * part : (shard + 1) * part, :].astype(f32)
            rows = slice(shard * kv_part, (shard + 1) * kv_part)
            gain_rows = jnp.concatenate(
                [gain_grad, jnp.zeros((part - 2 * kv_part - 2, width), f32)], axis=0
            )
            others = jnp.concatenate([grads[0][rows], grads[1][rows], gain_rows], axis=0)
            keep_ref[shard] = jnp.where(first, queries, others).astype(bf16)
            give_ref[shard] = jnp.where(first, others, queries).astype(bf16)


def finish(info, even, odd, dq_t, a_all, a, x, middle_grad, query_t, key_t, value_t, gains, gain_second, shards):
    pairs, terms, rows = even.shape
    width = x.shape[0]
    kv_width = key_t.shape[0]
    pack = jax.ShapeDtypeStruct((shards, width // shards, width), bf16)
    whole = lambda shape: pl.BlockSpec(shape, lambda i, info: (0,) * len(shape))
    pair = pl.BlockSpec((1, terms, rows), lambda i, info: (i, 0, 0))
    return pl.pallas_call(
        finish_kernel,
        out_shape=(
            pack,
            pack,
            jax.ShapeDtypeStruct((width, rows), f32),
            jax.ShapeDtypeStruct((width, rows // 2), bf16),
        ),
        grid_spec=pltpu.PrefetchScalarGridSpec(
            num_scalar_prefetch=1,
            grid=(pairs,),
            in_specs=[
                pair,
                pair,
                whole((width, rows)),
                pl.BlockSpec((2, width, rows), lambda i, info: (i, 0, 0)),
                whole((width, rows)),
                whole((width, rows)),
                whole((width, rows)),
                whole((width, width)),
                whole((kv_width, width)),
                whole((kv_width, width)),
                whole((width, 2)),
                whole((width, 1)),
            ],
            out_specs=(
                whole(pack.shape),
                whole(pack.shape),
                whole((width, rows)),
                whole((width, rows // 2)),
            ),
            scratch_shapes=[
                pltpu.VMEM((terms, width), f32),
                pltpu.VMEM((1, width), f32),
                pltpu.VMEM((width, width), bf16),
            ],
        ),
        compiler_params=pltpu.CompilerParams(vmem_limit_bytes=VMEM),
        cost_estimate=pl.CostEstimate(
            flops=4 * pairs * rows * width * terms, bytes_accessed=8 * 1024 * 1024, transcendentals=0
        ),
        name="finish",
    )(info, even, odd, dq_t, a_all, a, x, middle_grad, query_t, key_t, value_t, gains, gain_second)


def last_kernel(count, *refs):
    own_ref = refs[0]
    got_refs = refs[1 : 1 + count]
    x_ref, chunk_ref, back_ref, key_ref, value_ref, gain_ref, out_ref = refs[1 + count :]
    total = own_ref[...].astype(f32)
    for got in got_refs:
        total = total + got[...].astype(f32)
    total = total.astype(bf16)
    size = total.shape[0] // (2 * KV_HEADS)
    keys = [total[2 * g * size : (2 * g + 1) * size] for g in range(KV_HEADS)]
    values = [total[(2 * g + 1) * size : (2 * g + 2) * size] for g in range(KV_HEADS)]
    weights = jnp.concatenate([key_ref[...], value_ref[...]], axis=0).astype(f32).T.astype(bf16)
    d_a = mm(weights, jnp.concatenate(keys + values, axis=0), 1, 0)
    back = column_norm_back(d_a, x_ref[...].astype(f32), gain_ref[:, 0:1])
    half = back_ref.shape[1]
    out_ref[:, :half] = chunk_ref[:, :half] + back[:, :half]
    out_ref[:, half:] = back_ref[...].astype(f32) + back[:, half:]


def last(pair, got, x_own, chunk_grad, back, key_t, value_t, gains):
    width, rows = x_own.shape
    whole = lambda shape: pl.BlockSpec(shape, lambda i: (0,) * len(shape))
    return pl.pallas_call(
        functools.partial(last_kernel, len(got)),
        out_shape=jax.ShapeDtypeStruct((width, rows), f32),
        grid=(1,),
        in_specs=[whole(item.shape) for item in (pair, *got, x_own, chunk_grad, back, key_t, value_t, gains)],
        out_specs=whole((width, rows)),
        compiler_params=pltpu.CompilerParams(vmem_limit_bytes=VMEM // 4 * 3),
        cost_estimate=pl.CostEstimate(
            flops=2 * rows * width * pair.shape[0], bytes_accessed=6 * 1024 * 1024, transcendentals=0
        ),
        name="last",
    )(pair, *got, x_own, chunk_grad, back, key_t, value_t, gains)


def add_kernel(info_ref, keep_ref, got_ref, output_ref, *out_refs):
    for mask, out_ref in enumerate(out_refs):

        @pl.when(pl.program_id(0) == mask)
        def _(mask=mask, out_ref=out_ref):
            matrix = info_ref[0] ^ mask

            @pl.when(matrix < 3)
            def _():
                out_ref[...] = (keep_ref[0].astype(f32) + got_ref[0].astype(f32)).astype(bf16)

            @pl.when(matrix >= 3)
            def _():
                out_ref[...] = output_ref[...]


def add_rotated(info, keep, got, output):
    _, width, units = keep.shape
    feed = pl.BlockSpec((1, width, units), lambda i, info: (jnp.minimum(info[0] ^ i, 2), 0, 0))
    whole = pl.BlockSpec((width, units), lambda i, info: (0, 0))
    return pl.pallas_call(
        add_kernel,
        out_shape=[jax.ShapeDtypeStruct((width, units), bf16)] * 4,
        grid_spec=pltpu.PrefetchScalarGridSpec(
            num_scalar_prefetch=1,
            grid=(4,),
            in_specs=[feed, feed, whole],
            out_specs=[whole] * 4,
        ),
        compiler_params=pltpu.CompilerParams(vmem_limit_bytes=VMEM),
        name="add_rotated",
    )(info, keep, got, output)


def shard_pieces(piece):
    return [piece] + [swap(piece, "shard", mask) for mask in range(1, lax.axis_size("shard"))]


def in_order(pieces):
    me = lax.axis_index("shard")
    bit = 1
    while bit < len(pieces):
        odd = (me & bit) > 0
        pieces = [jnp.where(odd, pieces[j ^ bit], pieces[j]) for j in range(len(pieces))]
        bit *= 2
    return jnp.stack(pieces)


def scatter_shards(pieces):
    count = lax.axis_size("shard")
    me = lax.axis_index("shard")
    total = lax.dynamic_index_in_dim(pieces, me, 0, False).astype(f32)
    for mask in range(1, count):
        sent = lax.dynamic_index_in_dim(pieces, me ^ mask, 0, False).astype(bf16)
        total = total + swap(sent, "shard", mask).astype(f32)
    return total


def scatter_doubling(pieces):
    me = lax.axis_index("shard")
    mask = pieces.shape[0] // 2
    while mask:
        halves = pieces.reshape((2, mask) + pieces.shape[1:])
        upper = (me & mask) > 0
        sent = jnp.where(upper, halves[0], halves[1])
        kept = jnp.where(upper, halves[1], halves[0])
        total = kept.astype(f32) + swap(sent, "shard", mask).astype(f32)
        pieces = total.astype(bf16)
        mask //= 2
    return pieces[0]


def sum_context(value):
    total = value.astype(f32)
    low = value.astype(bf16)
    for mask in range(1, lax.axis_size("context")):
        total = total + swap(low, "context", mask).astype(f32)
    return total


def per_device(
    hidden_in,
    segment_ids,
    norm_gains,
    w_query,
    w_key,
    w_value,
    w_output,
    w_gate,
    w_up,
    w_down,
    cotangent,
):
    rows, width = hidden_in.shape[1], hidden_in.shape[2]
    half = rows // 2
    seg_row = segment_ids[0]
    length = seg_row.shape[0]
    shards = lax.axis_size("shard")
    contexts = lax.axis_size("context")
    blocks = lax.axis_size(SEQ)
    me = lax.axis_index(SEQ)
    core = lax.axis_index("tensor")
    context = lax.axis_index("context")
    part = w_query.shape[1]
    kv_part = w_key.shape[1]
    kv_width = kv_part * shards
    units = w_gate.shape[0]
    head_size = width // HEADS
    scale = head_size**-0.5

    starts = doc_starts(seg_row)
    place = (
        (jnp.arange(blocks, dtype=jnp.int32) ^ me)[:, None] * rows
        + jnp.arange(rows, dtype=jnp.int32)[None, :]
    ).reshape(1, -1)
    placed_starts = jnp.max(jnp.where(place >= starts[:, None], starts[:, None], 0), axis=0)
    positions = (place[0] - placed_starts).astype(f32)
    frequency = rope_base ** (-jnp.arange(head_size // 2, dtype=f32) * 2.0 / head_size)
    angles = frequency[:, None] * positions[None, :]
    cosine, sine = jnp.cos(angles), jnp.sin(angles)
    info = jnp.concatenate([jnp.reshape(me, (1,)).astype(jnp.int32), starts])

    x_own = hidden_in[0].T
    by_context = contexts == 4 and part % 16 == 0

    gain_rows = part - 2 * kv_part
    key_values = jnp.concatenate(
        [w_key.T, w_value.T, jnp.pad(norm_gains, ((0, gain_rows - 2), (0, width - part)))], axis=0
    )
    pack = jnp.where(core == 0, w_query.T, key_values)
    later = jnp.stack([w_gate.T, w_up.T, w_down.T, jnp.pad(w_output.T, ((0, 0), (0, units - width)))])
    if by_context:
        x_one, x_two = swap(x_own, "context", 1), swap(x_own, "context", 2)
        later_c = lax.dynamic_index_in_dim(later, context, 0, False)
        pack_mine = shard_pieces(pack)
        x_one, x_two, pack_mine, later_c, cosine, sine = lax.optimization_barrier(
            (x_one, x_two, pack_mine, later_c, cosine, sine)
        )
        fetched = shard_pieces(later_c)[1:]
        x_three = [swap(x_two[:, :half], "context", 1), swap(x_one[:, half:], "context", 2)]
        x_three, fetched[2], pack_mine = lax.optimization_barrier((x_three, fetched[2], pack_mine))
        x_near = jnp.stack([x_own, x_one, x_two, jnp.concatenate(x_three, axis=1)])
        pack_mine = jnp.stack(pack_mine)
        x_near, pack_mine = lax.optimization_barrier((x_near, pack_mine))
        x_far = swap(x_near, "tensor", 1)
        x_arrays = [x_near, x_far]
        layout = tuple((r % 2, r // 2) for r in range(8))
    else:
        near = [x_own] + [swap(x_own, "context", mask) for mask in range(1, contexts)]
        x_arrays = [item[None] for item in near] + [swap(jnp.stack(near), "tensor", 1)]
        layout = tuple((c if r == 0 else contexts, 0 if r == 0 else c) for c in range(contexts) for r in (0, 1))
        later_pieces = shard_pieces(later)
        pack_mine = jnp.stack(shard_pieces(pack))
    pack_theirs = swap(pack_mine, "tensor", 1)
    shard = lax.axis_index("shard")
    places = jnp.stack([shard, core, context]).astype(jnp.int32)
    query_t, key_t, value_t, gain_parts = unpack(places, [pack_mine], [pack_theirs], kv_part)
    query_t = query_t.reshape(width, width)
    key_t = key_t.reshape(kv_width, width)
    value_t = value_t.reshape(kv_width, width)
    gains = gain_parts[:, :2, :part].transpose(0, 2, 1).reshape(width, 2).astype(f32)

    def chunks(array, axis):
        return jnp.concatenate(
            [
                lax.slice_in_dim(array, 0, half, axis=axis),
                lax.slice_in_dim(array, length - half, length, axis=axis),
            ],
            axis=axis,
        )

    if by_context:
        query_t, fetched = lax.optimization_barrier((query_t, fetched))
        fetched = jnp.stack(fetched)
        fetched = [fetched] + [swap(fetched, "context", mask) for mask in range(1, 4)]
    a_all, keys, keys_t, values, values_t, queries_t, a, x = project(
        x_arrays, layout, query_t, key_t, value_t, gains, cosine, sine, scale
    )
    cos_q, sin_q = chunks(cosine, 1), chunks(sine, 1)

    queries_t, cot_own = lax.optimization_barrier((queries_t, cotangent[0].T))
    cot_got = lax.ppermute(cot_own[:, half:], SEQ, flip(blocks, blocks - 1))
    cot = jnp.concatenate([cot_own[:, :half], cot_got], axis=1)
    attended = attend(0, 2, (), info, queries_t, keys, values_t, rows)

    if by_context:
        attended, fetched, cot, later = lax.optimization_barrier((attended, fetched, cot, later))
        mine_all = [later] + fetched
    else:
        later_pieces = in_order(later_pieces).transpose(1, 0, 2, 3).reshape(4, width, units)
        attended, later_pieces = lax.optimization_barrier((attended, later_pieces))
        mine_all = [later_pieces]
    theirs_all = [swap(item, "tensor", 1) for item in mine_all]
    mixed_t, log_total = attend(2, 1, attended, info, queries_t, keys, values_t, rows)
    middle, second, cot_rows, second_t, layer_sum, d_second, grads_theirs, output_t = feed_first(
        places, x, mixed_t, cot, gains, theirs_all
    )
    ff_got = swap(grads_theirs, "tensor", 1)
    layer_keep, layer_send, middle_grad, mixed_grad_t, delta, gain_grad_second, output_sum, grads_mine = (
        feed_second(
            places, middle, mixed_t, cot, second, cot_rows, second_t, layer_sum, d_second, gains,
            output_t, mine_all,
        )
    )
    wide = units

    def back(group, earlier, info):
        return attend_back(
            group, earlier, info, queries_t, mixed_grad_t, keys, keys_t, values, log_total, delta,
            cosine, sine, cos_q, sin_q, rows, scale,
        )

    pair_of = flip(blocks, blocks - 1)
    if contexts == 4:
        both = add_rotated(places[2:], grads_mine, ff_got, output_sum)
        info, both = lax.optimization_barrier((info, both))
        got = [swap(item, "context", mask) for mask, item in enumerate(both) if mask]
        terms = back(0, (), info)
        terms = back(1, terms, info)
        terms, got = lax.optimization_barrier((terms, got))
        owned = both[0].astype(f32)
        for item in got:
            owned = owned + item.astype(f32)
        owned = owned.reshape(shards, part, wide)
        kept = lax.dynamic_index_in_dim(owned, shard, 0, False)
        sent = [
            lax.dynamic_index_in_dim(owned, shard ^ mask, 0, False).astype(bf16)
            for mask in range(1, shards)
        ]
        terms, kept, sent, layer_send = lax.optimization_barrier((terms, kept, sent, layer_send))
        got = [swap(item, "shard", mask + 1) for mask, item in enumerate(sent)]
        layer_got = lax.ppermute(layer_send, SEQ, pair_of)
        terms = back(2, terms, info)
        terms, got, layer_got = lax.optimization_barrier((terms, got, layer_got))
        for item in got:
            kept = kept + item.astype(f32)
        owned_low = kept.astype(bf16)
        spread = [owned_low] + [swap(owned_low, "context", mask) for mask in range(1, 4)]
    else:
        layer_got = lax.ppermute(layer_send, SEQ, pair_of)
        ff_sum = grads_mine.astype(f32) + ff_got.astype(f32)
        both = [*ff_sum, output_sum]
        terms = back(0, (), info)
        terms = back(1, terms, info)
        terms = back(2, terms, info)
    dq_t, even, odd = terms
    odd_got = swap(odd, "tensor", 1)
    finished = finish(
        places, even, odd, dq_t, a_all, a, x, middle_grad, query_t, key_t, value_t, gains,
        gain_grad_second, shards,
    )
    if contexts == 4:
        odd_got, spread, finished = lax.optimization_barrier((odd_got, spread, finished))
        for bit in (1, 2):
            away = (context & bit) > 0
            spread = [jnp.where(away, spread[j ^ bit], spread[j]) for j in range(4)]
        final = spread
    else:
        large = jnp.stack([item.astype(bf16) for item in both]).reshape(4, shards, part, wide).transpose(1, 0, 2, 3)
        final = lax.psum(scatter_shards(large).astype(bf16), "context")
    keep, give, chunk_grad, chunk_send = finished
    pair = [
        (even[mask].astype(f32) + odd_got[mask].astype(f32)).astype(bf16) for mask in range(contexts)
    ]

    grad_gate, grad_up, grad_down = [final[matrix].astype(f32).T for matrix in range(3)]
    output_low = final[3][:, :width]
    grad_output = (output_low.astype(f32) + swap(output_low, "tensor", 1).astype(f32)).T

    both = (keep.astype(f32) + swap(give, "tensor", 1).astype(f32)).astype(bf16)
    both, pair, chunk_send = lax.optimization_barrier((both, pair, chunk_send))
    pair_got = [swap(item, "context", mask) for mask, item in enumerate(pair) if mask]
    returned = lax.ppermute(chunk_send, SEQ, flip(blocks, blocks - 1))
    small = scatter_doubling(both)
    small, pair_got, returned, layer_got = lax.optimization_barrier(
        (small, pair_got, returned, layer_got)
    )
    layer_value = jnp.concatenate([layer_keep, layer_got], axis=1).T
    grad_hidden = last(pair[0], pair_got, x_own, chunk_grad, returned, key_t, value_t, gains).T
    small = sum_context(small).astype(bf16)
    small, grad_hidden = lax.optimization_barrier((small, grad_hidden))
    small_other = swap(small, "tensor", 1)
    grad_query = jnp.where(core == 0, small, small_other).astype(f32).T
    small = jnp.where(core == 0, small_other, small).astype(f32)
    grad_key = small[:kv_part].T
    grad_value = small[kv_part : 2 * kv_part].T
    gain_grads = small[2 * kv_part : 2 * kv_part + 2]
    grad_gains = lax.dynamic_slice_in_dim(gain_grads, shard * part, part, 1)

    return (
        layer_value[None],
        grad_hidden[None],
        grad_gains,
        grad_query,
        grad_key,
        grad_value,
        grad_output,
        grad_gate,
        grad_up,
        grad_down,
    )


def solution(mesh):
    return jax.shard_map(
        per_device,
        mesh=mesh,
        in_specs=(
            P("shard", ("context", "tensor"), None),
            P("shard", None),
            P(None, "shard"),
            P(None, "shard"),
            P(None, "shard"),
            P(None, "shard"),
            P(None, "shard"),
            P("tensor", "shard"),
            P("tensor", "shard"),
            P("tensor", "shard"),
            P("shard", ("context", "tensor"), None),
        ),
        out_specs=(
            P("shard", ("context", "tensor"), None),
            P("shard", ("context", "tensor"), None),
            P(None, "shard"),
            P(None, "shard"),
            P(None, "shard"),
            P(None, "shard"),
            P(None, "shard"),
            P("tensor", "shard"),
            P("tensor", "shard"),
            P("tensor", "shard"),
        ),
        check_vma=False,
    )
```

```python
import functools

import jax
import jax.numpy as jnp
from jax import lax
from jax.experimental import pallas as pl
from jax.experimental.pallas import tpu as pltpu
from jax.sharding import PartitionSpec as P

HEADS = 9
KV_HEADS = 3
DOCS = 4
GROUP = HEADS // KV_HEADS

rope_base = 100000.0
norm_eps = 1e-05
masked_score = -1e30

VMEM = 60 * 1024 * 1024
f32 = jnp.float32
bf16 = jnp.bfloat16
SEQ = ("context", "tensor")


def mm(left, right, left_dim, right_dim):
    return lax.dot_general(
        left, right, (((left_dim,), (right_dim,)), ((), ())), preferred_element_type=f32
    )


def flip(count, mask):
    return [(i, i ^ mask) for i in range(count)]


def swap(value, axis, mask):
    return lax.ppermute(value, axis, flip(lax.axis_size(axis), mask))


def doc_starts(seg_row):
    one_hot = (seg_row[None, :] == jnp.arange(DOCS, dtype=jnp.int32)[:, None]).astype(jnp.int32)
    doc_counts = jnp.sum(one_hot, axis=1)
    return jnp.cumsum(doc_counts) - doc_counts


def column_rms(hidden):
    return lax.rsqrt(jnp.mean(hidden * hidden, axis=0, keepdims=True) + norm_eps)


def column_norm_back(grad, hidden, gain):
    inverse = column_rms(hidden)
    unit = hidden * inverse
    scaled = grad * gain
    return (scaled - unit * jnp.mean(scaled * unit, axis=0, keepdims=True)) * inverse


def turn_head(head, cosine, sine, sign):
    half = cosine.shape[0]
    first, second = head[:half], head[half:]
    return jnp.concatenate(
        [first * cosine - sign * (second * sine), second * cosine + sign * (first * sine)], axis=0
    )


def doc_start(info_ref, index):
    start = jnp.int32(0)
    for doc in range(1, DOCS):
        start = jnp.where(index >= info_ref[1 + doc], info_ref[1 + doc], start)
    return start


def chunk_start(info_ref, chunk, blocks, size):
    me = info_ref[0]
    return jnp.where(chunk == 0, me * 2 * size, (blocks - 1 - me) * 2 * size + size)


def key_ranges(info_ref, chunk, blocks, key_block):
    size = key_block // 2
    first = chunk_start(info_ref, chunk, blocks, size)
    low = doc_start(info_ref, first) // key_block
    high = (first + size + key_block - 1) // key_block
    full_from = (doc_start(info_ref, first + size - 1) + key_block - 1) // key_block
    high = high - jnp.where(chunk == 0, 1, 0)
    full_from = jnp.minimum(jnp.maximum(full_from, low), high)
    full_to = jnp.minimum(jnp.maximum(first // key_block, full_from), high)
    return low, full_from, full_to, high


def allowed_mask(info_ref, block, key_block, chunk, blocks, keys):
    size = key_block // 2
    first = chunk_start(info_ref, chunk, blocks, size)
    index = first + lax.broadcasted_iota(jnp.int32, (1, size), 1)
    start = doc_start(info_ref, index)
    key_index = block * key_block + lax.broadcasted_iota(jnp.int32, (keys, size), 0)
    return (key_index >= start) & (key_index <= index)


def side_by_side(ref, size):
    return jnp.concatenate([ref[m * size : (m + 1) * size, :] for m in range(GROUP)], axis=1)


def forward_kernel(key_block, group, info_ref, *refs):
    if group:
        refs = refs[2:]
    q_ref, k_ref, vt_ref, o_ref, lse_ref, m_ref, l_ref, acc_ref, q_side = refs
    chunk = pl.program_id(1)
    me = info_ref[0]
    size = k_ref.shape[2]
    tokens = q_ref.shape[1]
    blocks = k_ref.shape[1] // key_block
    m_ref[...] = jnp.full_like(m_ref, masked_score)
    acc_ref[...] = jnp.zeros_like(acc_ref)
    q_side[...] = side_by_side(q_ref, size)

    def block_scores(block, masked, keys):
        place = pl.multiple_of((block ^ me) * key_block, key_block)
        scores = mm(k_ref[0, pl.ds(place, keys), :], q_side[...], 1, 0)
        if masked:
            mask = allowed_mask(info_ref, block, key_block, chunk, blocks, keys)
            scores = jnp.concatenate(
                [
                    jnp.where(mask, scores[:, m * tokens : (m + 1) * tokens], masked_score)
                    for m in range(GROUP)
                ],
                axis=1,
            )
        return scores

    def step(first, count, masked, keys=key_block):
        scores = [block_scores(first + i, masked, keys) for i in range(count)]
        old = m_ref[...]
        new = old
        for item in scores:
            new = jnp.maximum(new, jnp.max(item, axis=0, keepdims=True))
        m_ref[...] = new
        total = acc_ref[...] * jnp.exp(old - new)
        for i, item in enumerate(scores):
            place = pl.multiple_of(((first + i) ^ me) * key_block, key_block)
            weights = jnp.exp(item - new).astype(bf16)
            values = jnp.concatenate(
                [vt_ref[:, pl.ds(place, keys)], jnp.ones((16, keys), bf16)], axis=0
            )
            total = total + mm(values, weights, 1, 0)
        acc_ref[...] = total

    low, full_from, full_to, high = key_ranges(info_ref, chunk, blocks, key_block)
    pairs = (full_to - full_from) // 2
    pl.loop(low, full_from)(lambda b: step(b, 1, True))
    pl.loop(0, pairs)(lambda b: step(full_from + 2 * b, 2, False))
    pl.loop(full_from + 2 * pairs, full_to)(lambda b: step(b, 1, False))
    pl.loop(full_to, high)(lambda b: step(b, 1, True))
    pl.when(chunk == 0)(lambda: step(me, 1, True, key_block // 2))
    for member in range(GROUP):
        rows = slice(member * size, (member + 1) * size)
        lanes = slice(member * tokens, (member + 1) * tokens)
        total = acc_ref[size : size + 1, lanes]
        o_ref[rows, :] = acc_ref[:size, lanes] / total
        lse_ref[0, member : member + 1, :] = m_ref[:, lanes] + jnp.log(total)


def backward_kernel(key_block, scale, group, *refs):
    if group:
        refs = refs[:1] + refs[4:]
    (
        info_ref, q_ref, do_ref, k_ref, kt_ref, v_ref, lse_ref, delta_ref,
        cos_ref, sin_ref, cosq_ref, sinq_ref,
        dq_ref, even_ref, odd_ref, dk_ref, dv_ref, dq_sum, q_side, do_side,
    ) = refs
    chunk = pl.program_id(0)
    me = info_ref[0]
    size = k_ref.shape[2]
    blocks = dk_ref.shape[0]
    tokens = q_ref.shape[1]
    dq_sum[...] = jnp.zeros_like(dq_sum)
    q_side[...] = side_by_side(q_ref, size)
    do_side[...] = side_by_side(do_ref, size)
    log_total = jnp.concatenate([lse_ref[0, m : m + 1, :] for m in range(GROUP)], axis=1)
    delta = jnp.concatenate([delta_ref[0, m : m + 1, :] for m in range(GROUP)], axis=1)

    @pl.when(chunk == 0)
    def _():
        dk_ref[...] = jnp.zeros_like(dk_ref)
        dv_ref[...] = jnp.zeros_like(dv_ref)

    def step(block, masked, count=key_block):
        spot = block ^ me
        place = pl.multiple_of(spot * key_block, key_block)
        keys = k_ref[0, pl.ds(place, count), :]
        values = v_ref[0, pl.ds(place, count), :]
        keys_t = kt_ref[:, pl.ds(place, count)]
        scores = mm(keys, q_side[...], 1, 0)
        if masked:
            mask = allowed_mask(info_ref, block, key_block, chunk, blocks, count)
            scores = jnp.concatenate(
                [
                    jnp.where(mask, scores[:, m * tokens : (m + 1) * tokens], masked_score)
                    for m in range(GROUP)
                ],
                axis=1,
            )
        probs = jnp.exp(scores - log_total)
        prob_grad = mm(values, do_side[...], 1, 0)
        raw = (probs * (prob_grad - delta)).astype(bf16)
        dv = mm(do_side[...], probs.astype(bf16), 1, 1)
        dk = mm(q_side[...], raw, 1, 1)
        dq_sum[...] += mm(keys_t, raw, 1, 0)
        dk_ref[spot, :, :count] += dk
        dv_ref[spot, :, :count] += dv

    low, full_from, full_to, high = key_ranges(info_ref, chunk, blocks, key_block)
    pl.loop(low, full_from)(lambda b: step(b, True))
    pl.loop(full_from, full_to)(lambda b: step(b, False))
    pl.loop(full_to, high)(lambda b: step(b, True))
    pl.when(chunk == 0)(lambda: step(me, True, key_block // 2))
    for member in range(GROUP):
        rows = slice(member * size, (member + 1) * size)
        dq_ref[rows, :] = turn_head(
            dq_sum[:, member * tokens : (member + 1) * tokens] * scale, cosq_ref[...], sinq_ref[...], -1.0).astype(
            bf16
        )

    @pl.when(chunk == 1)
    def _():
        for block in range(blocks):
            columns = slice(block * key_block, (block + 1) * key_block)
            out_ref = odd_ref if block % 2 else even_ref
            out_ref[block // 2, :size, :] = turn_head(
                dk_ref[block], cos_ref[:, columns], sin_ref[:, columns], -1.0
            ).astype(bf16)
            out_ref[block // 2, size:, :] = dv_ref[block].astype(bf16)


def attend(group, groups, earlier, info, queries_t, keys, values_t, key_block):
    length, size = keys.shape[1], keys.shape[2]
    tokens = queries_t.shape[1]
    chunk = tokens // 2
    wide = GROUP * size
    head_block = pl.BlockSpec((wide, chunk), lambda g, c, info: (group + g, c))
    stat_block = pl.BlockSpec((1, GROUP, chunk), lambda g, c, info: (group + g, 0, c))
    elements = groups * GROUP * tokens * length // 2
    return pl.pallas_call(
        functools.partial(forward_kernel, key_block, group),
        out_shape=(
            jax.ShapeDtypeStruct((HEADS * size, tokens), f32),
            jax.ShapeDtypeStruct((KV_HEADS, GROUP, tokens), f32),
        ),
        grid_spec=pltpu.PrefetchScalarGridSpec(
            num_scalar_prefetch=1,
            grid=(groups, 2),
            in_specs=[pl.BlockSpec(memory_space=pl.ANY)] * len(earlier)
            + [
                head_block,
                pl.BlockSpec((1, length, size), lambda g, c, info: (group + g, 0, 0)),
                pl.BlockSpec((size, length), lambda g, c, info: (group + g, 0)),
            ],
            out_specs=(head_block, stat_block),
            scratch_shapes=[
                pltpu.VMEM((1, GROUP * chunk), f32),
                pltpu.VMEM((1, GROUP * chunk), f32),
                pltpu.VMEM((size + 16, GROUP * chunk), f32),
                pltpu.VMEM((size, GROUP * chunk), bf16),
            ],
        ),
        input_output_aliases={1 + number: number for number in range(len(earlier))},
        compiler_params=pltpu.CompilerParams(vmem_limit_bytes=VMEM),
        cost_estimate=pl.CostEstimate(
            flops=16 * elements * size, bytes_accessed=4 * 1024 * 1024, transcendentals=elements
        ),
        name="attend",
    )(info, *earlier, queries_t, keys, values_t)


def attend_back(
    group, earlier, info, queries_t, grads_t, keys, keys_t, values, log_total, delta,
    cosine, sine, cos_q, sin_q, key_block, scale,
):
    length, size = keys.shape[1], keys.shape[2]
    tokens = queries_t.shape[1]
    chunk = tokens // 2
    wide = GROUP * size
    blocks = length // key_block
    head_block = pl.BlockSpec((wide, chunk), lambda c, info: (group, c))
    stat_block = pl.BlockSpec((1, GROUP, chunk), lambda c, info: (group, 0, c))
    token_block = pl.BlockSpec((1, length, size), lambda c, info: (group, 0, 0))
    feature_block = pl.BlockSpec((size, length), lambda c, info: (group, 0))
    table = pl.BlockSpec((size // 2, length), lambda c, info: (0, 0))
    table_q = pl.BlockSpec((size // 2, chunk), lambda c, info: (0, c))
    terms = pl.BlockSpec((blocks // 2, 2 * size, key_block), lambda c, info: (0, group, 0))
    elements = GROUP * tokens * length // 2
    terms_shape = jax.ShapeDtypeStruct((blocks // 2, KV_HEADS * 2 * size, key_block), bf16)
    return pl.pallas_call(
        functools.partial(backward_kernel, key_block, scale, group),
        out_shape=(jax.ShapeDtypeStruct((HEADS * size, tokens), bf16), terms_shape, terms_shape),
        grid_spec=pltpu.PrefetchScalarGridSpec(
            num_scalar_prefetch=1,
            grid=(2,),
            in_specs=[pl.BlockSpec(memory_space=pl.ANY)] * len(earlier)
            + [
                head_block, head_block, token_block, feature_block, token_block, stat_block, stat_block,
                table, table, table_q, table_q,
            ],
            out_specs=(head_block, terms, terms),
            scratch_shapes=[
                pltpu.VMEM((blocks, size, key_block), f32),
                pltpu.VMEM((blocks, size, key_block), f32),
                pltpu.VMEM((size, GROUP * chunk), f32),
                pltpu.VMEM((size, GROUP * chunk), bf16),
                pltpu.VMEM((size, GROUP * chunk), bf16),
            ],
        ),
        input_output_aliases={1 + number: number for number in range(len(earlier))},
        compiler_params=pltpu.CompilerParams(vmem_limit_bytes=VMEM),
        cost_estimate=pl.CostEstimate(
            flops=40 * elements * size, bytes_accessed=4 * 1024 * 1024, transcendentals=elements
        ),
        name="attend_back",
    )(
        info, *earlier, queries_t, grads_t, keys, keys_t, values, log_total, delta,
        cosine, sine, cos_q, sin_q,
    )


def unpack_kernel(count, kv_part, info_ref, *refs):
    mine, theirs = refs[:count], refs[count : 2 * count]
    query_ref, key_ref, value_ref, gain_ref = refs[2 * count :]
    first = info_ref[1] == 0
    mask = 0
    for number in range(count):
        for row in range(mine[number].shape[0]):
            spot = info_ref[0] ^ mask
            left, right = mine[number][row], theirs[number][row]
            query_ref[spot] = jnp.where(first, left, right)
            other = jnp.where(first, right, left)
            key_ref[spot] = other[:kv_part]
            value_ref[spot] = other[kv_part : 2 * kv_part]
            gain_ref[spot] = other[2 * kv_part :]
            mask += 1


def unpack(info, mine, theirs, kv_part):
    count = len(mine)
    total = sum(item.shape[0] for item in mine)
    part, width = mine[0].shape[1:]
    whole = lambda shape: pl.BlockSpec(shape, lambda i, info: (0,) * len(shape))
    shapes = [(total, size, width) for size in (part, kv_part, kv_part, part - 2 * kv_part)]
    return pl.pallas_call(
        functools.partial(unpack_kernel, count, kv_part),
        out_shape=[jax.ShapeDtypeStruct(shape, bf16) for shape in shapes],
        grid_spec=pltpu.PrefetchScalarGridSpec(
            num_scalar_prefetch=1,
            grid=(1,),
            in_specs=[whole(item.shape) for item in (*mine, *theirs)],
            out_specs=[whole(shape) for shape in shapes],
        ),
        name="unpack",
    )(info, *mine, *theirs)


def project_kernel(layout, arrays, scale, *refs):
    pieces = len(layout)
    x_refs = [refs[array].at[row] for array, row in layout]
    query_ref, key_ref, value_ref, gain_ref, cos_ref, sin_ref = refs[arrays : arrays + 6]
    a_ref, k_ref, kt_ref, v_ref, vt_ref, q_ref, aq_ref, xq_ref, cos_q, sin_q = refs[
        arrays + 6 : arrays + 16
    ]
    held, sems = refs[arrays + 16 :]
    step = pl.program_id(0)
    tokens = xq_ref.shape[1]
    chunk = tokens // 2

    @pl.when(step == 0)
    def _():
        for number in range(pieces):
            pltpu.make_async_copy(x_refs[number], held.at[number], sems.at[number]).start()

    for number in range(pieces):

        @pl.when(step == number)
        def _(number=number):
            pltpu.make_async_copy(x_refs[number], held.at[number], sems.at[number]).wait()

    x_low = held[step]
    x = x_low.astype(f32)
    a = (x * column_rms(x) * gain_ref[:, 0:1]).astype(bf16)
    a_ref[0] = a
    cosine, sine = cos_ref[...], sin_ref[...]
    k_lin = mm(key_ref[...], a, 1, 0)
    v_lin = mm(value_ref[...], a, 1, 0)
    vt_ref[...] = v_lin.astype(bf16)
    size = k_ref.shape[2]
    for group in range(KV_HEADS):
        rows = slice(group * size, (group + 1) * size)
        turned = turn_head(k_lin[rows], cosine, sine, 1.0)
        kt_ref[rows, :] = turned.astype(bf16)
        k_ref[group] = turned.T.astype(bf16)
        v_ref[group] = v_lin[rows].T.astype(bf16)

    @pl.when(step == 0)
    def _():
        aq_ref[:, :chunk] = a[:, :chunk]
        xq_ref[:, :chunk] = x_low[:, :chunk]
        cos_q[:, :chunk] = cosine[:, :chunk]
        sin_q[:, :chunk] = sine[:, :chunk]

    @pl.when(step == pieces - 1)
    def _():
        aq_ref[:, chunk:] = a[:, chunk:]
        xq_ref[:, chunk:] = x_low[:, chunk:]
        cos_q[:, chunk:] = cosine[:, chunk:]
        sin_q[:, chunk:] = sine[:, chunk:]
        q_lin = mm(query_ref[...], aq_ref[...], 1, 0)
        for head in range(HEADS):
            rows = slice(head * size, (head + 1) * size)
            q_ref[rows, :] = (
                turn_head(q_lin[rows], cos_q[...], sin_q[...], 1.0).astype(bf16) * scale
            ).astype(bf16)


def project(x_arrays, layout, query_t, key_t, value_t, gains, cosine, sine, scale):
    pieces = len(layout)
    arrays = len(x_arrays)
    width, rows = x_arrays[0].shape[1:]
    kv_width = key_t.shape[0]
    size = kv_width // KV_HEADS
    length = pieces * rows
    whole = lambda array: pl.BlockSpec(array.shape, lambda i: (0,) * array.ndim)
    table = pl.BlockSpec((size // 2, rows), lambda i: (0, i))
    by_token = pl.BlockSpec((KV_HEADS, rows, size), lambda i: (0, i, 0))
    by_feature = pl.BlockSpec((kv_width, rows), lambda i: (0, i))
    own = pl.BlockSpec((width, rows), lambda i: (0, 0))
    own_shape = jax.ShapeDtypeStruct((width, rows), bf16)
    own_table = pl.BlockSpec((size // 2, rows), lambda i: (0, 0))
    table_shape = jax.ShapeDtypeStruct((size // 2, rows), f32)
    return pl.pallas_call(
        functools.partial(project_kernel, layout, arrays, scale),
        out_shape=(
            jax.ShapeDtypeStruct((pieces, width, rows), bf16),
            jax.ShapeDtypeStruct((KV_HEADS, length, size), bf16),
            jax.ShapeDtypeStruct((kv_width, length), bf16),
            jax.ShapeDtypeStruct((KV_HEADS, length, size), bf16),
            jax.ShapeDtypeStruct((kv_width, length), bf16),
            own_shape,
            own_shape,
            own_shape,
            table_shape,
            table_shape,
        ),
        grid=(pieces,),
        in_specs=[pl.BlockSpec(memory_space=pl.ANY)] * arrays
        + [whole(query_t), whole(key_t), whole(value_t), whole(gains), table, table],
        out_specs=(
            pl.BlockSpec((1, width, rows), lambda i: (i, 0, 0)),
            by_token,
            by_feature,
            by_token,
            by_feature,
            own,
            own,
            own,
            own_table,
            own_table,
        ),
        scratch_shapes=[
            pltpu.VMEM((pieces, width, rows), bf16),
            pltpu.SemaphoreType.DMA((pieces,)),
        ],
        compiler_params=pltpu.CompilerParams(vmem_limit_bytes=VMEM),
        cost_estimate=pl.CostEstimate(
            flops=8 * length * width * kv_width, bytes_accessed=8 * length * width, transcendentals=0
        ),
        name="project",
    )(*x_arrays, query_t, key_t, value_t, gains, cosine, sine)


def feed_tile(second, second_t, cot, cot_t, weights, grad_ref, sum_ref, db_ref):
    gate_t, up_t, down_t = weights
    gate = mm(second, gate_t, 1, 0)
    upward = mm(second, up_t, 1, 0)
    d_hidden = mm(cot, down_t, 1, 0)
    sig = 1.0 / (1.0 + jnp.exp(-gate))
    silu = gate * sig
    hidden = (silu * upward).astype(bf16)
    d_gate = (d_hidden * upward * sig * (1.0 + gate * (1.0 - sig))).astype(bf16)
    d_up = (d_hidden * silu).astype(bf16)
    sum_ref[...] += mm(down_t, hidden, 1, 1)
    db_ref[...] += mm(gate_t, d_gate, 1, 1) + mm(up_t, d_up, 1, 1)
    grad_ref[0] = mm(second_t, d_gate, 1, 0).astype(bf16)
    grad_ref[1] = mm(second_t, d_up, 1, 0).astype(bf16)
    grad_ref[2] = mm(cot_t, hidden, 1, 0).astype(bf16)


def hold_weights(info_ref, own_ref, other_refs, held):
    shard, context = info_ref[0], info_ref[2]
    for matrix in range(held.shape[0]):
        held[matrix, shard if held.shape[1] > 1 else 0] = own_ref[matrix]
    for number, other in enumerate(other_refs):
        for mask in range(1, held.shape[1]):
            held[context ^ number, shard ^ mask] = other[mask - 1]


def held_tiles(held, tile):
    lanes = pl.ds(pl.multiple_of(pl.program_id(0) * tile, tile), tile)
    return [
        held[matrix, :, :, lanes].reshape(held.shape[1] * held.shape[2], tile) for matrix in range(3)
    ]


def feed_first_kernel(count, info_ref, *refs):
    x_ref, o_ref, cot_ref, gain_ref = refs[count : count + 4]
    h_ref, second_ref, cot_rows, second_t, sum_ref, db_ref, grad_ref, output_ref = refs[
        count + 4 : count + 12
    ]
    held = refs[count + 12]
    width = x_ref.shape[0]

    @pl.when(pl.program_id(0) == 0)
    def _():
        hold_weights(info_ref, refs[0], refs[1:count], held)
        output_t = held[3].reshape(width, held.shape[3])[:, :width]
        output_ref[...] = output_t
        middle = x_ref[...].astype(f32) + mm(output_t, o_ref[...].astype(bf16), 1, 0)
        second = middle * column_rms(middle) * gain_ref[:, 1:2]
        h_ref[...] = middle
        second_t[...] = second.astype(bf16)
        second_ref[...] = second.T.astype(bf16)
        cot_rows[...] = cot_ref[...].astype(f32).T.astype(bf16)
        sum_ref[...] = middle
        db_ref[...] = jnp.zeros_like(db_ref)

    weights = held_tiles(held, grad_ref.shape[2])
    feed_tile(
        second_ref[...], second_t[...], cot_rows[...], cot_ref[...], weights, grad_ref, sum_ref, db_ref
    )


def feed_second_kernel(count, info_ref, *refs):
    (
        h_ref, o_ref, cot_ref, second_ref, cot_rows, second_t, sum_in_ref, db_in_ref, gain_ref, wo_ref,
    ) = refs[count : count + 10]
    layer_ref, send_ref, mg_ref, do_ref, delta_ref, gg_ref, go_ref, grad_ref = refs[
        count + 10 : count + 18
    ]
    sum_ref, db_ref, held = refs[count + 18 :]
    width = h_ref.shape[0]
    step = pl.program_id(0)

    @pl.when(step == 0)
    def _():
        hold_weights(info_ref, refs[0], refs[1:count], held)
        sum_ref[...] = sum_in_ref[...]
        db_ref[...] = db_in_ref[...]

    weights = held_tiles(held, grad_ref.shape[2])
    feed_tile(
        second_ref[...], second_t[...], cot_rows[...], cot_ref[...], weights, grad_ref, sum_ref, db_ref
    )

    @pl.when(step == pl.num_programs(0) - 1)
    def _():
        chunk = layer_ref.shape[1]
        layer_ref[...] = sum_ref[:, :chunk].astype(bf16)
        send_ref[...] = sum_ref[:, chunk:].astype(bf16)
        middle = h_ref[...]
        inverse = column_rms(middle)
        unit = middle * inverse
        grad = db_ref[...]
        gg_ref[...] = jnp.sum(grad * unit, axis=1, keepdims=True)
        scaled = grad * gain_ref[:, 1:2]
        back = (scaled - unit * jnp.mean(scaled * unit, axis=0, keepdims=True)) * inverse
        middle_grad = cot_ref[...].astype(f32) + back
        mg_ref[...] = middle_grad
        low = middle_grad.astype(bf16)
        d_o = mm(wo_ref[...].astype(f32).T.astype(bf16), low, 1, 0).astype(bf16)
        do_ref[...] = d_o
        mixed = o_ref[...]
        product = d_o.astype(f32) * mixed
        size = width // HEADS
        for head in range(HEADS):
            delta_ref[head // GROUP, head % GROUP : head % GROUP + 1, :] = jnp.sum(
                product[head * size : (head + 1) * size, :], axis=0, keepdims=True
            )
        go_ref[...] = jnp.zeros_like(go_ref)
        go_ref[:, :width] = mm(low, mixed.astype(bf16), 1, 1).astype(bf16)


def feed_specs(pieces, rows, width):
    part, units = pieces[0].shape[1:]
    tile = units
    whole = lambda shape: pl.BlockSpec(shape, lambda i, info: (0,) * len(shape))
    tokens = whole((rows, width))
    features = whole((width, rows))
    gains = whole((width, 2))
    weights = [whole(item.shape) for item in pieces]
    grads = pl.BlockSpec((3, width, tile), lambda i, info: (0, 0, i))
    held = pltpu.VMEM((4, width // part, part, units), bf16)
    return units // tile, whole, tokens, features, gains, weights, grads, held


def feed_first(info, x, mixed_t, cot, gains, pieces):
    width, rows = x.shape
    units = pieces[0].shape[2]
    count = len(pieces)
    steps, whole, tokens, features, gain_spec, weights, grads, held = feed_specs(pieces, rows, width)
    wide = jax.ShapeDtypeStruct((width, rows), f32)
    flat = jax.ShapeDtypeStruct((rows, width), bf16)
    return pl.pallas_call(
        functools.partial(feed_first_kernel, count),
        out_shape=(
            wide,
            flat,
            flat,
            jax.ShapeDtypeStruct((width, rows), bf16),
            wide,
            wide,
            jax.ShapeDtypeStruct((3, width, units), bf16),
            jax.ShapeDtypeStruct((width, width), bf16),
        ),
        grid_spec=pltpu.PrefetchScalarGridSpec(
            num_scalar_prefetch=1,
            grid=(steps,),
            in_specs=weights + [features, features, features, gain_spec],
            out_specs=(
                features, tokens, tokens, features, features, features, grads, whole((width, width)),
            ),
            scratch_shapes=[held],
        ),
        compiler_params=pltpu.CompilerParams(vmem_limit_bytes=VMEM),
        cost_estimate=pl.CostEstimate(
            flops=20 * rows * width * units, bytes_accessed=12 * units * width, transcendentals=0
        ),
        name="feed_first",
    )(info, *pieces, x, mixed_t, cot, gains)


def feed_second(
    info, middle, mixed_t, cot, second, cot_rows, second_t, layer_sum, d_second, gains, output_t, pieces
):
    width, rows = middle.shape
    units = pieces[0].shape[2]
    count = len(pieces)
    steps, whole, tokens, features, gain_spec, weights, grads, held = feed_specs(pieces, rows, width)
    return pl.pallas_call(
        functools.partial(feed_second_kernel, count),
        out_shape=(
            jax.ShapeDtypeStruct((width, rows // 2), bf16),
            jax.ShapeDtypeStruct((width, rows // 2), bf16),
            jax.ShapeDtypeStruct((width, rows), f32),
            jax.ShapeDtypeStruct((width, rows), bf16),
            jax.ShapeDtypeStruct((KV_HEADS, GROUP, rows), f32),
            jax.ShapeDtypeStruct((width, 1), f32),
            jax.ShapeDtypeStruct((width, units), bf16),
            jax.ShapeDtypeStruct((3, width, units), bf16),
        ),
        grid_spec=pltpu.PrefetchScalarGridSpec(
            num_scalar_prefetch=1,
            grid=(steps,),
            in_specs=weights
            + [
                features, features, features, tokens, tokens, features, features, features, gain_spec,
                whole((width, width)),
            ],
            out_specs=(
                whole((width, rows // 2)),
                whole((width, rows // 2)),
                features,
                features,
                whole((KV_HEADS, GROUP, rows)),
                whole((width, 1)),
                whole((width, units)),
                grads,
            ),
            scratch_shapes=[
                pltpu.VMEM((width, rows), f32),
                pltpu.VMEM((width, rows), f32),
                held,
            ],
        ),
        compiler_params=pltpu.CompilerParams(vmem_limit_bytes=VMEM),
        cost_estimate=pl.CostEstimate(
            flops=20 * rows * width * units, bytes_accessed=12 * units * width, transcendentals=0
        ),
        name="feed_second",
    )(
        info, *pieces, middle, mixed_t, cot, second, cot_rows, second_t, layer_sum, d_second, gains,
        output_t,
    )


def finish_kernel(
    info_ref, even_ref, odd_ref, dq_ref, a_ref, aq_ref, xq_ref, mg_ref, query_ref, key_ref, value_ref,
    gain_ref, gg2_ref, keep_ref, give_ref, chunk_ref, send_ref, kv_sum, gg_ref, q_sum,
):
    size = even_ref.shape[1] // (2 * KV_HEADS)
    step = pl.program_id(0)

    @pl.when(step == 0)
    def _():
        dq = dq_ref[...]
        grad_query = mm(dq, aq_ref[...], 1, 1)
        q_sum[...] = grad_query.astype(bf16)
        query_t = query_ref[...].astype(f32)
        gg_ref[...] = jnp.sum(query_t * grad_query, axis=0, keepdims=True)
        d_a = mm(query_t.T.astype(bf16), dq, 1, 0)
        chunk = mg_ref[...] + column_norm_back(d_a, xq_ref[...].astype(f32), gain_ref[:, 0:1])
        chunk_ref[...] = chunk
        send_ref[...] = chunk[:, chunk.shape[1] // 2 :].astype(bf16)
        kv_sum[...] = jnp.zeros_like(kv_sum)

    kv_sum[...] += mm(even_ref[0], a_ref[0], 1, 1) + mm(odd_ref[0], a_ref[1], 1, 1)

    @pl.when(step == pl.num_programs(0) - 1)
    def _():
        total = gg_ref[...]
        grads = [[], []]
        for group in range(KV_HEADS):
            rows = slice(group * size, (group + 1) * size)
            grad_key = kv_sum[2 * group * size : (2 * group + 1) * size, :]
            grad_value = kv_sum[(2 * group + 1) * size : (2 * group + 2) * size, :]
            grads[0].append(grad_key)
            grads[1].append(grad_value)
            total = total + jnp.sum(
                key_ref[rows, :].astype(f32) * grad_key + value_ref[rows, :].astype(f32) * grad_value,
                axis=0,
                keepdims=True,
            )
        gain_grad = jnp.concatenate([total / gain_ref[:, 0:1].T, gg2_ref[...].T], axis=0)
        grads = [jnp.concatenate(items, axis=0) for items in grads]
        shards, part, width = keep_ref.shape
        kv_part = KV_HEADS * size // shards
        first = info_ref[1] == 0
        for shard in range(shards):
            queries = q_sum[shard * part : (shard + 1) * part, :].astype(f32)
            rows = slice(shard * kv_part, (shard + 1) * kv_part)
            gain_rows = jnp.concatenate(
                [gain_grad, jnp.zeros((part - 2 * kv_part - 2, width), f32)], axis=0
            )
            others = jnp.concatenate([grads[0][rows], grads[1][rows], gain_rows], axis=0)
            keep_ref[shard] = jnp.where(first, queries, others).astype(bf16)
            give_ref[shard] = jnp.where(first, others, queries).astype(bf16)


def finish(info, even, odd, dq_t, a_all, a, x, middle_grad, query_t, key_t, value_t, gains, gain_second, shards):
    pairs, terms, rows = even.shape
    width = x.shape[0]
    kv_width = key_t.shape[0]
    pack = jax.ShapeDtypeStruct((shards, width // shards, width), bf16)
    whole = lambda shape: pl.BlockSpec(shape, lambda i, info: (0,) * len(shape))
    pair = pl.BlockSpec((1, terms, rows), lambda i, info: (i, 0, 0))
    return pl.pallas_call(
        finish_kernel,
        out_shape=(
            pack,
            pack,
            jax.ShapeDtypeStruct((width, rows), f32),
            jax.ShapeDtypeStruct((width, rows // 2), bf16),
        ),
        grid_spec=pltpu.PrefetchScalarGridSpec(
            num_scalar_prefetch=1,
            grid=(pairs,),
            in_specs=[
                pair,
                pair,
                whole((width, rows)),
                pl.BlockSpec((2, width, rows), lambda i, info: (i, 0, 0)),
                whole((width, rows)),
                whole((width, rows)),
                whole((width, rows)),
                whole((width, width)),
                whole((kv_width, width)),
                whole((kv_width, width)),
                whole((width, 2)),
                whole((width, 1)),
            ],
            out_specs=(
                whole(pack.shape),
                whole(pack.shape),
                whole((width, rows)),
                whole((width, rows // 2)),
            ),
            scratch_shapes=[
                pltpu.VMEM((terms, width), f32),
                pltpu.VMEM((1, width), f32),
                pltpu.VMEM((width, width), bf16),
            ],
        ),
        compiler_params=pltpu.CompilerParams(vmem_limit_bytes=VMEM),
        cost_estimate=pl.CostEstimate(
            flops=4 * pairs * rows * width * terms, bytes_accessed=8 * 1024 * 1024, transcendentals=0
        ),
        name="finish",
    )(info, even, odd, dq_t, a_all, a, x, middle_grad, query_t, key_t, value_t, gains, gain_second)


def last_kernel(count, *refs):
    own_ref = refs[0]
    got_refs = refs[1 : 1 + count]
    x_ref, chunk_ref, back_ref, key_ref, value_ref, gain_ref, out_ref = refs[1 + count :]
    total = own_ref[...].astype(f32)
    for got in got_refs:
        total = total + got[...].astype(f32)
    total = total.astype(bf16)
    size = total.shape[0] // (2 * KV_HEADS)
    keys = [total[2 * g * size : (2 * g + 1) * size] for g in range(KV_HEADS)]
    values = [total[(2 * g + 1) * size : (2 * g + 2) * size] for g in range(KV_HEADS)]
    weights = jnp.concatenate([key_ref[...], value_ref[...]], axis=0).astype(f32).T.astype(bf16)
    d_a = mm(weights, jnp.concatenate(keys + values, axis=0), 1, 0)
    back = column_norm_back(d_a, x_ref[...].astype(f32), gain_ref[:, 0:1])
    half = back_ref.shape[1]
    out_ref[:, :half] = chunk_ref[:, :half] + back[:, :half]
    out_ref[:, half:] = back_ref[...].astype(f32) + back[:, half:]


def last(pair, got, x_own, chunk_grad, back, key_t, value_t, gains):
    width, rows = x_own.shape
    whole = lambda shape: pl.BlockSpec(shape, lambda i: (0,) * len(shape))
    return pl.pallas_call(
        functools.partial(last_kernel, len(got)),
        out_shape=jax.ShapeDtypeStruct((width, rows), f32),
        grid=(1,),
        in_specs=[whole(item.shape) for item in (pair, *got, x_own, chunk_grad, back, key_t, value_t, gains)],
        out_specs=whole((width, rows)),
        compiler_params=pltpu.CompilerParams(vmem_limit_bytes=VMEM // 4 * 3),
        cost_estimate=pl.CostEstimate(
            flops=2 * rows * width * pair.shape[0], bytes_accessed=6 * 1024 * 1024, transcendentals=0
        ),
        name="last",
    )(pair, *got, x_own, chunk_grad, back, key_t, value_t, gains)


def add_kernel(info_ref, keep_ref, got_ref, output_ref, *out_refs):
    for mask, out_ref in enumerate(out_refs):

        @pl.when(pl.program_id(0) == mask)
        def _(mask=mask, out_ref=out_ref):
            matrix = info_ref[0] ^ mask

            @pl.when(matrix < 3)
            def _():
                out_ref[...] = (keep_ref[0].astype(f32) + got_ref[0].astype(f32)).astype(bf16)

            @pl.when(matrix >= 3)
            def _():
                out_ref[...] = output_ref[...]


def add_rotated(info, keep, got, output):
    _, width, units = keep.shape
    feed = pl.BlockSpec((1, width, units), lambda i, info: (jnp.minimum(info[0] ^ i, 2), 0, 0))
    whole = pl.BlockSpec((width, units), lambda i, info: (0, 0))
    return pl.pallas_call(
        add_kernel,
        out_shape=[jax.ShapeDtypeStruct((width, units), bf16)] * 4,
        grid_spec=pltpu.PrefetchScalarGridSpec(
            num_scalar_prefetch=1,
            grid=(4,),
            in_specs=[feed, feed, whole],
            out_specs=[whole] * 4,
        ),
        compiler_params=pltpu.CompilerParams(vmem_limit_bytes=VMEM),
        name="add_rotated",
    )(info, keep, got, output)


def shard_pieces(piece):
    return [piece] + [swap(piece, "shard", mask) for mask in range(1, lax.axis_size("shard"))]


def in_order(pieces):
    me = lax.axis_index("shard")
    bit = 1
    while bit < len(pieces):
        odd = (me & bit) > 0
        pieces = [jnp.where(odd, pieces[j ^ bit], pieces[j]) for j in range(len(pieces))]
        bit *= 2
    return jnp.stack(pieces)


def scatter_shards(pieces):
    count = lax.axis_size("shard")
    me = lax.axis_index("shard")
    total = lax.dynamic_index_in_dim(pieces, me, 0, False).astype(f32)
    for mask in range(1, count):
        sent = lax.dynamic_index_in_dim(pieces, me ^ mask, 0, False).astype(bf16)
        total = total + swap(sent, "shard", mask).astype(f32)
    return total


def scatter_doubling(pieces):
    me = lax.axis_index("shard")
    mask = pieces.shape[0] // 2
    while mask:
        halves = pieces.reshape((2, mask) + pieces.shape[1:])
        upper = (me & mask) > 0
        sent = jnp.where(upper, halves[0], halves[1])
        kept = jnp.where(upper, halves[1], halves[0])
        total = kept.astype(f32) + swap(sent, "shard", mask).astype(f32)
        pieces = total.astype(bf16)
        mask //= 2
    return pieces[0]


def sum_context(value):
    total = value.astype(f32)
    low = value.astype(bf16)
    for mask in range(1, lax.axis_size("context")):
        total = total + swap(low, "context", mask).astype(f32)
    return total


def per_device(
    hidden_in,
    segment_ids,
    norm_gains,
    w_query,
    w_key,
    w_value,
    w_output,
    w_gate,
    w_up,
    w_down,
    cotangent,
):
    rows, width = hidden_in.shape[1], hidden_in.shape[2]
    half = rows // 2
    seg_row = segment_ids[0]
    length = seg_row.shape[0]
    shards = lax.axis_size("shard")
    contexts = lax.axis_size("context")
    blocks = lax.axis_size(SEQ)
    me = lax.axis_index(SEQ)
    core = lax.axis_index("tensor")
    context = lax.axis_index("context")
    part = w_query.shape[1]
    kv_part = w_key.shape[1]
    kv_width = kv_part * shards
    units = w_gate.shape[0]
    head_size = width // HEADS
    scale = head_size**-0.5

    starts = doc_starts(seg_row)
    place = (
        (jnp.arange(blocks, dtype=jnp.int32) ^ me)[:, None] * rows
        + jnp.arange(rows, dtype=jnp.int32)[None, :]
    ).reshape(1, -1)
    placed_starts = jnp.max(jnp.where(place >= starts[:, None], starts[:, None], 0), axis=0)
    positions = (place[0] - placed_starts).astype(f32)
    frequency = rope_base ** (-jnp.arange(head_size // 2, dtype=f32) * 2.0 / head_size)
    angles = frequency[:, None] * positions[None, :]
    cosine, sine = jnp.cos(angles), jnp.sin(angles)
    info = jnp.concatenate([jnp.reshape(me, (1,)).astype(jnp.int32), starts])

    x_own = hidden_in[0].T
    by_context = contexts == 4 and part % 16 == 0

    gain_rows = part - 2 * kv_part
    key_values = jnp.concatenate(
        [w_key.T, w_value.T, jnp.pad(norm_gains, ((0, gain_rows - 2), (0, width - part)))], axis=0
    )
    pack = jnp.where(core == 0, w_query.T, key_values)
    later = jnp.stack([w_gate.T, w_up.T, w_down.T, jnp.pad(w_output.T, ((0, 0), (0, units - width)))])
    if by_context:
        x_one, x_two = swap(x_own, "context", 1), swap(x_own, "context", 2)
        later_c = lax.dynamic_index_in_dim(later, context, 0, False)
        pack_mine = shard_pieces(pack)
        x_one, x_two, pack_mine, later_c, cosine, sine = lax.optimization_barrier(
            (x_one, x_two, pack_mine, later_c, cosine, sine)
        )
        fetched = shard_pieces(later_c)[1:]
        x_three = [swap(x_two[:, :half], "context", 1), swap(x_one[:, half:], "context", 2)]
        x_three, fetched[2], pack_mine = lax.optimization_barrier((x_three, fetched[2], pack_mine))
        x_near = jnp.stack([x_own, x_one, x_two, jnp.concatenate(x_three, axis=1)])
        pack_mine = jnp.stack(pack_mine)
        x_near, pack_mine = lax.optimization_barrier((x_near, pack_mine))
        x_far = swap(x_near, "tensor", 1)
        x_arrays = [x_near, x_far]
        layout = tuple((r % 2, r // 2) for r in range(8))
    else:
        near = [x_own] + [swap(x_own, "context", mask) for mask in range(1, contexts)]
        x_arrays = [item[None] for item in near] + [swap(jnp.stack(near), "tensor", 1)]
        layout = tuple((c if r == 0 else contexts, 0 if r == 0 else c) for c in range(contexts) for r in (0, 1))
        later_pieces = shard_pieces(later)
        pack_mine = jnp.stack(shard_pieces(pack))
    pack_theirs = swap(pack_mine, "tensor", 1)
    shard = lax.axis_index("shard")
    places = jnp.stack([shard, core, context]).astype(jnp.int32)
    query_t, key_t, value_t, gain_parts = unpack(places, [pack_mine], [pack_theirs], kv_part)
    query_t = query_t.reshape(width, width)
    key_t = key_t.reshape(kv_width, width)
    value_t = value_t.reshape(kv_width, width)
    gains = gain_parts[:, :2, :part].transpose(0, 2, 1).reshape(width, 2).astype(f32)

    if by_context:
        query_t, fetched = lax.optimization_barrier((query_t, fetched))
        fetched = jnp.stack(fetched)
        fetched = [fetched] + [swap(fetched, "context", mask) for mask in range(1, 4)]
    a_all, keys, keys_t, values, values_t, queries_t, a, x, cos_q, sin_q = project(
        x_arrays, layout, query_t, key_t, value_t, gains, cosine, sine, scale
    )

    queries_t, cot_own = lax.optimization_barrier((queries_t, cotangent[0].T))
    cot_got = lax.ppermute(cot_own[:, half:], SEQ, flip(blocks, blocks - 1))
    cot = jnp.concatenate([cot_own[:, :half], cot_got], axis=1)
    attended = attend(0, 2, (), info, queries_t, keys, values_t, rows)

    if by_context:
        attended, fetched, cot, later = lax.optimization_barrier((attended, fetched, cot, later))
        mine_all = [later] + fetched
    else:
        later_pieces = in_order(later_pieces).transpose(1, 0, 2, 3).reshape(4, width, units)
        attended, later_pieces = lax.optimization_barrier((attended, later_pieces))
        mine_all = [later_pieces]
    theirs_all = [swap(item, "tensor", 1) for item in mine_all]
    mixed_t, log_total = attend(2, 1, attended, info, queries_t, keys, values_t, rows)
    middle, second, cot_rows, second_t, layer_sum, d_second, grads_theirs, output_t = feed_first(
        places, x, mixed_t, cot, gains, theirs_all
    )
    ff_got = swap(grads_theirs, "tensor", 1)
    layer_keep, layer_send, middle_grad, mixed_grad_t, delta, gain_grad_second, output_sum, grads_mine = (
        feed_second(
            places, middle, mixed_t, cot, second, cot_rows, second_t, layer_sum, d_second, gains,
            output_t, mine_all,
        )
    )
    wide = units

    def back(group, earlier, info):
        return attend_back(
            group, earlier, info, queries_t, mixed_grad_t, keys, keys_t, values, log_total, delta,
            cosine, sine, cos_q, sin_q, rows, scale,
        )

    pair_of = flip(blocks, blocks - 1)
    if contexts == 4:
        both = add_rotated(places[2:], grads_mine, ff_got, output_sum)
        info, both = lax.optimization_barrier((info, both))
        got = [swap(item, "context", mask) for mask, item in enumerate(both) if mask]
        terms = back(0, (), info)
        terms = back(1, terms, info)
        terms, got = lax.optimization_barrier((terms, got))
        owned = both[0].astype(f32)
        for item in got:
            owned = owned + item.astype(f32)
        owned = owned.reshape(shards, part, wide)
        kept = lax.dynamic_index_in_dim(owned, shard, 0, False)
        sent = [
            lax.dynamic_index_in_dim(owned, shard ^ mask, 0, False).astype(bf16)
            for mask in range(1, shards)
        ]
        terms, kept, sent, layer_send = lax.optimization_barrier((terms, kept, sent, layer_send))
        got = [swap(item, "shard", mask + 1) for mask, item in enumerate(sent)]
        layer_got = lax.ppermute(layer_send, SEQ, pair_of)
        terms = back(2, terms, info)
        terms, got, layer_got = lax.optimization_barrier((terms, got, layer_got))
        for item in got:
            kept = kept + item.astype(f32)
        owned_low = kept.astype(bf16)
        spread = [owned_low] + [swap(owned_low, "context", mask) for mask in range(1, 4)]
    else:
        layer_got = lax.ppermute(layer_send, SEQ, pair_of)
        ff_sum = grads_mine.astype(f32) + ff_got.astype(f32)
        both = [*ff_sum, output_sum]
        terms = back(0, (), info)
        terms = back(1, terms, info)
        terms = back(2, terms, info)
    dq_t, even, odd = terms
    odd_got = swap(odd, "tensor", 1)
    finished = finish(
        places, even, odd, dq_t, a_all, a, x, middle_grad, query_t, key_t, value_t, gains,
        gain_grad_second, shards,
    )
    if contexts == 4:
        odd_got, spread, finished = lax.optimization_barrier((odd_got, spread, finished))
        for bit in (1, 2):
            away = (context & bit) > 0
            spread = [jnp.where(away, spread[j ^ bit], spread[j]) for j in range(4)]
        final = spread
    else:
        large = jnp.stack([item.astype(bf16) for item in both]).reshape(4, shards, part, wide).transpose(1, 0, 2, 3)
        final = lax.psum(scatter_shards(large).astype(bf16), "context")
    keep, give, chunk_grad, chunk_send = finished
    pair = [
        (even[mask].astype(f32) + odd_got[mask].astype(f32)).astype(bf16) for mask in range(contexts)
    ]

    grad_gate, grad_up, grad_down = [final[matrix].astype(f32).T for matrix in range(3)]
    output_low = final[3][:, :width]
    grad_output = (output_low.astype(f32) + swap(output_low, "tensor", 1).astype(f32)).T

    both = (keep.astype(f32) + swap(give, "tensor", 1).astype(f32)).astype(bf16)
    both, pair, chunk_send = lax.optimization_barrier((both, pair, chunk_send))
    pair_got = [swap(item, "context", mask) for mask, item in enumerate(pair) if mask]
    returned = lax.ppermute(chunk_send, SEQ, flip(blocks, blocks - 1))
    small = scatter_doubling(both)
    small, pair_got, returned, layer_got = lax.optimization_barrier(
        (small, pair_got, returned, layer_got)
    )
    layer_value = jnp.concatenate([layer_keep, layer_got], axis=1).T
    grad_hidden = last(pair[0], pair_got, x_own, chunk_grad, returned, key_t, value_t, gains).T
    small = sum_context(small).astype(bf16)
    small, grad_hidden = lax.optimization_barrier((small, grad_hidden))
    small_other = swap(small, "tensor", 1)
    grad_query = jnp.where(core == 0, small, small_other).astype(f32).T
    small = jnp.where(core == 0, small_other, small).astype(f32)
    grad_key = small[:kv_part].T
    grad_value = small[kv_part : 2 * kv_part].T
    gain_grads = small[2 * kv_part : 2 * kv_part + 2]
    grad_gains = lax.dynamic_slice_in_dim(gain_grads, shard * part, part, 1)

    return (
        layer_value[None],
        grad_hidden[None],
        grad_gains,
        grad_query,
        grad_key,
        grad_value,
        grad_output,
        grad_gate,
        grad_up,
        grad_down,
    )


def solution(mesh):
    return jax.shard_map(
        per_device,
        mesh=mesh,
        in_specs=(
            P("shard", ("context", "tensor"), None),
            P("shard", None),
            P(None, "shard"),
            P(None, "shard"),
            P(None, "shard"),
            P(None, "shard"),
            P(None, "shard"),
            P("tensor", "shard"),
            P("tensor", "shard"),
            P("tensor", "shard"),
            P("shard", ("context", "tensor"), None),
        ),
        out_specs=(
            P("shard", ("context", "tensor"), None),
            P("shard", ("context", "tensor"), None),
            P(None, "shard"),
            P(None, "shard"),
            P(None, "shard"),
            P(None, "shard"),
            P(None, "shard"),
            P("tensor", "shard"),
            P("tensor", "shard"),
            P("tensor", "shard"),
        ),
        check_vma=False,
    )
```
